512 devices in a mesh: gx: 32 (over y, z_lo), gy: 16 (over z_hi, x, core).
Axes of the slice: x: 4, y: 8, z: 8 (z_hi: 2, z_lo: 4; z = z_hi * 4 + z_lo), core: 2. Of those that a mesh axis runs over, the one named last changes fastest.
Arguments:
- local_residual: float32 [512, 256, 64], P('gx', 'gy'), may hold values from -6 to 6
- lengths: float32 [3, 64, 32, 8], P(None, 'gx', 'gy'), may hold values from 0.5 to 2
- coarse_inverse: bfloat16 [32, 512, 512], P('gx', 'gy'), may hold values from -0.026516504 to 0.2265165
Outputs:
- preconditioned: float32 [512, 256, 64], P('gx', 'gy')
- mid_result: float32 [256, 128, 32], P('gx', 'gy')
- coarse_correction: float32 [64, 32, 8], P('gx', 'gy')
The draws below stay inside these ranges and needn't reach their ends.
All inputs are finite; a program needn't handle non-finite values.
Results may differ from the reference program's by a relative error of at most 0.00315.
Values may be sent and summed in bfloat16 or wider, within the bound.
A program may use at most 128 MiB of HBM per device.

```python
import math
import jax
import jax.numpy as jnp
import numpy as np
from jax import lax

ORDER = 7
MID_ORDER = 3
EX = 2
EY = 2
EZ = 8
NEX = 64
NEY = 32
SLAB = 512
N_GX = 32
N_GY = 16


def draw_local_residual(key, part):
    key = jax.random.fold_in(key, 11)
    extent = (NEX * (ORDER + 1), NEY * (ORDER + 1), EZ * (ORDER + 1))
    return jnp.clip(jax.random.normal(key, extent, jnp.float32), -6.0, 6.0)


def draw_coarse_inverse(key, part):
    key = jax.random.fold_in(key, 23)
    slab_count = NEX // EX
    extent = (slab_count, SLAB, SLAB)
    spread = 0.5 / math.sqrt(SLAB)
    perturb = jnp.clip(jax.random.normal(key, extent, jnp.float32), -6.0, 6.0)
    scales = jnp.ones((slab_count, SLAB, 1), jnp.float32)
    identity = jnp.eye(SLAB, dtype=jnp.float32)
    return (0.1 * scales * (identity[None] + spread * perturb)).astype(jnp.bfloat16)


def block_scale(stream_key, dims, split, least, high):
    loudness = 1.0
    for axis_at, shards_of in split:
        steps = jax.random.uniform(jax.random.fold_in(jax.random.fold_in(stream_key, 6), axis_at), (shards_of,), jnp.float32, least / len(split), high / len(split))
        loudness = loudness * jnp.repeat(jnp.exp(steps), dims[axis_at] // shards_of).reshape((-1,) + (1,) * (len(dims) - 1 - axis_at))
    return loudness


def setup_inputs(seed: int = 0) -> dict:
    splits = jax.random.split(jax.random.key(seed), 4)
    local_residual = draw_local_residual(jax.random.fold_in(splits[3], 71), 0)
    lengths = jnp.clip(jnp.exp(math.log(2.0) - 1.3862944 * jax.random.uniform(splits[1], (3, NEX, NEY, EZ), jnp.float32) ** block_scale(splits[1], (3, NEX, NEY, EZ), ((1, 32), (2, 16)), -0.2, 0.2)), 0.5, 2.0)
    coarse_inverse = draw_coarse_inverse(jax.random.fold_in(splits[3], 71), 0)
    return {"local_residual": local_residual, "lengths": lengths, "coarse_inverse": coarse_inverse}


PRECISE = lax.Precision.HIGHEST

def legendre_pair(order, point):
    older = 1.0
    newer = point
    for degree in range(2, order + 1):
        nexter = ((2 * degree - 1) * point * newer - (degree - 1) * older) / degree
        older = newer
        newer = nexter
    return (newer, older)

def jacobi_eigen(matrix):
    count_n = len(matrix)
    work = [list(row_items) for row_items in matrix]
    vectors = [[1.0 if row_at == col_at else 0.0 for col_at in range(count_n)] for row_at in range(count_n)]
    for sweep_count in range(60):
        for lower_at in range(count_n):
            for upper_at in range(lower_at + 1, count_n):
                off_value = work[lower_at][upper_at]
                if abs(off_value) < 1e-18 * (abs(work[lower_at][lower_at]) + abs(work[upper_at][upper_at])):
                    continue
                angle_ratio = (work[upper_at][upper_at] - work[lower_at][lower_at]) / (2.0 * off_value)
                sign_value = 1.0 if angle_ratio >= 0 else -1.0
                tangent = sign_value / (abs(angle_ratio) + math.sqrt(angle_ratio * angle_ratio + 1.0))
                cosine = 1.0 / math.sqrt(tangent * tangent + 1.0)
                sine_value = tangent * cosine
                for other_at in range(count_n):
                    left_value = work[other_at][lower_at]
                    right_value = work[other_at][upper_at]
                    work[other_at][lower_at] = cosine * left_value - sine_value * right_value
                    work[other_at][upper_at] = sine_value * left_value + cosine * right_value
                for other_at in range(count_n):
                    left_value = work[lower_at][other_at]
                    right_value = work[upper_at][other_at]
                    work[lower_at][other_at] = cosine * left_value - sine_value * right_value
                    work[upper_at][other_at] = sine_value * left_value + cosine * right_value
                for other_at in range(count_n):
                    left_value = vectors[other_at][lower_at]
                    right_value = vectors[other_at][upper_at]
                    vectors[other_at][lower_at] = cosine * left_value - sine_value * right_value
                    vectors[other_at][upper_at] = sine_value * left_value + cosine * right_value
    eigen_list = [work[row_at][row_at] for row_at in range(count_n)]
    ordering = sorted(range(count_n), key=lambda index_at: eigen_list[index_at])
    rates = [eigen_list[index_at] for index_at in ordering]
    basis = [[vectors[row_at][index_at] for index_at in ordering] for row_at in range(count_n)]
    return (rates, basis)

def gll_tables(order):
    point_count = order + 1
    node_list = []
    for node_at in range(point_count):
        point = math.cos(math.pi * node_at / order)
        for newton_step in range(100):
            top_value, lower_value = legendre_pair(order, point)
            point = point - (point * top_value - lower_value) / ((order + 1) * top_value)
        node_list.append(point)
    node_list = node_list[::-1]
    node_list[0] = -1.0
    node_list[-1] = 1.0
    values = [legendre_pair(order, point)[0] for point in node_list]
    weight_list = [2.0 / (order * (order + 1) * value_at ** 2) for value_at in values]
    derivative = [[0.0] * point_count for row_at in range(point_count)]
    for row_at in range(point_count):
        for col_at in range(point_count):
            if row_at != col_at:
                derivative[row_at][col_at] = values[row_at] / (values[col_at] * (node_list[row_at] - node_list[col_at]))
    derivative[0][0] = -order * (order + 1) / 4.0
    derivative[order][order] = order * (order + 1) / 4.0
    stiff_list = [[sum((derivative[inner_at][row_at] * weight_list[inner_at] * derivative[inner_at][col_at] for inner_at in range(point_count))) for col_at in range(point_count)] for row_at in range(point_count)]
    extent = 3 * order + 1
    big_stiff = [[0.0] * extent for row_at in range(extent)]
    big_mass = [0.0] * extent
    for offset_at in (0, order, 2 * order):
        for row_at in range(point_count):
            big_mass[offset_at + row_at] += weight_list[row_at]
            for col_at in range(point_count):
                big_stiff[offset_at + row_at][offset_at + col_at] += stiff_list[row_at][col_at]
    chosen = list(range(order - 1, 2 * order + 2))
    root_mass = [1.0 / math.sqrt(big_mass[index_at]) for index_at in chosen]
    scaled = [[root_mass[row_at] * big_stiff[chosen[row_at]][chosen[col_at]] * root_mass[col_at] for col_at in range(len(chosen))] for row_at in range(len(chosen))]
    rates, basis = jacobi_eigen(scaled)
    eigen_basis = [[root_mass[row_at] * basis[row_at][col_at] for col_at in range(len(chosen))] for row_at in range(len(chosen))]
    return (np.array(node_list), np.array(weight_list), np.array(stiff_list), np.array(eigen_basis), np.array(rates))

def interp_table(fine_nodes, coarse_nodes):
    coarse_count = len(coarse_nodes)
    columns = []
    for column in range(coarse_count):
        factors_list = [(fine_nodes - coarse_nodes[other_node]) / (coarse_nodes[column] - coarse_nodes[other_node]) for other_node in range(coarse_count) if other_node != column]
        columns.append(np.prod(np.stack(factors_list), axis=0))
    return np.stack(columns, axis=1)

def element_factors(lengths):
    first_len, second_len, third_len = (lengths[0], lengths[1], lengths[2])
    return jnp.stack([second_len * third_len / (2.0 * first_len), first_len * third_len / (2.0 * second_len), first_len * second_len / (2.0 * third_len)]).reshape(3, -1)

def to_elements(values_in, points):
    size_x, size_y, size_z = values_in.shape
    blocks = values_in.reshape(size_x // points, points, size_y // points, points, size_z // points, points)
    return blocks.transpose(1, 3, 5, 0, 2, 4).reshape(points, points, points, -1)

def to_field(elements, counts):
    points = elements.shape[0]
    blocks = elements.reshape(points, points, points, counts[0], counts[1], counts[2])
    return blocks.transpose(3, 0, 4, 1, 5, 2).reshape(counts[0] * points, counts[1] * points, counts[2] * points)

def face_masks(extent, points, offset):
    position = (np.arange(extent) - offset) % points
    return ((position == 0).astype(np.float32), (position == points - 1).astype(np.float32))

def assemble(padded, points, offset):
    lower_mask, upper_mask = face_masks(padded.shape[0], points, offset)
    zero_slab = jnp.zeros_like(padded[:1])
    previous = jnp.concatenate([zero_slab, padded[:-1]], 0)
    following = jnp.concatenate([padded[1:], zero_slab], 0)
    summed = padded + lower_mask[:, None, None] * previous + upper_mask[:, None, None] * following
    lower_mask, upper_mask = face_masks(summed.shape[1], points, offset)
    zero_slab = jnp.zeros_like(summed[:, :1])
    previous = jnp.concatenate([zero_slab, summed[:, :-1]], 1)
    following = jnp.concatenate([summed[:, 1:], zero_slab], 1)
    summed = summed + lower_mask[None, :, None] * previous + upper_mask[None, :, None] * following
    lower_mask, upper_mask = face_masks(summed.shape[2], points, 0)
    return summed + lower_mask * jnp.roll(summed, 1, 2) + upper_mask * jnp.roll(summed, -1, 2)

def extend(assembled, points, start, counts):
    first_len, second_len, third_len = counts
    left_part = assembled[start - 2:start - 2 + first_len * points:points]
    own_part = assembled[start:start + first_len * points].reshape((first_len, points) + assembled.shape[1:])
    right_part = assembled[start + points + 1:start + points + 1 + first_len * points:points]
    section_one = jnp.concatenate([left_part[:, None], own_part, right_part[:, None]], 1)
    left_part = section_one[:, :, start - 2:start - 2 + second_len * points:points]
    own_part = section_one[:, :, start:start + second_len * points].reshape(section_one.shape[:2] + (second_len, points) + section_one.shape[3:])
    right_part = section_one[:, :, start + points + 1:start + points + 1 + second_len * points:points]
    section_two = jnp.concatenate([left_part[:, :, :, None], own_part, right_part[:, :, :, None]], 3)
    own_part = section_two.reshape(section_two.shape[:4] + (third_len, points))
    left_part = jnp.roll(own_part[..., points - 2], 1, 4)
    right_part = jnp.roll(own_part[..., 1], -1, 4)
    section_three = jnp.concatenate([left_part[..., None], own_part, right_part[..., None]], 5)
    extent = points + 2
    return section_three.transpose(1, 3, 5, 0, 2, 4).reshape(extent, extent, extent, -1)

def fast_solve(extended, eigen_basis, eigen_rates, factors):
    basis_table = jnp.asarray(eigen_basis, jnp.float32)
    rate_table = jnp.asarray(eigen_rates, jnp.float32)
    modal = jnp.einsum('ai,abcE->ibcE', basis_table, extended, precision=PRECISE)
    modal = jnp.einsum('bj,ibcE->ijcE', basis_table, modal, precision=PRECISE)
    modal = jnp.einsum('ck,ijcE->ijkE', basis_table, modal, precision=PRECISE)
    divisor = factors[0] * rate_table[:, None, None, None] + factors[1] * rate_table[None, :, None, None] + factors[2] * rate_table[None, None, :, None]
    modal = modal / divisor
    inner_rows = basis_table[1:-1]
    result = jnp.einsum('ai,ijkE->ajkE', inner_rows, modal, precision=PRECISE)
    result = jnp.einsum('bj,ajkE->abkE', inner_rows, result, precision=PRECISE)
    return jnp.einsum('ck,abkE->abcE', inner_rows, result, precision=PRECISE)

def schwarz_local(padded, points, counts, tables, factors):
    assembled = assemble(padded, points, 2)
    extended = extend(assembled, points, 2, counts)
    return fast_solve(extended, tables[3], tables[4], factors)

def apply_stiffness(values, tables, factors):
    matrix = jnp.asarray(tables[2], jnp.float32)
    mass_diag = jnp.asarray(tables[1], jnp.float32)
    along_x = jnp.einsum('ai,ijkE->ajkE', matrix, values, precision=PRECISE) * (mass_diag[None, :, None, None] * mass_diag[None, None, :, None]) * factors[0]
    along_y = jnp.einsum('bj,ijkE->ibkE', matrix, values, precision=PRECISE) * (mass_diag[:, None, None, None] * mass_diag[None, None, :, None]) * factors[1]
    along_z = jnp.einsum('ck,ijkE->ijcE', matrix, values, precision=PRECISE) * (mass_diag[:, None, None, None] * mass_diag[None, :, None, None]) * factors[2]
    return along_x + along_y + along_z

def restrict(values, lagrange):
    matrix = jnp.asarray(lagrange, jnp.float32)
    result = jnp.einsum('ia,ijkE->ajkE', matrix, values, precision=PRECISE)
    result = jnp.einsum('jb,ajkE->abkE', matrix, result, precision=PRECISE)
    return jnp.einsum('kc,abkE->abcE', matrix, result, precision=PRECISE)

def prolong(values, lagrange):
    matrix = jnp.asarray(lagrange, jnp.float32)
    result = jnp.einsum('ai,ijkE->ajkE', matrix, values, precision=PRECISE)
    result = jnp.einsum('bj,ajkE->abkE', matrix, result, precision=PRECISE)
    return jnp.einsum('ck,abkE->abcE', matrix, result, precision=PRECISE)

def average_weight(extent, points, at_bottom, at_top, number_type):

    def line_weight(count_in):
        position = np.arange(count_in) % points
        return np.where((position == 0) | (position == points - 1), 0.5, 1.0)
    across = jnp.asarray(line_weight(extent[1]), number_type)
    across = across.at[0].set(jnp.where(at_bottom, 1.0, 0.5)).at[-1].set(jnp.where(at_top, 1.0, 0.5))
    return jnp.asarray(line_weight(extent[0]), number_type)[:, None, None] * across[None, :, None] * jnp.asarray(line_weight(extent[2]), number_type)[None, None, :]

def corner_spread(vertex, counts):
    stacked = jnp.stack([jnp.stack([jnp.stack([vertex[step_x:step_x + counts[0], step_y:step_y + counts[1], step_z:step_z + counts[2]] for step_z in (0, 1)]) for step_y in (0, 1)]) for step_x in (0, 1)])
    return stacked.reshape(2, 2, 2, -1)

def pad_global(values_in, rim_width):
    wrapped = jnp.concatenate([values_in[-rim_width:], values_in, values_in[:rim_width]], 0)
    zero_rows = jnp.zeros((wrapped.shape[0], rim_width, wrapped.shape[2]), values_in.dtype)
    return jnp.concatenate([zero_rows, wrapped, zero_rows], 1)

def reference(local_residual, lengths, coarse_inverse):
    fine_points = ORDER + 1
    mid_points = MID_ORDER + 1
    fine_tables = gll_tables(ORDER)
    mid_tables = gll_tables(MID_ORDER)
    low_tables = gll_tables(1)
    down_fine = interp_table(fine_tables[0], mid_tables[0])
    down_mid = interp_table(mid_tables[0], low_tables[0])
    counts = (NEX, NEY, EZ)
    factors = element_factors(lengths)
    weight_fine = average_weight(local_residual.shape, fine_points, True, True, local_residual.dtype)
    weight_mid = average_weight((NEX * mid_points, NEY * mid_points, EZ * mid_points), mid_points, True, True, local_residual.dtype)

    def smooth(values_in, points, tables, weight):
        local_part = schwarz_local(pad_global(values_in, 2), points, counts, tables, factors)
        summed = assemble(pad_global(to_field(local_part, counts), 1), points, 1)[1:-1, 1:-1]
        return summed * weight
    first_fine = to_elements(smooth(local_residual, fine_points, fine_tables, weight_fine), fine_points)
    local_elements = to_elements(local_residual, fine_points)
    residual_fine = local_elements - apply_stiffness(first_fine, fine_tables, factors)
    residual_mid = restrict(residual_fine, down_fine)
    first_mid = to_elements(smooth(to_field(residual_mid, counts), mid_points, mid_tables, weight_mid), mid_points)
    residual_low = restrict(residual_mid - apply_stiffness(first_mid, mid_tables, factors), down_mid)
    corners = residual_low.reshape(2, 2, 2, NEX, NEY, EZ)
    z_summed = corners[:, :, 0] + jnp.roll(corners[:, :, 1], 1, 4)
    x_summed = z_summed[0] + jnp.roll(z_summed[1], 1, 1)
    coarse_residual = x_summed[0] + jnp.concatenate([jnp.zeros_like(x_summed[1][:, :1]), x_summed[1][:, :-1]], 1)
    vectors = coarse_residual.astype(jnp.bfloat16).reshape(N_GX, EX, N_GY, EY, EZ).transpose(0, 2, 1, 3, 4).reshape(N_GX, SLAB)

    def solve_slab(pair_in):
        return jnp.dot(pair_in[0], pair_in[1], preferred_element_type=jnp.float32)
    solved = lax.map(solve_slab, (coarse_inverse, vectors))
    correction = solved.reshape(N_GX, N_GY, EX, EY, EZ).transpose(0, 2, 1, 3, 4).reshape(NEX, NEY, EZ)
    with_x = jnp.concatenate([correction, correction[:1]], 0)
    with_y = jnp.concatenate([with_x, jnp.zeros_like(with_x[:, :1])], 1)
    with_z = jnp.concatenate([with_y, with_y[:, :, :1]], 2)
    low_values = corner_spread(with_z, counts)
    mid_update = first_mid + prolong(low_values, down_mid)
    post_mid = smooth(to_field(residual_mid - apply_stiffness(mid_update, mid_tables, factors), counts), mid_points, mid_tables, weight_mid)
    mid_result = mid_update + to_elements(post_mid, mid_points)
    fine_update = first_fine + prolong(mid_result, down_fine)
    post_fine = smooth(to_field(local_elements - apply_stiffness(fine_update, fine_tables, factors), counts), fine_points, fine_tables, weight_fine)
    preconditioned = to_field(fine_update, counts) + post_fine
    return (preconditioned, to_field(mid_result, counts), correction)
```

```python
import functools
import math

import jax
import jax.numpy as jnp
import ml_dtypes
import numpy as np
from jax import lax
from jax.experimental import pallas as pl
from jax.experimental.pallas import tpu as pltpu
from jax.sharding import PartitionSpec as P

ORDER = 7
MID_ORDER = 3


def legendre_pair(order, point):
    older = 1.0
    newer = point
    for degree in range(2, order + 1):
        nexter = ((2 * degree - 1) * point * newer - (degree - 1) * older) / degree
        older = newer
        newer = nexter
    return (newer, older)


def jacobi_eigen(matrix):
    count_n = len(matrix)
    work = [list(row_items) for row_items in matrix]
    vectors = [
        [1.0 if row_at == col_at else 0.0 for col_at in range(count_n)] for row_at in range(count_n)
    ]
    for sweep_count in range(60):
        for lower_at in range(count_n):
            for upper_at in range(lower_at + 1, count_n):
                off_value = work[lower_at][upper_at]
                if abs(off_value) < 1e-18 * (
                    abs(work[lower_at][lower_at]) + abs(work[upper_at][upper_at])
                ):
                    continue
                angle_ratio = (work[upper_at][upper_at] - work[lower_at][lower_at]) / (
                    2.0 * off_value
                )
                sign_value = 1.0 if angle_ratio >= 0 else -1.0
                tangent = sign_value / (
                    abs(angle_ratio) + math.sqrt(angle_ratio * angle_ratio + 1.0)
                )
                cosine = 1.0 / math.sqrt(tangent * tangent + 1.0)
                sine_value = tangent * cosine
                for other_at in range(count_n):
                    left_value = work[other_at][lower_at]
                    right_value = work[other_at][upper_at]
                    work[other_at][lower_at] = cosine * left_value - sine_value * right_value
                    work[other_at][upper_at] = sine_value * left_value + cosine * right_value
                for other_at in range(count_n):
                    left_value = work[lower_at][other_at]
                    right_value = work[upper_at][other_at]
                    work[lower_at][other_at] = cosine * left_value - sine_value * right_value
                    work[upper_at][other_at] = sine_value * left_value + cosine * right_value
                for other_at in range(count_n):
                    left_value = vectors[other_at][lower_at]
                    right_value = vectors[other_at][upper_at]
                    vectors[other_at][lower_at] = cosine * left_value - sine_value * right_value
                    vectors[other_at][upper_at] = sine_value * left_value + cosine * right_value
    eigen_list = [work[row_at][row_at] for row_at in range(count_n)]
    ordering = sorted(range(count_n), key=lambda index_at: eigen_list[index_at])
    rates = [eigen_list[index_at] for index_at in ordering]
    basis = [[vectors[row_at][index_at] for index_at in ordering] for row_at in range(count_n)]
    return (rates, basis)


def gll_tables(order):
    point_count = order + 1
    node_list = []
    for node_at in range(point_count):
        point = math.cos(math.pi * node_at / order)
        for newton_step in range(100):
            top_value, lower_value = legendre_pair(order, point)
            point = point - (point * top_value - lower_value) / ((order + 1) * top_value)
        node_list.append(point)
    node_list = node_list[::-1]
    node_list[0] = -1.0
    node_list[-1] = 1.0
    values = [legendre_pair(order, point)[0] for point in node_list]
    weight_list = [2.0 / (order * (order + 1) * value_at**2) for value_at in values]
    derivative = [[0.0] * point_count for row_at in range(point_count)]
    for row_at in range(point_count):
        for col_at in range(point_count):
            if row_at != col_at:
                derivative[row_at][col_at] = values[row_at] / (
                    values[col_at] * (node_list[row_at] - node_list[col_at])
                )
    derivative[0][0] = -order * (order + 1) / 4.0
    derivative[order][order] = order * (order + 1) / 4.0
    stiff_list = [
        [
            sum(
                (
                    derivative[inner_at][row_at]
                    * weight_list[inner_at]
                    * derivative[inner_at][col_at]
                    for inner_at in range(point_count)
                )
            )
            for col_at in range(point_count)
        ]
        for row_at in range(point_count)
    ]
    extent = 3 * order + 1
    big_stiff = [[0.0] * extent for row_at in range(extent)]
    big_mass = [0.0] * extent
    for offset_at in (0, order, 2 * order):
        for row_at in range(point_count):
            big_mass[offset_at + row_at] += weight_list[row_at]
            for col_at in range(point_count):
                big_stiff[offset_at + row_at][offset_at + col_at] += stiff_list[row_at][col_at]
    chosen = list(range(order - 1, 2 * order + 2))
    root_mass = [1.0 / math.sqrt(big_mass[index_at]) for index_at in chosen]
    scaled = [
        [
            root_mass[row_at] * big_stiff[chosen[row_at]][chosen[col_at]] * root_mass[col_at]
            for col_at in range(len(chosen))
        ]
        for row_at in range(len(chosen))
    ]
    rates, basis = jacobi_eigen(scaled)
    eigen_basis = [
        [root_mass[row_at] * basis[row_at][col_at] for col_at in range(len(chosen))]
        for row_at in range(len(chosen))
    ]
    return (
        np.array(node_list),
        np.array(weight_list),
        np.array(stiff_list),
        np.array(eigen_basis),
        np.array(rates),
    )


def interp_table(fine_nodes, coarse_nodes):
    coarse_count = len(coarse_nodes)
    columns = []
    for column in range(coarse_count):
        factors_list = [
            (fine_nodes - coarse_nodes[other_node])
            / (coarse_nodes[column] - coarse_nodes[other_node])
            for other_node in range(coarse_count)
            if other_node != column
        ]
        columns.append(np.prod(np.stack(factors_list), axis=0))
    return np.stack(columns, axis=1)

BF = jnp.bfloat16
F32 = jnp.float32
RING = ((-1, 0), (1, 0), (0, -1), (-1, -1), (1, -1), (0, 1), (-1, 1), (1, 1))
GROUPS = ((0, 2), (2, 5), (5, 8))
AHEAD = (-1, 1, 2, 0)
HALO_ROWS = (32, 32, 32, 8, 8, 32, 8, 8)
FACE_ROWS = (16, 16, 16, 8, 8, 16, 8, 8)
MESH = pl.DeviceIdType.MESH


def offsets(rows):
    return tuple(int(at) for at in np.concatenate([[0], np.cumsum(rows)]))


def blocks(matrix, count):
    return np.kron(np.eye(count), matrix)


def line_extension(points, elements, periodic):
    size = elements * points
    width = size if periodic else size + 4
    table = np.zeros((elements, points + 2, width))

    def column(at):
        if periodic:
            return at % size
        if at < 0:
            return {-2: size, -1: size + 1}[at]
        if at >= size:
            return {size: size + 2, size + 1: size + 3}[at]
        return at

    for element in range(elements):
        start = element * points
        table[element, 0, column(start - 2)] += 1
        for at in range(points):
            table[element, 1 + at, start + at] += 1
        table[element, 1, column(start - 1)] += 1
        table[element, points, column(start + points)] += 1
        table[element, points + 1, column(start + points + 1)] += 1
    return table.reshape(elements * (points + 2), width)


def line_weights(points, elements):
    position = np.arange(points * elements) % points
    return np.where((position == 0) | (position == points - 1), 0.5, 1.0)


def z_back(inner, points, elements):
    table = blocks(inner, elements)
    total = np.array(table)
    size = points * elements
    for element in range(elements):
        low, high = element * points, (element * points - 1) % size
        total[low] = table[low] + table[high]
        total[high] = total[low]
    return (total * line_weights(points, elements)[:, None]).T


RIGHT = (
    "az", "bz", "bzra", "jz", "kz7", "rp", "pz", "azm", "bzm", "rb", "rj", "rk3", "rc", "rcj",
    "s64", "s32", "s256", "s80", "sl80", "s48", "sl48", "select",
)


def fitted(table, right):
    rows, columns = table.shape[-2:]
    more = ((0, -rows % 128 if right else 0), (0, -columns % 128))
    return np.pad(table, ((0, 0),) * (table.ndim - 2) + more)


def side_by_side(*parts):
    return np.concatenate([np.pad(part, ((0, 0), (0, -part.shape[1] % 128))) for part in parts], 1)


def corner_columns(inner_table, elements):
    points = inner_table.shape[0]
    table = np.zeros((elements * points, 256))
    for corner in range(2):
        for lane in range(128):
            element = (lane % elements - corner) % elements
            table[element * points : (element + 1) * points, corner * 128 + lane] = inner_table[:, corner]
    return table


def build_tables(n_gy, ez):
    p, q = ORDER + 1, MID_ORDER + 1
    fine, mid, low = gll_tables(ORDER), gll_tables(MID_ORDER), gll_tables(1)
    jf = interp_table(fine[0], mid[0])
    jm = interp_table(mid[0], low[0])
    k7, w7, s7, l7 = fine[2], np.diag(fine[1]), fine[3], fine[4]
    k3, w3, s3, l3 = mid[2], np.diag(mid[1]), mid[3], mid[4]
    pair, plain = {}, {}
    modes = p + 2
    a1 = blocks(s7.T, 2) @ line_extension(p, 2, False)
    own, sides = a1[:, : 2 * p], {-1: a1[:, 2 * p : 2 * p + 2], 1: a1[:, 2 * p + 2 :]}
    pair["wo"] = np.kron(own, own)
    parts = []
    for dx, dy in RING:
        if dy == 0:
            parts.append(np.kron(sides[dx], own))
        elif dx == 0:
            parts.append(np.concatenate([np.kron(own, sides[dy][:, at : at + 1]) for at in range(2)], 1))
        else:
            parts.append(np.pad(np.kron(sides[dx], sides[dy]), ((0, 0), (0, 4))))
    pair["wh"] = np.concatenate(parts, 1)
    pair["az"] = (blocks(s7.T, ez) @ line_extension(p, ez, True)).T
    inner = s7[1:-1]
    raw = blocks(inner, 2)
    back = np.array(raw)
    back[p - 1] = back[p] = raw[p - 1] + raw[p]
    face = {-1: raw[:1], 1: raw[-1:]}
    pair["bo"] = np.kron(back, back)
    parts, rows = [], []
    edge = {-1: 0, 1: 2 * p - 1}
    for tx, ty in RING:
        scatter = np.zeros((16, 256)) if 0 in (tx, ty) else np.zeros((8, 256))
        if ty == 0:
            parts.append(np.kron(face[tx], back))
            for at in range(16):
                scatter[at, edge[tx] * 16 + at] = 1
        elif tx == 0:
            parts.append(np.kron(back, face[ty]))
            for at in range(16):
                scatter[at, at * 16 + edge[ty]] = 1
        else:
            parts.append(np.pad(np.kron(face[tx], face[ty]), ((0, 7), (0, 0))))
            scatter[0, edge[tx] * 16 + edge[ty]] = 1
        rows.append(scatter)
    pair["bf"] = np.concatenate(parts, 0)
    scat = np.concatenate(rows, 0).T
    plain["scat"] = (scat, BF)
    bz = z_back(inner, p, ez)
    pair["bz"] = bz

    def weights(points):
        line = line_weights(points, 2)
        low_side, high_side = np.zeros(2 * points), np.zeros(2 * points)
        low_side[0], high_side[-1] = 0.5, 0.5
        return np.stack([np.kron(line, line), np.kron(line, low_side), np.kron(line, high_side)], 1)

    wt7, wt3 = weights(p), weights(q)
    columns = np.zeros((256, 128))
    columns[:, 0:3] = wt7
    columns[:96, 3:6] = scat.T @ wt7
    columns[:64, 6:9] = wt3
    columns[:, 9] = np.kron(np.tile(fine[1], 2), np.tile(fine[1], 2))
    plain["columns"] = (columns, F32)

    def three(stiff, mass, count):
        stiff, mass = blocks(stiff, count), blocks(mass, count)
        return np.kron(stiff, mass), np.kron(mass, stiff), np.kron(mass, mass)

    la = np.concatenate(three(jf.T @ k7, jf.T @ w7, 2), 0)
    ra = side_by_side(blocks(w7 @ jf, ez), blocks(k7 @ jf, ez))
    pair["la"] = la
    pair["lar"] = la @ scat
    pair["bzra"] = bz @ ra
    pair["jxy"] = np.kron(blocks(jf.T, 2), blocks(jf.T, 2))
    pair["jz"] = blocks(jf, ez)
    k7x, k7y, _ = three(k7, w7, 2)
    pair["k7"] = np.concatenate([k7x, k7y], 0)
    pair["kz7"] = blocks(k7, ez)
    plain["wz7"] = (np.tile(np.tile(fine[1], ez)[None], (8, 1)), F32)
    pair["lp"] = np.concatenate(three(k7 @ jf, w7 @ jf, 2), 0)
    pair["rp"] = side_by_side(blocks((w7 @ jf).T, ez), blocks((k7 @ jf).T, ez))
    pair["pxy"] = np.kron(blocks(jf, 2), blocks(jf, 2))
    pair["pz"] = blocks(jf.T, ez)

    def factor_rows(elements, scale):
        table = np.zeros((len(elements), 16))
        for at, (ex, ey) in enumerate(elements):
            for d in range(3):
                if scale[d] is not None:
                    table[at, d * 4 + ex * 2 + ey] = scale[d][at]
        return table

    def grid_elements(per):
        return [(x // per, y // per) for x in range(2 * per) for y in range(2 * per)]

    def direction_rows(elements):
        one = np.ones(len(elements))
        return np.concatenate([factor_rows(elements, [one if d == e else None for e in range(3)]) for d in range(3)], 0)

    spread = lambda per: np.kron(np.eye(ez), np.ones((1, per)))
    plain["e7"] = (direction_rows(grid_elements(p)), BF)
    plain["e3"] = (direction_rows(grid_elements(q)), BF)
    plain["e1"] = (direction_rows(grid_elements(2)), BF)
    plain["s64"] = (spread(p), BF)
    plain["s32"] = (spread(q), BF)
    plain["s256"] = (corner_columns(np.ones((1, 2)), ez), BF)
    grid = grid_elements(modes)
    li = np.array([l7[x % modes] for x in range(2 * modes) for y in range(2 * modes)])
    lj = np.array([l7[y % modes] for x in range(2 * modes) for y in range(2 * modes)])
    pair["ld7"] = factor_rows(grid, [li, lj, None])
    plain["le7"] = (factor_rows(grid, [None, None, np.ones(len(grid))]), BF)
    plain["s80"] = (spread(modes), BF)
    pair["sl80"] = spread(modes) * np.tile(l7, ez)[None]

    m3 = q + 2
    ext = np.zeros((4, m3, 6 * q))
    for element in range(4):
        start = q * (element + 1)
        ext[element, 0, start - 2] += 1
        for at in range(q):
            ext[element, 1 + at, start + at] += 1
        ext[element, 1, start - 1] += 1
        ext[element, q, start + q] += 1
        ext[element, q + 1, start + q + 1] += 1
    a1m = blocks(s3.T, 4) @ ext.reshape(4 * m3, 6 * q)
    order = RING + ((0, 0),)
    span = lambda d: slice((d + 1) * 2 * q, (d + 2) * 2 * q)
    wm = [np.kron(a1m[:, span(dx)], a1m[:, span(dy)]) for dx, dy in order]
    pair["wmn"] = np.concatenate(wm[:8], 1)
    pair["wmo"] = wm[8]
    pair["azm"] = (blocks(s3.T, ez) @ line_extension(q, ez, True)).T
    inner3 = s3[1:-1]
    raw3 = blocks(inner3, 4)
    back3 = np.array(raw3[q : 3 * q])
    for at in (q - 1, 2 * q - 1, 3 * q - 1):
        total = raw3[at] + raw3[at + 1]
        for row in (at, at + 1):
            if q <= row < 3 * q:
                back3[row - q] = total
    bm = np.kron(back3, back3)
    pair["bm"] = bm
    bzm = z_back(inner3, q, ez)
    pair["bzm"] = bzm
    ll = np.concatenate(three(jm.T @ k3, jm.T @ w3, 2), 0)
    pair["lb"] = np.concatenate([ll @ ((wt3[:, 0] + extra)[:, None] * bm) for extra in (0, wt3[:, 1], wt3[:, 2])], 0)
    pair["rb"] = bzm @ np.concatenate([corner_columns(w3 @ jm, ez), corner_columns(k3 @ jm, ez)], 1)
    pair["jl"] = np.kron(blocks(jm.T, 2), blocks(jm.T, 2))
    pair["rj"] = corner_columns(jm, ez)
    place = {direction: at for at, direction in enumerate(order)}

    def ring_row(ex, ey, d):
        dx, dy = ex // 2 - 1, ey // 2 - 1
        return place[(dx, dy)] * 16 + d * 4 + (ex % 2) * 2 + ey % 2

    ld3, le3 = np.zeros((576, 144)), np.zeros((576, 144))
    for x in range(24):
        for y in range(24):
            ex, ey = x // m3 + 1, y // m3 + 1
            ld3[x * 24 + y, ring_row(ex, ey, 0)] = l3[x % m3]
            ld3[x * 24 + y, ring_row(ex, ey, 1)] = l3[y % m3]
            le3[x * 24 + y, ring_row(ex, ey, 2)] = 1
    pair["ld3"] = ld3
    plain["le3"] = (le3, BF)
    plain["s48"] = (spread(m3), BF)
    pair["sl48"] = spread(m3) * np.tile(l3, ez)[None]
    er = np.zeros((3, 9, 2 * q, 2 * q, 144))
    for at in range(9):
        for x in range(2 * q):
            for y in range(2 * q):
                for d in range(3):
                    er[d, at, x, y, at * 16 + d * 4 + (x // q) * 2 + y // q] = 1
    plain["er"] = (er.reshape(3 * 576, 144), BF)
    pair["k3"] = np.concatenate(three(k3, w3, 2), 0)
    pair["rk3"] = side_by_side(blocks(w3, ez), blocks(k3, ez))
    vertex_line = lambda table: np.array(
        [[table[at % q, v - at // q] if 0 <= v - at // q <= 1 else 0.0 for v in range(8)] for at in range(6 * q)]
    )
    stiff1, mass1, plain1 = vertex_line(k3 @ jm), vertex_line(w3 @ jm), vertex_line(jm)

    def vertex_columns(left, right, dx, dy):
        table = np.zeros((64, 4, 4, 8))
        for iy in range(4):
            for ix, ahead in enumerate(AHEAD):
                for x in range(2):
                    for y in range(2):
                        table[:, iy, ix, x * 2 + y] = np.kron(
                            left[span(dx), (ahead + 1) * 2 + x], right[span(dy), iy * 2 + y]
                        )
        return table.reshape(64, 128)

    pair["lc"] = np.concatenate(
        [
            vertex_columns(left, right, dx, dy)
            for left, right in ((stiff1, mass1), (mass1, stiff1), (mass1, mass1))
            for dx, dy in order
        ],
        0,
    )
    pair["jc"] = vertex_columns(plain1, plain1, 0, 0)

    def z_vertices(table):
        result = np.zeros((ez, ez * q))
        for element in range(ez):
            for at in range(q):
                result[element, element * q + at] += table[at, 0]
                result[(element + 1) % ez, element * q + at] += table[at, 1]
        return np.tile(result, (4, 1))

    pair["rc"] = side_by_side(z_vertices(w3 @ jm), z_vertices(k3 @ jm))
    pair["rcj"] = z_vertices(jm)
    mask, left = np.zeros((n_gy, 16, 128)), np.zeros((n_gy, 16, 16))
    for gy in range(n_gy):
        for row in range(16):
            vx, vy = row // 8 + row // 4 % 2, row // 2 % 2 + row % 2
            owner = gy + vy // 2
            if owner < n_gy:
                first = owner * 32 + (vx % 2) * 16 + (vy % 2) * 8
                mask[gy, row, first % 128 : first % 128 + 8] = 1
                left[gy, first // 128 + 4 * (vx // 2), row] = 1
    plain["mask"] = (mask.reshape(-1, 128), F32)
    plain["left"] = (left.reshape(-1, 16), BF)
    chosen = np.zeros((8, 32))
    select = np.zeros((32, 8))
    for lane in range(32):
        chosen[lane // 8, lane] = 1
        select[lane, lane % 8] = 1
    plain["chosen"] = (chosen, F32)
    plain["select"] = (select, BF)
    tables = {}
    for name, table in pair.items():
        table = fitted(np.asarray(table, np.float64), name in RIGHT)
        high = table.astype(ml_dtypes.bfloat16)
        tables[name] = np.stack([high, (table - high.astype(np.float64)).astype(ml_dtypes.bfloat16)])
    for name, (table, kind) in plain.items():
        table = fitted(np.asarray(table), name in RIGHT)
        tables[name] = table.astype(ml_dtypes.bfloat16 if kind is BF else np.float32)[None]
    return tables


STAGES = (
    (
        "columns", "wo", "jxy", "jz", "s80", "sl80", "ld7", "le7", "e7", "e3", "e1", "s64", "s32", "s256",
        "wz7", "chosen", "mask",
    ),
    ("wh", "az", "bf", "bo", "la", "bzra", "ld3", "le3", "s48", "sl48", "er", "lar"),
    (
        "wmo", "jl", "rj", "scat", "bz", "k7", "kz7", "wmn", "azm", "lb", "rb", "left", "bm", "bzm", "select",
        "rk3", "k3", "lc", "rc", "jc", "rcj", "rp", "lp", "pxy", "pz",
    ),
)


def pack(tables):
    stacks, places = {}, {}
    for stage, names in enumerate(STAGES):
        for name in names:
            table = tables[name]
            key = (stage, table.dtype.name, table.shape[-1])
            parts = stacks.setdefault(key, [])
            at = sum(part.shape[0] for part in parts)
            height = -(-table.shape[1] // 16) * 16
            for part in table:
                parts.append(np.pad(part, ((0, height - part.shape[0]), (0, 0))))
            places[name] = (key, at, height, table.shape[1])
    keys = tuple(stacks)
    return keys, [np.concatenate(stacks[key], 0) for key in keys], places


class Table:
    def __init__(self, ref, place):
        _, self.at, self.height, self.rows = place
        self.ref = ref
        self.shape = (2, self.rows, ref.shape[-1])

    def __getitem__(self, part):
        part = 0 if part is Ellipsis else part
        return self.ref[self.at + part * self.height : self.at + part * self.height + self.rows, :]

    def piece(self, part, start, rows):
        return self.ref[pl.ds(self.at + part * self.height + start, rows), :]


def dot(a, b):
    return jnp.dot(a, b, preferred_element_type=F32)


def split(x):
    high = x.astype(BF)
    return high, (x - high.astype(F32)).astype(BF)


def wide(x, lanes=128):
    if x.shape[1] == lanes:
        return x
    return jnp.concatenate([x, jnp.zeros((x.shape[0], lanes - x.shape[1]), x.dtype)], 1)


def tall(x, rows):
    if x.shape[0] == rows:
        return x
    return jnp.concatenate([x, jnp.zeros((rows - x.shape[0], x.shape[1]), x.dtype)], 0)


def left3(table, x):
    high, rest = split(tall(x, table.shape[-1]))
    return dot(table[0], high) + dot(table[0], rest) + dot(table[1], high)


def terms3(table, x):
    high, rest = split(tall(x, table.shape[-1]))
    rows = table.shape[1] // 3
    results = []
    for term in range(3):
        lanes = slice(128, 256) if term == 2 else slice(0, 128)
        main, small = table.piece(0, term * rows, rows), table.piece(1, term * rows, rows)
        results.append(dot(main, high[:, lanes]) + dot(main, rest[:, lanes]) + dot(small, high[:, lanes]))
    return results


def right3(x, table):
    high, rest = split(wide(x, table.shape[-2]))
    return dot(high, table[0]) + dot(rest, table[0]) + dot(high, table[1])


def left2(table, x):
    high, rest = split(tall(x, table.shape[-1]))
    return dot(table[...], high) + dot(table[...], rest)


def right2(x, table):
    high, rest = split(wide(x, table.shape[-2]))
    return dot(high, table[...]) + dot(rest, table[...])


KEPT = {
    "fine_f": (768, 128), "mid_f": (192, 128), "low_f": (48, 256), "ring_f": (1728, 128), "inverse7": (400, 128),
    "inverse3": (576, 128), "wt7": (256, 128), "wr7": (96, 128), "wt3": (64, 128), "base_mid": (64, 128),
    "base_low": (16, 256), "local": (256, 128), "first_fine": (256, 128), "base_fine": (256, 128),
    "first_mid": (64, 128), "modal": (400, 128), "modal3": (576, 128), "own_part": (192, 128), "base_ring": (576, 128),
    "ww7": (256, 128),
}


def cycle_kernel(keys, places, n_gx, n_gy, *refs):
    r_hbm, len_hbm, inv_hbm = refs[:3]
    count = len(keys)
    packed = refs[3 : 3 + count]
    out_fine, out_mid, out_low = refs[3 + count : 6 + count]
    stores = refs[6 + count : 6 + 2 * count]
    (
        r_ref, len_ref, inv_ref, rs, fs, hb1, fb1, rm, fm, hb2, fb2, hs1, hs2, st1, st2, held, gs, gb, cb,
        send_sem, recv_sem, gsend, grecv, csend, crecv, in_sem, table_sem,
    ) = refs[6 + 2 * count : -len(KEPT)]
    inputs = [
        pltpu.make_async_copy(source, target, in_sem.at[at])
        for at, (source, target) in enumerate(((len_hbm, len_ref), (r_hbm, r_ref), (inv_hbm, inv_ref)))
    ]
    loads = [pltpu.make_async_copy(packed[at], stores[at], table_sem.at[at]) for at in range(count)]
    for load in inputs + loads:
        load.start()

    def ready(stage):
        for key, load in zip(keys, loads):
            if key[0] == stage:
                load.wait()

    kept = dict(zip(KEPT, refs[-len(KEPT) :]))

    def keep(name, value):
        kept[name][...] = value
        return kept[name]

    t = {name: Table(stores[keys.index(place[0])], place) for name, place in places.items()}
    gx, gy = lax.axis_index("gx"), lax.axis_index("gy")
    last = n_gy - 1
    at_bottom, at_top = gy == 0, gy == last
    not_bottom, not_top = gy > 0, gy < last
    sent = {0: None, 1: not_bottom, 2: not_top}

    def guarded(condition, action):
        if condition is None:
            action()
        else:
            pl.when(condition)(action)

    def exchange(phase, source, buffer, rows):
        at = offsets(rows)

        def group(number):
            def action():
                for index in range(*GROUPS[number]):
                    tx, ty = RING[index]
                    slot = RING.index((-tx, -ty))
                    landing = (0, 2, 1)[number]
                    pltpu.make_async_remote_copy(
                        src_ref=source(index),
                        dst_ref=buffer.at[pl.ds(at[slot], rows[slot])],
                        send_sem=send_sem.at[phase, number],
                        recv_sem=recv_sem.at[phase, landing],
                        device_id=(lax.rem(gx + (tx + n_gx), n_gx), gy + ty),
                        device_id_type=MESH,
                    ).start()

            return action

        for number in range(3):
            guarded(sent[number], group(number))

    def settle(phase, sems, buffer, rows):
        at = offsets(rows)
        for number in range(3):
            first, end = GROUPS[number]
            piece = buffer.at[pl.ds(at[first], at[end] - at[first])]
            guarded(sent[number], lambda: pltpu.make_async_copy(piece, piece, sems.at[phase, number]).wait())

    def clear(number):
        first, end = GROUPS[number]
        for buffer, rows in (
            (fs, (16,) * 8), (hb1, HALO_ROWS), (fb1, FACE_ROWS), (rm, (64,) * 8),
            (fm, (64,) * 8), (hb2, HALO_ROWS), (fb2, FACE_ROWS),
        ):
            at = offsets(rows)
            buffer[at[first] : at[end], :] = jnp.zeros((at[end] - at[first], buffer.shape[1]), F32)

    @pl.when(at_bottom)
    def _():
        clear(1)
        cb[0:32, :] = jnp.zeros((32, 32), F32)

    @pl.when(at_top)
    def _():
        clear(2)
        cb[64:96, :] = jnp.zeros((32, 32), F32)

    @pl.when(gy >= last - 1)
    def _():
        cb[96:128, :] = jnp.zeros((32, 32), F32)

    def halo(field, stage):
        at = offsets(HALO_ROWS)
        for index, (tx, ty) in enumerate(RING):
            xs, ys = (14, 0)[tx < 0], (14, 0)[ty < 0]
            if ty == 0:
                stage[at[index] : at[index] + 32, :] = field[xs : xs + 2, :, :].reshape(32, 64)
            elif tx == 0:
                stage[at[index] : at[index] + 16, :] = field[:, ys, :]
                stage[at[index] + 16 : at[index] + 32, :] = field[:, ys + 1, :]
            else:
                stage[at[index] : at[index] + 2, :] = field[xs, ys : ys + 2, :]
                stage[at[index] + 2 : at[index] + 4, :] = field[xs + 1, ys : ys + 2, :]
                stage[at[index] + 4 : at[index] + 8, :] = jnp.zeros((4, 64), F32)

    at_halo, at_face = offsets(HALO_ROWS), offsets(FACE_ROWS)

    inputs[0].wait()
    own_f = 8 * 16
    for ex in range(2):
        a, b, c = len_ref[0, ex], len_ref[1, ex], len_ref[2, ex]
        fs[own_f + ex * 2 : own_f + ex * 2 + 2, :] = b * c / (2.0 * a)
        fs[own_f + 4 + ex * 2 : own_f + 6 + ex * 2, :] = a * c / (2.0 * b)
        fs[own_f + 8 + ex * 2 : own_f + 10 + ex * 2, :] = a * b / (2.0 * c)
    fs[own_f + 12 : own_f + 16, :] = jnp.zeros((4, 8), F32)
    inputs[1].wait()
    halo(r_ref, hs1)
    exchange(1, lambda index: hs1.at[pl.ds(at_halo[index], HALO_ROWS[index])], hb1, HALO_ROWS)
    exchange(0, lambda index: fs.at[pl.ds(own_f, 16)], fs, (16,) * 8)

    bottom_on = jnp.where(at_bottom, 1.0, 0.0)
    top_on = jnp.where(at_top, 1.0, 0.0)

    ready(0)
    columns = t["columns"][...]

    def wall_weight(rows, at):
        piece = columns[0:rows]
        return piece[:, at : at + 1] + bottom_on * piece[:, at + 1 : at + 2] + top_on * piece[:, at + 2 : at + 3]

    wt7 = keep("wt7", jnp.broadcast_to(wall_weight(256, 0), (256, 128)))
    wr7 = keep("wr7", jnp.broadcast_to(wall_weight(96, 3), (96, 128)))
    wt3 = keep("wt3", jnp.broadcast_to(wall_weight(64, 6), (64, 128)))
    ww7 = keep("ww7", jnp.broadcast_to(columns[:, 9:10], (256, 128)))
    r = wide(r_ref[...].reshape(256, 64))
    f_own = wide(fs[own_f : own_f + 16, :])
    d7 = left3(t["ld7"], right2(f_own, t["s80"])) + left2(t["le7"], right3(f_own, t["sl80"]))
    inverse7 = keep("inverse7", jnp.where(d7 > 0.0, 1.0 / jnp.where(d7 > 0.0, d7, 1.0), 0.0))
    modal = keep("modal", left3(t["wo"], r))
    base_mid = keep("base_mid", right3(left3(t["jxy"], r), t["jz"]))
    fine_f = keep("fine_f", left2(t["e7"], right2(f_own, t["s64"])))
    mid_f = keep("mid_f", left2(t["e3"], right2(f_own, t["s32"])))
    low_f = keep("low_f", left2(t["e1"], right2(f_own, t["s256"])))

    def fine_back(modal, buffer, stage, phase):
        modal = right3(modal, t["az"]) * inverse7[...]
        stage[...] = left3(t["bf"], modal)[:, : stage.shape[1]]
        exchange(phase, lambda index: stage.at[pl.ds(at_face[index], FACE_ROWS[index])], buffer, FACE_ROWS)
        return left3(t["bo"], modal)

    ready(1)
    settle(1, recv_sem, hb1, HALO_ROWS)
    modal = modal[...] + left3(t["wh"], wide(hb1[...]))
    local = keep("local", fine_back(modal, fb1, st1, 2) * wt7[...])
    own_part = keep("own_part", jnp.concatenate(terms3(t["la"], right3(local[...], t["bzra"])), 0))
    settle(0, recv_sem, fs, (16,) * 8)
    ring_f = wide(fs[...])
    d3 = left3(t["ld3"], right2(ring_f, t["s48"])) + left2(t["le3"], right3(ring_f, t["sl48"]))
    inverse3 = keep("inverse3", jnp.where(d3 > 0.0, 1.0 / jnp.where(d3 > 0.0, d3, 1.0), 0.0))
    ring_f = keep("ring_f", left2(t["er"], right2(ring_f, t["s32"])))

    settle(2, recv_sem, fb1, FACE_ROWS)
    faces = wide(fb1[...]) * wr7[...]
    face_part = terms3(t["lar"], right3(faces, t["bzra"]))
    residual_mid = base_mid[...] - (
        mid_f[0:64] * (own_part[0:64] + face_part[0])
        + mid_f[64:128] * (own_part[64:128] + face_part[1])
        + mid_f[128:192] * (own_part[128:192] + face_part[2])
    )
    rm[512:576, :] = residual_mid[:, 0:32]
    exchange(3, lambda index: rm.at[pl.ds(512, 64)], rm, (64,) * 8)

    ready(2)
    own_modal = keep("modal3", left3(t["wmo"], residual_mid))
    base_low = keep("base_low", right3(left3(t["jl"], residual_mid), t["rj"]))
    first_fine = keep("first_fine", right3(local[...] + left2(t["scat"], faces), t["bz"]))
    massed = left3(t["k7"], first_fine[...] * t["wz7"][...][0:1])
    along_z = right3(first_fine[...], t["kz7"]) * ww7[...]
    base_fine = keep(
        "base_fine",
        wide(r_ref[...].reshape(256, 64))
        - (fine_f[0:256] * massed[0:256] + fine_f[256:512] * massed[256:512] + fine_f[512:768] * along_z),
    )

    settle(3, recv_sem, rm, (64,) * 8)
    modal3 = own_modal[...] + left3(t["wmn"], wide(rm[0:512, :]))
    modal3 = right3(modal3, t["azm"]) * inverse3[...]
    variant = jnp.where(at_bottom, 1, jnp.where(at_top, 2, 0))
    rows = pl.multiple_of(variant * 48, 16)
    high, rest = split(tall(modal3, t["lb"].shape[-1]))
    lb_high, lb_rest = t["lb"].piece(0, rows, 48), t["lb"].piece(1, rows, 48)
    low = dot(lb_high, high) + dot(lb_high, rest) + dot(lb_rest, high)
    low = right3(low, t["rb"])
    low = base_low[...] - (
        low_f[0:16] * low[0:16, 0:256] + low_f[16:32] * low[16:32, 0:256] + low_f[32:48] * low[32:48, 256:512]
    )
    wall = pl.multiple_of(gy * 16, 16)
    high, rest = split(tall((low[:, 0:128] + low[:, 128:256]) * t["mask"].piece(0, wall, 16), 128))
    lefts = t["left"].piece(0, wall, 16)
    message = (dot(lefts, high) + dot(lefts, rest))[0:8]
    gs[...] = message

    def send_slab(step, ahead):
        slot = step + jnp.where(ahead == 0, -1, n_gy - 1)
        pltpu.make_async_remote_copy(
            src_ref=gs,
            dst_ref=gb.at[slot],
            send_sem=gsend,
            recv_sem=grecv,
            device_id=(lax.rem(gx + ahead, n_gx), lax.rem(gy + step, n_gy)),
            device_id_type=MESH,
        ).start()

    for step in range(1, n_gy):
        send_slab(step, 0)
    for step in range(n_gy):
        send_slab(step, 1)

    first_mid = keep("first_mid", right3(left3(t["bm"], modal3) * wt3[...], t["bzm"]))
    fm[512:576, :] = first_mid[:, 0:32]
    exchange(4, lambda index: fm.at[pl.ds(512, 64)], fm, (64,) * 8)

    pltpu.make_async_copy(gb, gb, grecv).wait()
    here = gs[...] + jnp.sum(gb[0 : n_gy - 1], axis=0)
    behind = jnp.sum(gb[n_gy - 1 :], axis=0)
    inputs[2].wait()
    chunks = inv_ref.shape[2] // 128
    vector = here + pltpu.roll(behind, 4, 0)
    row = lax.broadcasted_iota(jnp.int32, (8, 128), 0)
    vector = jnp.concatenate([jnp.where(row == chunk, vector, 0.0) for chunk in range(chunks)], 1)
    vector = tall(vector, 16).astype(BF)
    inverse = tall(inv_ref[0], 128)
    solved = lax.dot_general(vector, inverse, (((1,), (1,)), ((), ())), preferred_element_type=F32)
    solved = jnp.sum(solved, axis=0, keepdims=True)
    solved = jnp.broadcast_to(solved, (8, 128)) * t["chosen"][...]
    own_c = (4 + 3) * 8
    cb[own_c : own_c + 8, :] = solved[:, 0:32]

    def send_correction(iy):
        def action():
            for ix, ahead in enumerate(AHEAD):
                if (ahead, iy - 1) != (0, 0):
                    pltpu.make_async_remote_copy(
                        src_ref=cb.at[pl.ds(own_c, 8)],
                        dst_ref=cb.at[pl.ds((iy * 4 + ix) * 8, 8)],
                        send_sem=csend.at[iy],
                        recv_sem=crecv.at[iy],
                        device_id=(lax.rem(gx - ahead + n_gx, n_gx), gy - (iy - 1)),
                        device_id_type=MESH,
                    ).start()

        return action

    to_group = (not_top, None, not_bottom, gy > 1)
    from_group = (not_bottom, None, not_top, gy < last - 1)
    for iy in range(4):
        guarded(to_group[iy], send_correction(iy))

    def settle_corrections(sems, conditions):
        for iy in range(4):
            piece = cb.at[pl.ds(iy * 32, 24 if iy == 1 else 32)]
            guarded(conditions[iy], lambda: pltpu.make_async_copy(piece, piece, sems.at[iy]).wait())

    low_out = right2(tall(solved, 16), t["select"])
    out_low[0] = low_out[0:2, 0:8]
    out_low[1] = low_out[2:4, 0:8]
    settle(4, recv_sem, fm, (64,) * 8)
    turned = right3(wide(fm[...]), t["rk3"])
    parts = []
    for at in range(9):
        piece = terms3(t["k3"], turned[at * 64 : (at + 1) * 64])
        parts.append(
            wide(rm[at * 64 : (at + 1) * 64, :])
            - (
                ring_f[at * 64 : (at + 1) * 64] * piece[0]
                + ring_f[576 + at * 64 : 576 + (at + 1) * 64] * piece[1]
                + ring_f[1152 + at * 64 : 1152 + (at + 1) * 64] * piece[2]
            )
        )
    base_ring = keep("base_ring", jnp.concatenate(parts, 0))
    modal3 = keep("modal3", left3(t["wmn"], base_ring[0:512]) + left3(t["wmo"], base_ring[512:576]))

    settle_corrections(crecv, from_group)
    corrections = wide(cb[...])
    change = terms3(t["lc"], right3(corrections, t["rc"]))
    change = (
        ring_f[0:576] * change[0]
        + ring_f[576:1152] * change[1]
        + ring_f[1152:1728] * change[2]
    )
    modal3 = modal3[...] - left3(t["wmn"], change[0:512]) - left3(t["wmo"], change[512:576])
    modal3 = right3(modal3, t["azm"]) * inverse3[...]
    held[0:64, :] = first_mid[...] + right3(left3(t["jc"], corrections), t["rcj"])
    mid_result = held[0:64, :] + right3(left3(t["bm"], modal3) * wt3[...], t["bzm"])

    turned = right3(mid_result, t["rp"])
    turned = terms3(t["lp"], turned)
    residual = base_fine[...] - (
        fine_f[0:256] * turned[0]
        + fine_f[256:512] * turned[1]
        + fine_f[512:768] * turned[2]
    )
    rs[...] = residual[:, 0:64].reshape(16, 16, 64)
    halo(rs, hs2)
    exchange(5, lambda index: hs2.at[pl.ds(at_halo[index], HALO_ROWS[index])], hb2, HALO_ROWS)
    out_mid[...] = mid_result[:, 0:32].reshape(8, 8, 32)
    modal = keep("modal", left3(t["wo"], residual))
    held[...] = first_fine[...] + right3(left3(t["pxy"], mid_result), t["pz"])
    settle(5, recv_sem, hb2, HALO_ROWS)
    modal = modal[...] + left3(t["wh"], wide(hb2[...]))
    local = fine_back(modal, fb2, st2, 6) * wt7[...]
    held[...] = held[...] + right3(local, t["bz"])
    settle(6, recv_sem, fb2, FACE_ROWS)
    result = held[...] + left2(t["scat"], right3(wide(fb2[...]) * wr7[...], t["bz"]))
    out_fine[...] = result[:, 0:64].reshape(16, 16, 64)

    for phase, buffer, rows in (
        (0, fs, (16,) * 8), (1, hb1, HALO_ROWS), (2, fb1, FACE_ROWS), (3, rm, (64,) * 8),
        (4, fm, (64,) * 8), (5, hb2, HALO_ROWS), (6, fb2, FACE_ROWS),
    ):
        settle(phase, send_sem, buffer, rows)
    pltpu.make_async_copy(gb, gb, gsend).wait()
    settle_corrections(csend, to_group)


def shards(n_gx, n_gy, local_residual, lengths, coarse_inverse):
    keys, packed, places = pack(build_tables(n_gy, lengths.shape[3]))
    vmem = pl.BlockSpec(memory_space=pltpu.VMEM)
    modes = lengths.shape[3] * (ORDER + 3)
    scratch = [pltpu.VMEM(table.shape, BF if key[1] == "bfloat16" else F32) for key, table in zip(keys, packed)]
    scratch += [
        pltpu.VMEM(local_residual.shape, F32),
        pltpu.VMEM(lengths.shape, F32),
        pltpu.VMEM(coarse_inverse.shape, BF),
        pltpu.VMEM((16, 16, 64), F32),
        pltpu.VMEM((144, 8), F32),
        pltpu.VMEM((160, 64), F32),
        pltpu.VMEM((96, modes), F32),
        pltpu.VMEM((576, 32), F32),
        pltpu.VMEM((576, 32), F32),
        pltpu.VMEM((160, 64), F32),
        pltpu.VMEM((96, modes), F32),
        pltpu.VMEM((160, 64), F32),
        pltpu.VMEM((160, 64), F32),
        pltpu.VMEM((96, modes), F32),
        pltpu.VMEM((96, modes), F32),
        pltpu.VMEM((256, 128), F32),
        pltpu.VMEM((8, 128), F32),
        pltpu.VMEM((2 * n_gy - 1, 8, 128), F32),
        pltpu.VMEM((128, 32), F32),
        pltpu.SemaphoreType.DMA((7, 3)),
        pltpu.SemaphoreType.DMA((7, 3)),
        pltpu.SemaphoreType.DMA,
        pltpu.SemaphoreType.DMA,
        pltpu.SemaphoreType.DMA((4,)),
        pltpu.SemaphoreType.DMA((4,)),
        pltpu.SemaphoreType.DMA((3,)),
        pltpu.SemaphoreType.DMA((len(keys),)),
    ]
    scratch += [pltpu.VMEM(shape, F32) for shape in KEPT.values()]
    return pl.pallas_call(
        functools.partial(cycle_kernel, keys, places, n_gx, n_gy),
        out_shape=(
            jax.ShapeDtypeStruct((16, 16, 64), F32),
            jax.ShapeDtypeStruct((8, 8, 32), F32),
            jax.ShapeDtypeStruct((2, 2, 8), F32),
        ),
        in_specs=[pl.BlockSpec(memory_space=pl.ANY)] * (3 + len(keys)),
        out_specs=(vmem, vmem, vmem),
        scratch_shapes=scratch,
        compiler_params=pltpu.CompilerParams(has_side_effects=True, vmem_limit_bytes=60 * 1024 * 1024),
    )(local_residual, lengths, coarse_inverse, *[jnp.asarray(table) for table in packed])


def solution(mesh):
    in_specs = (P("gx", "gy", None), P(None, "gx", "gy", None), P("gx", "gy", None))
    out_specs = (P("gx", "gy", None), P("gx", "gy", None), P("gx", "gy", None))
    return jax.shard_map(
        functools.partial(shards, mesh.shape["gx"], mesh.shape["gy"]),
        mesh=mesh,
        in_specs=in_specs,
        out_specs=out_specs,
        check_vma=False,
    )
```

```python
import functools
import math

import jax
import jax.numpy as jnp
import ml_dtypes
import numpy as np
from jax import lax
from jax.experimental import pallas as pl
from jax.experimental.pallas import tpu as pltpu
from jax.sharding import PartitionSpec as P

ORDER = 7
MID_ORDER = 3


def legendre_pair(order, point):
    older = 1.0
    newer = point
    for degree in range(2, order + 1):
        nexter = ((2 * degree - 1) * point * newer - (degree - 1) * older) / degree
        older = newer
        newer = nexter
    return (newer, older)


def jacobi_eigen(matrix):
    count_n = len(matrix)
    work = [list(row_items) for row_items in matrix]
    vectors = [
        [1.0 if row_at == col_at else 0.0 for col_at in range(count_n)] for row_at in range(count_n)
    ]
    for sweep_count in range(60):
        for lower_at in range(count_n):
            for upper_at in range(lower_at + 1, count_n):
                off_value = work[lower_at][upper_at]
                if abs(off_value) < 1e-18 * (
                    abs(work[lower_at][lower_at]) + abs(work[upper_at][upper_at])
                ):
                    continue
                angle_ratio = (work[upper_at][upper_at] - work[lower_at][lower_at]) / (
                    2.0 * off_value
                )
                sign_value = 1.0 if angle_ratio >= 0 else -1.0
                tangent = sign_value / (
                    abs(angle_ratio) + math.sqrt(angle_ratio * angle_ratio + 1.0)
                )
                cosine = 1.0 / math.sqrt(tangent * tangent + 1.0)
                sine_value = tangent * cosine
                for other_at in range(count_n):
                    left_value = work[other_at][lower_at]
                    right_value = work[other_at][upper_at]
                    work[other_at][lower_at] = cosine * left_value - sine_value * right_value
                    work[other_at][upper_at] = sine_value * left_value + cosine * right_value
                for other_at in range(count_n):
                    left_value = work[lower_at][other_at]
                    right_value = work[upper_at][other_at]
                    work[lower_at][other_at] = cosine * left_value - sine_value * right_value
                    work[upper_at][other_at] = sine_value * left_value + cosine * right_value
                for other_at in range(count_n):
                    left_value = vectors[other_at][lower_at]
                    right_value = vectors[other_at][upper_at]
                    vectors[other_at][lower_at] = cosine * left_value - sine_value * right_value
                    vectors[other_at][upper_at] = sine_value * left_value + cosine * right_value
    eigen_list = [work[row_at][row_at] for row_at in range(count_n)]
    ordering = sorted(range(count_n), key=lambda index_at: eigen_list[index_at])
    rates = [eigen_list[index_at] for index_at in ordering]
    basis = [[vectors[row_at][index_at] for index_at in ordering] for row_at in range(count_n)]
    return (rates, basis)


def gll_tables(order):
    point_count = order + 1
    node_list = []
    for node_at in range(point_count):
        point = math.cos(math.pi * node_at / order)
        for newton_step in range(100):
            top_value, lower_value = legendre_pair(order, point)
            point = point - (point * top_value - lower_value) / ((order + 1) * top_value)
        node_list.append(point)
    node_list = node_list[::-1]
    node_list[0] = -1.0
    node_list[-1] = 1.0
    values = [legendre_pair(order, point)[0] for point in node_list]
    weight_list = [2.0 / (order * (order + 1) * value_at**2) for value_at in values]
    derivative = [[0.0] * point_count for row_at in range(point_count)]
    for row_at in range(point_count):
        for col_at in range(point_count):
            if row_at != col_at:
                derivative[row_at][col_at] = values[row_at] / (
                    values[col_at] * (node_list[row_at] - node_list[col_at])
                )
    derivative[0][0] = -order * (order + 1) / 4.0
    derivative[order][order] = order * (order + 1) / 4.0
    stiff_list = [
        [
            sum(
                (
                    derivative[inner_at][row_at]
                    * weight_list[inner_at]
                    * derivative[inner_at][col_at]
                    for inner_at in range(point_count)
                )
            )
            for col_at in range(point_count)
        ]
        for row_at in range(point_count)
    ]
    extent = 3 * order + 1
    big_stiff = [[0.0] * extent for row_at in range(extent)]
    big_mass = [0.0] * extent
    for offset_at in (0, order, 2 * order):
        for row_at in range(point_count):
            big_mass[offset_at + row_at] += weight_list[row_at]
            for col_at in range(point_count):
                big_stiff[offset_at + row_at][offset_at + col_at] += stiff_list[row_at][col_at]
    chosen = list(range(order - 1, 2 * order + 2))
    root_mass = [1.0 / math.sqrt(big_mass[index_at]) for index_at in chosen]
    scaled = [
        [
            root_mass[row_at] * big_stiff[chosen[row_at]][chosen[col_at]] * root_mass[col_at]
            for col_at in range(len(chosen))
        ]
        for row_at in range(len(chosen))
    ]
    rates, basis = jacobi_eigen(scaled)
    eigen_basis = [
        [root_mass[row_at] * basis[row_at][col_at] for col_at in range(len(chosen))]
        for row_at in range(len(chosen))
    ]
    return (
        np.array(node_list),
        np.array(weight_list),
        np.array(stiff_list),
        np.array(eigen_basis),
        np.array(rates),
    )


def interp_table(fine_nodes, coarse_nodes):
    coarse_count = len(coarse_nodes)
    columns = []
    for column in range(coarse_count):
        factors_list = [
            (fine_nodes - coarse_nodes[other_node])
            / (coarse_nodes[column] - coarse_nodes[other_node])
            for other_node in range(coarse_count)
            if other_node != column
        ]
        columns.append(np.prod(np.stack(factors_list), axis=0))
    return np.stack(columns, axis=1)

BF = jnp.bfloat16
F32 = jnp.float32
RING = ((-1, 0), (1, 0), (0, -1), (-1, -1), (1, -1), (0, 1), (-1, 1), (1, 1))
GROUPS = ((0, 2), (2, 5), (5, 8))
AHEAD = (-1, 1, 2, 0)
FACE_ROWS = (16, 16, 16, 8, 8, 16, 8, 8)
BLOCK_ROWS = (16,) * 8
MESH = pl.DeviceIdType.MESH


def offsets(rows):
    return tuple(int(at) for at in np.concatenate([[0], np.cumsum(rows)]))


def blocks(matrix, count):
    return np.kron(np.eye(count), matrix)


def line_extension(points, elements, periodic):
    size = elements * points
    width = size if periodic else size + 4
    table = np.zeros((elements, points + 2, width))

    def column(at):
        if periodic:
            return at % size
        if at < 0:
            return {-2: size, -1: size + 1}[at]
        if at >= size:
            return {size: size + 2, size + 1: size + 3}[at]
        return at

    for element in range(elements):
        start = element * points
        table[element, 0, column(start - 2)] += 1
        for at in range(points):
            table[element, 1 + at, start + at] += 1
        table[element, 1, column(start - 1)] += 1
        table[element, points, column(start + points)] += 1
        table[element, points + 1, column(start + points + 1)] += 1
    return table.reshape(elements * (points + 2), width)


def line_weights(points, elements):
    position = np.arange(points * elements) % points
    return np.where((position == 0) | (position == points - 1), 0.5, 1.0)


def z_back(inner, points, elements):
    table = blocks(inner, elements)
    total = np.array(table)
    size = points * elements
    for element in range(elements):
        low, high = element * points, (element * points - 1) % size
        total[low] = table[low] + table[high]
        total[high] = total[low]
    return (total * line_weights(points, elements)[:, None]).T


RIGHT = (
    "az", "bz", "bzra", "jz", "kz7", "rp", "pz", "azm", "bzm", "rb", "rj", "rk3", "rc", "rcj",
    "s64", "s32", "s256", "s80", "sl80", "s48", "sl48", "select",
)


def fitted(table, right):
    rows, columns = table.shape[-2:]
    more = ((0, -rows % 128 if right else 0), (0, -columns % 128))
    return np.pad(table, ((0, 0),) * (table.ndim - 2) + more)


def side_by_side(*parts):
    return np.concatenate([np.pad(part, ((0, 0), (0, -part.shape[1] % 128))) for part in parts], 1)


def corner_columns(inner_table, elements):
    points = inner_table.shape[0]
    table = np.zeros((elements * points, 256))
    for corner in range(2):
        for lane in range(128):
            element = (lane % elements - corner) % elements
            table[element * points : (element + 1) * points, corner * 128 + lane] = inner_table[:, corner]
    return table


def build_tables(n_gy, ez):
    p, q = ORDER + 1, MID_ORDER + 1
    fine, mid, low = gll_tables(ORDER), gll_tables(MID_ORDER), gll_tables(1)
    jf = interp_table(fine[0], mid[0])
    jm = interp_table(mid[0], low[0])
    k7, w7, s7, l7 = fine[2], np.diag(fine[1]), fine[3], fine[4]
    k3, w3, s3, l3 = mid[2], np.diag(mid[1]), mid[3], mid[4]
    pair, plain = {}, {}
    modes = p + 2
    a1 = blocks(s7.T, 2) @ line_extension(p, 2, False)
    own, sides = a1[:, : 2 * p], {-1: a1[:, 2 * p : 2 * p + 2], 1: a1[:, 2 * p + 2 :]}
    pair["wo"] = np.kron(own, own)
    halves = []
    for half in range(2):
        layer = slice(half, half + 1)
        parts = []
        for dx, dy in RING:
            if dy == 0:
                parts.append(np.kron(sides[dx][:, layer], own))
            elif dx == 0:
                parts.append(np.kron(own, sides[dy][:, layer]))
            else:
                parts.append(np.pad(np.kron(sides[dx], sides[dy][:, layer]), ((0, 0), (0, 6))))
        halves.append(np.concatenate(parts, 1))
    pair["wh"] = side_by_side(*halves)
    pair["az"] = (blocks(s7.T, ez) @ line_extension(p, ez, True)).T
    inner = s7[1:-1]
    raw = blocks(inner, 2)
    back = np.array(raw)
    back[p - 1] = back[p] = raw[p - 1] + raw[p]
    face = {-1: raw[:1], 1: raw[-1:]}
    pair["bo"] = np.kron(back, back)
    parts, rows = [], []
    edge = {-1: 0, 1: 2 * p - 1}
    for tx, ty in RING:
        scatter = np.zeros((16, 256)) if 0 in (tx, ty) else np.zeros((8, 256))
        if ty == 0:
            parts.append(np.kron(face[tx], back))
            for at in range(16):
                scatter[at, edge[tx] * 16 + at] = 1
        elif tx == 0:
            parts.append(np.kron(back, face[ty]))
            for at in range(16):
                scatter[at, at * 16 + edge[ty]] = 1
        else:
            parts.append(np.pad(np.kron(face[tx], face[ty]), ((0, 7), (0, 0))))
            scatter[0, edge[tx] * 16 + edge[ty]] = 1
        rows.append(scatter)
    pair["bf"] = np.concatenate(parts, 0)
    scat = np.concatenate(rows, 0).T
    plain["scat"] = (scat, BF)
    bz = z_back(inner, p, ez)
    pair["bz"] = bz

    def weights(points):
        line = line_weights(points, 2)
        low_side, high_side = np.zeros(2 * points), np.zeros(2 * points)
        low_side[0], high_side[-1] = 0.5, 0.5
        return np.stack([np.kron(line, line), np.kron(line, low_side), np.kron(line, high_side)], 1)

    wt7, wt3 = weights(p), weights(q)
    columns = np.zeros((256, 128))
    columns[:, 0:3] = wt7
    columns[:96, 3:6] = scat.T @ wt7
    columns[:64, 6:9] = wt3
    columns[:, 9] = np.kron(np.tile(fine[1], 2), np.tile(fine[1], 2))
    plain["columns"] = (columns, F32)

    def three(stiff, mass, count):
        stiff, mass = blocks(stiff, count), blocks(mass, count)
        return np.kron(stiff, mass), np.kron(mass, stiff), np.kron(mass, mass)

    la = np.concatenate(three(jf.T @ k7, jf.T @ w7, 2), 0)
    ra = side_by_side(blocks(w7 @ jf, ez), blocks(k7 @ jf, ez))
    pair["la"] = la
    pair["lar"] = la @ scat
    pair["bzra"] = bz @ ra
    pair["jxy"] = np.kron(blocks(jf.T, 2), blocks(jf.T, 2))
    pair["jz"] = blocks(jf, ez)
    k7x, k7y, _ = three(k7, w7, 2)
    pair["k7"] = np.concatenate([k7x, k7y], 0)
    pair["kz7"] = blocks(k7, ez)
    plain["wz7"] = (np.tile(np.tile(fine[1], ez)[None], (8, 1)), F32)
    pair["lp"] = np.concatenate(three(k7 @ jf, w7 @ jf, 2), 0)
    pair["rp"] = side_by_side(blocks((w7 @ jf).T, ez), blocks((k7 @ jf).T, ez))
    pair["pxy"] = np.kron(blocks(jf, 2), blocks(jf, 2))
    pair["pz"] = blocks(jf.T, ez)

    def factor_rows(elements, scale):
        table = np.zeros((len(elements), 16))
        for at, (ex, ey) in enumerate(elements):
            for d in range(3):
                if scale[d] is not None:
                    table[at, d * 4 + ex * 2 + ey] = scale[d][at]
        return table

    def grid_elements(per):
        return [(x // per, y // per) for x in range(2 * per) for y in range(2 * per)]

    def direction_rows(elements):
        one = np.ones(len(elements))
        return np.concatenate([factor_rows(elements, [one if d == e else None for e in range(3)]) for d in range(3)], 0)

    spread = lambda per: np.kron(np.eye(ez), np.ones((1, per)))
    plain["e7"] = (direction_rows(grid_elements(p)), BF)
    plain["e3"] = (direction_rows(grid_elements(q)), BF)
    plain["e1"] = (direction_rows(grid_elements(2)), BF)
    plain["s64"] = (spread(p), BF)
    plain["s32"] = (spread(q), BF)
    plain["s256"] = (corner_columns(np.ones((1, 2)), ez), BF)
    grid = grid_elements(modes)
    li = np.array([l7[x % modes] for x in range(2 * modes) for y in range(2 * modes)])
    lj = np.array([l7[y % modes] for x in range(2 * modes) for y in range(2 * modes)])
    pair["ld7"] = factor_rows(grid, [li, lj, None])
    plain["le7"] = (factor_rows(grid, [None, None, np.ones(len(grid))]), BF)
    plain["s80"] = (spread(modes), BF)
    pair["sl80"] = spread(modes) * np.tile(l7, ez)[None]

    m3 = q + 2
    ext = np.zeros((4, m3, 6 * q))
    for element in range(4):
        start = q * (element + 1)
        ext[element, 0, start - 2] += 1
        for at in range(q):
            ext[element, 1 + at, start + at] += 1
        ext[element, 1, start - 1] += 1
        ext[element, q, start + q] += 1
        ext[element, q + 1, start + q + 1] += 1
    a1m = blocks(s3.T, 4) @ ext.reshape(4 * m3, 6 * q)
    order = RING + ((0, 0),)
    span = lambda d: slice((d + 1) * 2 * q, (d + 2) * 2 * q)
    wm = [np.kron(a1m[:, span(dx)], a1m[:, span(dy)]) for dx, dy in order]
    pair["wmn"] = np.concatenate(wm[:8], 1)
    pair["wmo"] = wm[8]
    pair["azm"] = (blocks(s3.T, ez) @ line_extension(q, ez, True)).T
    inner3 = s3[1:-1]
    raw3 = blocks(inner3, 4)
    back3 = np.array(raw3[q : 3 * q])
    for at in (q - 1, 2 * q - 1, 3 * q - 1):
        total = raw3[at] + raw3[at + 1]
        for row in (at, at + 1):
            if q <= row < 3 * q:
                back3[row - q] = total
    bm = np.kron(back3, back3)
    pair["bm"] = bm
    bzm = z_back(inner3, q, ez)
    pair["bzm"] = bzm
    ll = np.concatenate(three(jm.T @ k3, jm.T @ w3, 2), 0)
    pair["lb"] = np.concatenate([ll @ ((wt3[:, 0] + extra)[:, None] * bm) for extra in (0, wt3[:, 1], wt3[:, 2])], 0)
    pair["rb"] = bzm @ np.concatenate([corner_columns(w3 @ jm, ez), corner_columns(k3 @ jm, ez)], 1)
    pair["jl"] = np.kron(blocks(jm.T, 2), blocks(jm.T, 2))
    pair["rj"] = corner_columns(jm, ez)
    place = {direction: at for at, direction in enumerate(order)}

    def ring_row(ex, ey, d):
        dx, dy = ex // 2 - 1, ey // 2 - 1
        return place[(dx, dy)] * 16 + d * 4 + (ex % 2) * 2 + ey % 2

    ld3, le3 = np.zeros((576, 144)), np.zeros((576, 144))
    for x in range(24):
        for y in range(24):
            ex, ey = x // m3 + 1, y // m3 + 1
            ld3[x * 24 + y, ring_row(ex, ey, 0)] = l3[x % m3]
            ld3[x * 24 + y, ring_row(ex, ey, 1)] = l3[y % m3]
            le3[x * 24 + y, ring_row(ex, ey, 2)] = 1
    pair["ld3"] = ld3
    plain["le3"] = (le3, BF)
    plain["s48"] = (spread(m3), BF)
    pair["sl48"] = spread(m3) * np.tile(l3, ez)[None]
    er = np.zeros((3, 9, 2 * q, 2 * q, 144))
    for at in range(9):
        for x in range(2 * q):
            for y in range(2 * q):
                for d in range(3):
                    er[d, at, x, y, at * 16 + d * 4 + (x // q) * 2 + y // q] = 1
    plain["er"] = (er.reshape(3 * 576, 144), BF)
    pair["k3"] = np.concatenate(three(k3, w3, 2), 0)
    pair["rk3"] = side_by_side(blocks(w3, ez), blocks(k3, ez))
    vertex_line = lambda table: np.array(
        [[table[at % q, v - at // q] if 0 <= v - at // q <= 1 else 0.0 for v in range(8)] for at in range(6 * q)]
    )
    stiff1, mass1, plain1 = vertex_line(k3 @ jm), vertex_line(w3 @ jm), vertex_line(jm)

    def vertex_columns(left, right, dx, dy):
        table = np.zeros((64, 4, 4, 8))
        for iy in range(4):
            for ix, ahead in enumerate(AHEAD):
                for x in range(2):
                    for y in range(2):
                        table[:, iy, ix, x * 2 + y] = np.kron(
                            left[span(dx), (ahead + 1) * 2 + x], right[span(dy), iy * 2 + y]
                        )
        return table.reshape(64, 128)

    pair["lc"] = np.concatenate(
        [
            vertex_columns(left, right, dx, dy)
            for left, right in ((stiff1, mass1), (mass1, stiff1), (mass1, mass1))
            for dx, dy in order
        ],
        0,
    )
    pair["jc"] = vertex_columns(plain1, plain1, 0, 0)

    def z_vertices(table):
        result = np.zeros((ez, ez * q))
        for element in range(ez):
            for at in range(q):
                result[element, element * q + at] += table[at, 0]
                result[(element + 1) % ez, element * q + at] += table[at, 1]
        return np.tile(result, (4, 1))

    pair["rc"] = side_by_side(z_vertices(w3 @ jm), z_vertices(k3 @ jm))
    pair["rcj"] = z_vertices(jm)
    mask, left = np.zeros((n_gy, 16, 128)), np.zeros((n_gy, 16, 16))
    for gy in range(n_gy):
        for row in range(16):
            vx, vy = row // 8 + row // 4 % 2, row // 2 % 2 + row % 2
            owner = gy + vy // 2
            if owner < n_gy:
                first = owner * 32 + (vx % 2) * 16 + (vy % 2) * 8
                mask[gy, row, first % 128 : first % 128 + 8] = 1
                left[gy, first // 128 + 4 * (vx // 2), row] = 1
    plain["mask"] = (mask.reshape(-1, 128), F32)
    plain["left"] = (left.reshape(-1, 16), BF)
    chosen = np.zeros((8, 32))
    select = np.zeros((32, 8))
    for lane in range(32):
        chosen[lane // 8, lane] = 1
        select[lane, lane % 8] = 1
    plain["chosen"] = (chosen, F32)
    plain["select"] = (select, BF)
    tables = {}
    for name, table in pair.items():
        table = fitted(np.asarray(table, np.float64), name in RIGHT)
        high = table.astype(ml_dtypes.bfloat16)
        rest = (table - high.astype(np.float64)).astype(ml_dtypes.bfloat16)
        if name in RIGHT:
            tables[name] = np.block([[high, rest], [high, np.zeros_like(rest)]])[None]
        else:
            tables[name] = np.stack([high, rest])
    for name, (table, kind) in plain.items():
        table = fitted(np.asarray(table), name in RIGHT)
        table = np.concatenate([table, table], 0) if name in RIGHT else table
        tables[name] = table.astype(ml_dtypes.bfloat16 if kind is BF else np.float32)[None]
    return tables


STAGES = (
    (
        "columns", "wo", "jxy", "jz", "s80", "sl80", "ld7", "le7", "e7", "e3", "e1", "s64", "s32", "s256",
        "wz7", "chosen", "mask",
    ),
    ("wh", "az", "bf", "bo", "la", "bzra", "ld3", "le3", "s48", "sl48", "er", "lar"),
    (
        "wmo", "jl", "rj", "scat", "bz", "k7", "kz7", "wmn", "azm", "lb", "rb", "left", "bm", "bzm", "select",
        "rk3", "k3", "lc", "rc", "jc", "rcj", "rp", "lp", "pxy", "pz",
    ),
)


def pack(tables):
    stacks, places = {}, {}
    for stage, names in enumerate(STAGES):
        for name in names:
            table = tables[name]
            key = (stage, table.dtype.name, table.shape[-1])
            parts = stacks.setdefault(key, [])
            at = sum(part.shape[0] for part in parts)
            height = -(-table.shape[1] // 16) * 16
            for part in table:
                parts.append(np.pad(part, ((0, height - part.shape[0]), (0, 0))))
            places[name] = (key, at, height, table.shape[1])
    keys = tuple(stacks)
    return keys, [np.concatenate(stacks[key], 0) for key in keys], places


class Table:
    def __init__(self, ref, place):
        _, self.at, self.height, self.rows = place
        self.ref = ref
        self.shape = (2, self.rows, ref.shape[-1])

    def __getitem__(self, part):
        part = 0 if part is Ellipsis else part
        return self.ref[self.at + part * self.height : self.at + part * self.height + self.rows, :]

    def piece(self, part, start, rows):
        return self.ref[pl.ds(self.at + part * self.height + start, rows), :]


def dot(a, b):
    return jnp.dot(a, b, preferred_element_type=F32)


def split(x):
    high = x.astype(BF)
    return high, (x - high.astype(F32)).astype(BF)


def wide(x, lanes=128):
    if x.shape[1] == lanes:
        return x
    return jnp.concatenate([x, jnp.zeros((x.shape[0], lanes - x.shape[1]), x.dtype)], 1)


def tall(x, rows):
    if x.shape[0] == rows:
        return x
    return jnp.concatenate([x, jnp.zeros((rows - x.shape[0], x.shape[1]), x.dtype)], 0)


def halves(x):
    middle = x.shape[1] // 2
    return x[:, :middle] + x[:, middle:]


def exactly(main, small, x):
    high, rest = split(x)
    return halves(dot(main, jnp.concatenate([high, rest], 1))) + dot(small, high)


def left3(table, x):
    return exactly(table[0], table[1], tall(x, table.shape[-1]))


def left2(table, x):
    return halves(dot(table[...], jnp.concatenate(split(tall(x, table.shape[-1])), 1)))


def terms3(table, x):
    x = tall(x, table.shape[-1])
    rows = table.shape[1] // 3
    first = exactly(table.piece(0, 0, 2 * rows), table.piece(1, 0, 2 * rows), x[:, 0:128])
    third = exactly(table.piece(0, 2 * rows, rows), table.piece(1, 2 * rows, rows), x[:, 128:256])
    return first[0:rows], first[rows:], third


def right3(x, table):
    return halves(right2(x, table))


def right2(x, table):
    return dot(jnp.concatenate(split(wide(x)), 1), table[...])


KEPT = {
    "fine_f": (768, 128), "mid_f": (192, 128), "low_f": (48, 256), "ring_f": (1728, 128), "inverse7": (400, 128),
    "inverse3": (576, 128), "wt7": (256, 128), "wr7": (96, 128), "wt3": (64, 128), "base_mid": (64, 128),
    "base_low": (16, 256), "local": (256, 128), "first_fine": (256, 128), "base_fine": (256, 128),
    "first_mid": (64, 128), "modal": (400, 128), "modal3": (576, 128), "own_part": (192, 128), "base_ring": (576, 128),
    "ww7": (256, 128),
}


def cycle_kernel(keys, places, n_gx, n_gy, *refs):
    r_hbm, len_hbm, inv_hbm = refs[:3]
    count = len(keys)
    packed = refs[3 : 3 + count]
    out_fine, out_mid, out_low = refs[3 + count : 6 + count]
    stores = refs[6 + count : 6 + 2 * count]
    (
        r_ref, len_ref, inv_ref, rs, fs, hb1, fb1, rm, fm, rp, fp, hb2, fb2, hs1, hs2, st1, st2, held, gs, gb, cb,
        send_sem, recv_sem, gsend, grecv, csend, crecv, in_sem, table_sem,
    ) = refs[6 + 2 * count : -len(KEPT)]
    gx, gy = lax.axis_index("gx"), lax.axis_index("gy")
    last = n_gy - 1
    barrier = pltpu.get_barrier_semaphore()

    def greet(ahead, row):
        pl.semaphore_signal(
            barrier, inc=1, device_id=(lax.rem(gx + (ahead + n_gx), n_gx), row), device_id_type=MESH
        )

    def greet_if(row):
        @pl.when((row >= 0) & (row <= last))
        def _():
            greet(1, row)
            greet(2, row)

    for step in range(-1, 3):
        greet_if(gy + step)
    for step in range(1, n_gy):
        greet(0, lax.rem(gy + step, n_gy))
    for step in range(n_gy):
        greet(-1, lax.rem(gy + step, n_gy))
    inputs = [
        pltpu.make_async_copy(source, target, in_sem.at[at])
        for at, (source, target) in enumerate(((len_hbm, len_ref), (r_hbm, r_ref), (inv_hbm, inv_ref)))
    ]
    loads = [pltpu.make_async_copy(packed[at], stores[at], table_sem.at[at]) for at in range(count)]
    for load in inputs + loads:
        load.start()

    def ready(stage):
        for key, load in zip(keys, loads):
            if key[0] == stage:
                load.wait()

    kept = dict(zip(KEPT, refs[-len(KEPT) :]))

    def keep(name, value):
        kept[name][...] = value
        return kept[name]

    t = {name: Table(stores[keys.index(place[0])], place) for name, place in places.items()}
    at_bottom, at_top = gy == 0, gy == last
    not_bottom, not_top = gy > 0, gy < last
    sent = {0: None, 1: not_bottom, 2: not_top}

    def guarded(condition, action):
        if condition is None:
            action()
        else:
            pl.when(condition)(action)

    def exchange(phase, source, buffer, rows):
        at = offsets(rows)

        def group(number):
            def action():
                for index in range(*GROUPS[number]):
                    tx, ty = RING[index]
                    slot = RING.index((-tx, -ty))
                    landing = (0, 2, 1)[number]
                    pltpu.make_async_remote_copy(
                        src_ref=source(index),
                        dst_ref=buffer.at[pl.ds(at[slot], rows[slot])],
                        send_sem=send_sem.at[phase, number],
                        recv_sem=recv_sem.at[phase, landing],
                        device_id=(lax.rem(gx + (tx + n_gx), n_gx), gy + ty),
                        device_id_type=MESH,
                    ).start()

            return action

        for number in (1, 2, 0):
            guarded(sent[number], group(number))

    def settle(phase, sems, buffer, rows):
        at = offsets(rows)
        for number in range(3):
            first, end = GROUPS[number]
            piece = buffer.at[pl.ds(at[first], at[end] - at[first])]
            guarded(sent[number], lambda: pltpu.make_async_copy(piece, piece, sems.at[phase, number]).wait())

    def clear(number):
        first, end = GROUPS[number]
        for buffer, rows in (
            (fs, BLOCK_ROWS), (hb1, FACE_ROWS), (fb1, FACE_ROWS), (rp, BLOCK_ROWS),
            (fp, BLOCK_ROWS), (hb2, FACE_ROWS), (fb2, FACE_ROWS),
        ):
            at = offsets(rows)
            buffer[at[first] : at[end], :] = jnp.zeros((at[end] - at[first], buffer.shape[1]), F32)

    @pl.when(at_bottom)
    def _():
        clear(1)
        cb[0:32, :] = jnp.zeros((32, 128), F32)

    @pl.when(at_top)
    def _():
        clear(2)
        cb[64:96, :] = jnp.zeros((32, 128), F32)

    @pl.when(gy >= last - 1)
    def _():
        cb[96:128, :] = jnp.zeros((32, 128), F32)

    def halo(field, stage):
        at = offsets(FACE_ROWS)
        for index, (tx, ty) in enumerate(RING):
            xs, ys = (14, 0)[tx < 0], (14, 0)[ty < 0]
            if ty == 0:
                layers = field[xs, :, :], field[xs + 1, :, :]
            elif tx == 0:
                layers = field[:, ys, :], field[:, ys + 1, :]
            else:
                layers = field[xs : xs + 2, ys, :], field[xs : xs + 2, ys + 1, :]
            stage[at[index] : at[index + 1], :] = tall(jnp.concatenate(layers, 1), at[index + 1] - at[index])

    def unfold(buffer):
        packed_rows = tall(buffer[...], 128)
        return jnp.concatenate([packed_rows, pltpu.roll(packed_rows, 64, 1)], 0)

    def fold(block):
        result = block[0:16]
        for part in range(1, 4):
            result = result + pltpu.roll(block[part * 16 : part * 16 + 16], part * 32, 1)
        return result

    def spread_blocks(folded, blocks_ref):
        for part in range(4):
            turned_back = pltpu.roll(folded[0:128, :], (128 - part * 32) % 128, 1) if part else folded[0:128, :]
            for slot in range(8):
                blocks_ref[slot * 64 + part * 16 : slot * 64 + part * 16 + 16, :] = turned_back[
                    slot * 16 : slot * 16 + 16
                ]

    at_face = offsets(FACE_ROWS)

    inputs[0].wait()
    own_f = 8 * 16
    for ex in range(2):
        a, b, c = len_ref[0, ex], len_ref[1, ex], len_ref[2, ex]
        fs[own_f + ex * 2 : own_f + ex * 2 + 2, :] = wide(b * c / (2.0 * a))
        fs[own_f + 4 + ex * 2 : own_f + 6 + ex * 2, :] = wide(a * c / (2.0 * b))
        fs[own_f + 8 + ex * 2 : own_f + 10 + ex * 2, :] = wide(a * b / (2.0 * c))
    fs[own_f + 12 : own_f + 16, :] = jnp.zeros((4, 128), F32)
    inputs[1].wait()
    halo(r_ref, hs1)
    near = jnp.minimum(gy + 1, last) - jnp.maximum(gy - 2, 0) + 1
    pl.semaphore_wait(barrier, 2 * n_gy - 1 + 2 * near)
    exchange(1, lambda index: hs1.at[pl.ds(at_face[index], FACE_ROWS[index])], hb1, FACE_ROWS)
    exchange(0, lambda index: fs.at[pl.ds(own_f, 16)], fs, BLOCK_ROWS)

    bottom_on = jnp.where(at_bottom, 1.0, 0.0)
    top_on = jnp.where(at_top, 1.0, 0.0)

    ready(0)
    columns = t["columns"][...]

    def wall_weight(rows, at):
        piece = columns[0:rows]
        return piece[:, at : at + 1] + bottom_on * piece[:, at + 1 : at + 2] + top_on * piece[:, at + 2 : at + 3]

    wt7 = keep("wt7", jnp.broadcast_to(wall_weight(256, 0), (256, 128)))
    wr7 = keep("wr7", jnp.broadcast_to(wall_weight(96, 3), (96, 128)))
    wt3 = keep("wt3", jnp.broadcast_to(wall_weight(64, 6), (64, 128)))
    ww7 = keep("ww7", jnp.broadcast_to(columns[:, 9:10], (256, 128)))
    r = wide(r_ref[...].reshape(256, 64))
    f_own = wide(fs[own_f : own_f + 16, :])
    d7 = left3(t["ld7"], right2(f_own, t["s80"])) + left2(t["le7"], right3(f_own, t["sl80"]))
    inverse7 = keep("inverse7", jnp.where(d7 > 0.0, 1.0 / jnp.where(d7 > 0.0, d7, 1.0), 0.0))
    modal = keep("modal", left3(t["wo"], r))
    base_mid = keep("base_mid", right3(left3(t["jxy"], r), t["jz"]))
    fine_f = keep("fine_f", left2(t["e7"], right2(f_own, t["s64"])))
    mid_f = keep("mid_f", left2(t["e3"], right2(f_own, t["s32"])))
    low_f = keep("low_f", left2(t["e1"], right2(f_own, t["s256"])))

    def fine_back(modal, buffer, stage, phase):
        modal = right3(modal, t["az"]) * inverse7[...]
        stage[...] = left3(t["bf"], modal)
        exchange(phase, lambda index: stage.at[pl.ds(at_face[index], FACE_ROWS[index])], buffer, FACE_ROWS)
        return left3(t["bo"], modal)

    ready(1)
    settle(1, recv_sem, hb1, FACE_ROWS)
    modal = modal[...] + left3(t["wh"], unfold(hb1))
    local = keep("local", fine_back(modal, fb1, st1, 2) * wt7[...])
    own_part = keep("own_part", jnp.concatenate(terms3(t["la"], right3(local[...], t["bzra"])), 0))
    settle(0, recv_sem, fs, BLOCK_ROWS)
    ring_f = wide(fs[...])
    d3 = left3(t["ld3"], right2(ring_f, t["s48"])) + left2(t["le3"], right3(ring_f, t["sl48"]))
    inverse3 = keep("inverse3", jnp.where(d3 > 0.0, 1.0 / jnp.where(d3 > 0.0, d3, 1.0), 0.0))
    ring_f = keep("ring_f", left2(t["er"], right2(ring_f, t["s32"])))

    settle(2, recv_sem, fb1, FACE_ROWS)
    faces = wide(fb1[...]) * wr7[...]
    face_part = terms3(t["lar"], right3(faces, t["bzra"]))
    residual_mid = base_mid[...] - (
        mid_f[0:64] * (own_part[0:64] + face_part[0])
        + mid_f[64:128] * (own_part[64:128] + face_part[1])
        + mid_f[128:192] * (own_part[128:192] + face_part[2])
    )
    rp[128:144, :] = fold(residual_mid)
    exchange(3, lambda index: rp.at[pl.ds(128, 16)], rp, BLOCK_ROWS)
    rm[512:576, :] = residual_mid

    ready(2)
    own_modal = keep("modal3", left3(t["wmo"], residual_mid))
    base_low = keep("base_low", right3(left3(t["jl"], residual_mid), t["rj"]))
    first_fine = keep("first_fine", right3(local[...] + left2(t["scat"], faces), t["bz"]))
    massed = left3(t["k7"], first_fine[...] * t["wz7"][...][0:1])
    along_z = right3(first_fine[...], t["kz7"]) * ww7[...]
    base_fine = keep(
        "base_fine",
        wide(r_ref[...].reshape(256, 64))
        - (fine_f[0:256] * massed[0:256] + fine_f[256:512] * massed[256:512] + fine_f[512:768] * along_z),
    )

    settle(3, recv_sem, rp, BLOCK_ROWS)
    spread_blocks(rp, rm)
    modal3 = own_modal[...] + left3(t["wmn"], rm[0:512, :])
    modal3 = right3(modal3, t["azm"]) * inverse3[...]
    variant = jnp.where(at_bottom, 1, jnp.where(at_top, 2, 0))
    rows = pl.multiple_of(variant * 48, 16)
    low = exactly(t["lb"].piece(0, rows, 48), t["lb"].piece(1, rows, 48), tall(modal3, t["lb"].shape[-1]))
    low = right3(low, t["rb"])
    low = base_low[...] - (
        low_f[0:16] * low[0:16, 0:256] + low_f[16:32] * low[16:32, 0:256] + low_f[32:48] * low[32:48, 256:512]
    )
    wall = pl.multiple_of(gy * 16, 16)
    low = tall(halves(low) * t["mask"].piece(0, wall, 16), 128)
    message = halves(dot(t["left"].piece(0, wall, 16), jnp.concatenate(split(low), 1)))[0:8]
    gs[...] = message

    def send_slab(step, ahead):
        slot = step + jnp.where(ahead == 0, -1, n_gy - 1)
        pltpu.make_async_remote_copy(
            src_ref=gs,
            dst_ref=gb.at[slot],
            send_sem=gsend,
            recv_sem=grecv,
            device_id=(lax.rem(gx + ahead, n_gx), lax.rem(gy + step, n_gy)),
            device_id_type=MESH,
        ).start()

    for step in range(1, n_gy):
        send_slab(step, 0)
    for step in range(n_gy):
        send_slab(step, 1)

    first_mid = keep("first_mid", right3(left3(t["bm"], modal3) * wt3[...], t["bzm"]))
    fm[512:576, :] = first_mid[...]
    fp[128:144, :] = fold(first_mid[...])
    exchange(4, lambda index: fp.at[pl.ds(128, 16)], fp, BLOCK_ROWS)

    pltpu.make_async_copy(gb, gb, grecv).wait()
    here = gs[...] + jnp.sum(gb[0 : n_gy - 1], axis=0)
    behind = jnp.sum(gb[n_gy - 1 :], axis=0)
    inputs[2].wait()
    chunks = inv_ref.shape[2] // 128
    vector = here + pltpu.roll(behind, 4, 0)
    row = lax.broadcasted_iota(jnp.int32, (8, 128), 0)
    vector = jnp.concatenate([jnp.where(row == chunk, vector, 0.0) for chunk in range(chunks)], 1)
    vector = tall(vector, 16).astype(BF)
    inverse = tall(inv_ref[0], 128)
    solved = lax.dot_general(vector, inverse, (((1,), (1,)), ((), ())), preferred_element_type=F32)
    solved = jnp.sum(solved, axis=0, keepdims=True)
    solved = jnp.broadcast_to(solved, (8, 128)) * t["chosen"][...]
    own_c = (4 + 3) * 8
    cb[own_c : own_c + 8, :] = solved

    def send_correction(iy):
        def action():
            for ix, ahead in enumerate(AHEAD):
                if (ahead, iy - 1) != (0, 0):
                    pltpu.make_async_remote_copy(
                        src_ref=cb.at[pl.ds(own_c, 8)],
                        dst_ref=cb.at[pl.ds((iy * 4 + ix) * 8, 8)],
                        send_sem=csend.at[iy],
                        recv_sem=crecv.at[iy],
                        device_id=(lax.rem(gx - ahead + n_gx, n_gx), gy - (iy - 1)),
                        device_id_type=MESH,
                    ).start()

        return action

    to_group = (not_top, None, not_bottom, gy > 1)
    from_group = (not_bottom, None, not_top, gy < last - 1)
    for iy in range(4):
        guarded(to_group[iy], send_correction(iy))

    def settle_corrections(sems, conditions):
        for iy in range(4):
            piece = cb.at[pl.ds(iy * 32, 24 if iy == 1 else 32)]
            guarded(conditions[iy], lambda: pltpu.make_async_copy(piece, piece, sems.at[iy]).wait())

    low_out = right2(tall(solved, 16), t["select"])
    out_low[0] = low_out[0:2, 0:8]
    out_low[1] = low_out[2:4, 0:8]
    settle(4, recv_sem, fp, BLOCK_ROWS)
    spread_blocks(fp, fm)
    turned = right3(fm[...], t["rk3"])
    parts = []
    for at in range(9):
        piece = terms3(t["k3"], turned[at * 64 : (at + 1) * 64])
        parts.append(
            rm[at * 64 : (at + 1) * 64, :]
            - (
                ring_f[at * 64 : (at + 1) * 64] * piece[0]
                + ring_f[576 + at * 64 : 576 + (at + 1) * 64] * piece[1]
                + ring_f[1152 + at * 64 : 1152 + (at + 1) * 64] * piece[2]
            )
        )
    base_ring = keep("base_ring", jnp.concatenate(parts, 0))
    modal3 = keep("modal3", left3(t["wmn"], base_ring[0:512]) + left3(t["wmo"], base_ring[512:576]))

    settle_corrections(crecv, from_group)
    corrections = wide(cb[...])
    change = terms3(t["lc"], right3(corrections, t["rc"]))
    change = (
        ring_f[0:576] * change[0]
        + ring_f[576:1152] * change[1]
        + ring_f[1152:1728] * change[2]
    )
    modal3 = modal3[...] - left3(t["wmn"], change[0:512]) - left3(t["wmo"], change[512:576])
    modal3 = right3(modal3, t["azm"]) * inverse3[...]
    held[0:64, :] = first_mid[...] + right3(left3(t["jc"], corrections), t["rcj"])
    mid_result = held[0:64, :] + right3(left3(t["bm"], modal3) * wt3[...], t["bzm"])

    turned = right3(mid_result, t["rp"])
    turned = terms3(t["lp"], turned)
    residual = base_fine[...] - (
        fine_f[0:256] * turned[0]
        + fine_f[256:512] * turned[1]
        + fine_f[512:768] * turned[2]
    )
    rs[...] = residual[:, 0:64].reshape(16, 16, 64)
    halo(rs, hs2)
    exchange(5, lambda index: hs2.at[pl.ds(at_face[index], FACE_ROWS[index])], hb2, FACE_ROWS)
    out_mid[...] = mid_result[:, 0:32].reshape(8, 8, 32)
    modal = keep("modal", left3(t["wo"], residual))
    held[...] = first_fine[...] + right3(left3(t["pxy"], mid_result), t["pz"])
    settle(5, recv_sem, hb2, FACE_ROWS)
    modal = modal[...] + left3(t["wh"], unfold(hb2))
    local = fine_back(modal, fb2, st2, 6) * wt7[...]
    held[...] = held[...] + right3(local, t["bz"])
    settle(6, recv_sem, fb2, FACE_ROWS)
    result = held[...] + left2(t["scat"], right3(wide(fb2[...]) * wr7[...], t["bz"]))
    out_fine[...] = result[:, 0:64].reshape(16, 16, 64)

    for phase, buffer, rows in (
        (0, fs, BLOCK_ROWS), (1, hb1, FACE_ROWS), (2, fb1, FACE_ROWS), (3, rp, BLOCK_ROWS),
        (4, fp, BLOCK_ROWS), (5, hb2, FACE_ROWS), (6, fb2, FACE_ROWS),
    ):
        settle(phase, send_sem, buffer, rows)
    pltpu.make_async_copy(gb, gb, gsend).wait()
    settle_corrections(csend, to_group)


def hand_over(*refs):
    copies = [pltpu.make_async_copy(refs[at], refs[3 + at], refs[6].at[at]) for at in range(3)]
    for copy in copies:
        copy.start()
    for copy in copies:
        copy.wait()


def shards(n_gx, n_gy, local_residual, lengths, coarse_inverse):
    keys, packed, places = pack(build_tables(n_gy, lengths.shape[3]))
    vmem = pl.BlockSpec(memory_space=pltpu.VMEM)
    scratch = [pltpu.VMEM(table.shape, BF if key[1] == "bfloat16" else F32) for key, table in zip(keys, packed)]
    scratch += [
        pltpu.VMEM(local_residual.shape, F32),
        pltpu.VMEM(lengths.shape, F32),
        pltpu.VMEM(coarse_inverse.shape, BF),
        pltpu.VMEM((16, 16, 64), F32),
        pltpu.VMEM((144, 128), F32),
        pltpu.VMEM((96, 128), F32),
        pltpu.VMEM((96, 128), F32),
        pltpu.VMEM((576, 128), F32),
        pltpu.VMEM((576, 128), F32),
        pltpu.VMEM((144, 128), F32),
        pltpu.VMEM((144, 128), F32),
        pltpu.VMEM((96, 128), F32),
        pltpu.VMEM((96, 128), F32),
        pltpu.VMEM((96, 128), F32),
        pltpu.VMEM((96, 128), F32),
        pltpu.VMEM((96, 128), F32),
        pltpu.VMEM((96, 128), F32),
        pltpu.VMEM((256, 128), F32),
        pltpu.VMEM((8, 128), F32),
        pltpu.VMEM((2 * n_gy - 1, 8, 128), F32),
        pltpu.VMEM((128, 128), F32),
        pltpu.SemaphoreType.DMA((7, 3)),
        pltpu.SemaphoreType.DMA((7, 3)),
        pltpu.SemaphoreType.DMA,
        pltpu.SemaphoreType.DMA,
        pltpu.SemaphoreType.DMA((4,)),
        pltpu.SemaphoreType.DMA((4,)),
        pltpu.SemaphoreType.DMA((3,)),
        pltpu.SemaphoreType.DMA((len(keys),)),
    ]
    scratch += [pltpu.VMEM(shape, F32) for shape in KEPT.values()]
    outs = pl.pallas_call(
        functools.partial(cycle_kernel, keys, places, n_gx, n_gy),
        out_shape=(
            jax.ShapeDtypeStruct((16, 16, 64), F32),
            jax.ShapeDtypeStruct((8, 8, 32), F32),
            jax.ShapeDtypeStruct((2, 2, 8), F32),
        ),
        in_specs=[pl.BlockSpec(memory_space=pl.ANY)] * (3 + len(keys)),
        out_specs=(vmem, vmem, vmem),
        scratch_shapes=scratch,
        compiler_params=pltpu.CompilerParams(collective_id=0, has_side_effects=True, vmem_limit_bytes=60 * 1024 * 1024),
    )(local_residual, lengths, coarse_inverse, *[jnp.asarray(table) for table in packed])
    return pl.pallas_call(
        hand_over,
        out_shape=tuple(jax.ShapeDtypeStruct(out.shape, out.dtype) for out in outs),
        in_specs=[vmem] * 3,
        out_specs=[pl.BlockSpec(memory_space=pl.ANY)] * 3,
        scratch_shapes=[pltpu.SemaphoreType.DMA((3,))],
    )(*outs)


def solution(mesh):
    in_specs = (P("gx", "gy", None), P(None, "gx", "gy", None), P("gx", "gy", None))
    out_specs = (P("gx", "gy", None), P("gx", "gy", None), P("gx", "gy", None))
    return jax.shard_map(
        functools.partial(shards, mesh.shape["gx"], mesh.shape["gy"]),
        mesh=mesh,
        in_specs=in_specs,
        out_specs=out_specs,
        check_vma=False,
    )
```

```python
import functools
import math

import jax
import jax.numpy as jnp
import ml_dtypes
import numpy as np
from jax import lax
from jax.experimental import pallas as pl
from jax.experimental.pallas import tpu as pltpu
from jax.sharding import PartitionSpec as P

ORDER = 7
MID_ORDER = 3


def legendre_pair(order, point):
    older = 1.0
    newer = point
    for degree in range(2, order + 1):
        nexter = ((2 * degree - 1) * point * newer - (degree - 1) * older) / degree
        older = newer
        newer = nexter
    return (newer, older)


def jacobi_eigen(matrix):
    count_n = len(matrix)
    work = [list(row_items) for row_items in matrix]
    vectors = [
        [1.0 if row_at == col_at else 0.0 for col_at in range(count_n)] for row_at in range(count_n)
    ]
    for sweep_count in range(60):
        for lower_at in range(count_n):
            for upper_at in range(lower_at + 1, count_n):
                off_value = work[lower_at][upper_at]
                if abs(off_value) < 1e-18 * (
                    abs(work[lower_at][lower_at]) + abs(work[upper_at][upper_at])
                ):
                    continue
                angle_ratio = (work[upper_at][upper_at] - work[lower_at][lower_at]) / (
                    2.0 * off_value
                )
                sign_value = 1.0 if angle_ratio >= 0 else -1.0
                tangent = sign_value / (
                    abs(angle_ratio) + math.sqrt(angle_ratio * angle_ratio + 1.0)
                )
                cosine = 1.0 / math.sqrt(tangent * tangent + 1.0)
                sine_value = tangent * cosine
                for other_at in range(count_n):
                    left_value = work[other_at][lower_at]
                    right_value = work[other_at][upper_at]
                    work[other_at][lower_at] = cosine * left_value - sine_value * right_value
                    work[other_at][upper_at] = sine_value * left_value + cosine * right_value
                for other_at in range(count_n):
                    left_value = work[lower_at][other_at]
                    right_value = work[upper_at][other_at]
                    work[lower_at][other_at] = cosine * left_value - sine_value * right_value
                    work[upper_at][other_at] = sine_value * left_value + cosine * right_value
                for other_at in range(count_n):
                    left_value = vectors[other_at][lower_at]
                    right_value = vectors[other_at][upper_at]
                    vectors[other_at][lower_at] = cosine * left_value - sine_value * right_value
                    vectors[other_at][upper_at] = sine_value * left_value + cosine * right_value
    eigen_list = [work[row_at][row_at] for row_at in range(count_n)]
    ordering = sorted(range(count_n), key=lambda index_at: eigen_list[index_at])
    rates = [eigen_list[index_at] for index_at in ordering]
    basis = [[vectors[row_at][index_at] for index_at in ordering] for row_at in range(count_n)]
    return (rates, basis)


def gll_tables(order):
    point_count = order + 1
    node_list = []
    for node_at in range(point_count):
        point = math.cos(math.pi * node_at / order)
        for newton_step in range(100):
            top_value, lower_value = legendre_pair(order, point)
            point = point - (point * top_value - lower_value) / ((order + 1) * top_value)
        node_list.append(point)
    node_list = node_list[::-1]
    node_list[0] = -1.0
    node_list[-1] = 1.0
    values = [legendre_pair(order, point)[0] for point in node_list]
    weight_list = [2.0 / (order * (order + 1) * value_at**2) for value_at in values]
    derivative = [[0.0] * point_count for row_at in range(point_count)]
    for row_at in range(point_count):
        for col_at in range(point_count):
            if row_at != col_at:
                derivative[row_at][col_at] = values[row_at] / (
                    values[col_at] * (node_list[row_at] - node_list[col_at])
                )
    derivative[0][0] = -order * (order + 1) / 4.0
    derivative[order][order] = order * (order + 1) / 4.0
    stiff_list = [
        [
            sum(
                (
                    derivative[inner_at][row_at]
                    * weight_list[inner_at]
                    * derivative[inner_at][col_at]
                    for inner_at in range(point_count)
                )
            )
            for col_at in range(point_count)
        ]
        for row_at in range(point_count)
    ]
    extent = 3 * order + 1
    big_stiff = [[0.0] * extent for row_at in range(extent)]
    big_mass = [0.0] * extent
    for offset_at in (0, order, 2 * order):
        for row_at in range(point_count):
            big_mass[offset_at + row_at] += weight_list[row_at]
            for col_at in range(point_count):
                big_stiff[offset_at + row_at][offset_at + col_at] += stiff_list[row_at][col_at]
    chosen = list(range(order - 1, 2 * order + 2))
    root_mass = [1.0 / math.sqrt(big_mass[index_at]) for index_at in chosen]
    scaled = [
        [
            root_mass[row_at] * big_stiff[chosen[row_at]][chosen[col_at]] * root_mass[col_at]
            for col_at in range(len(chosen))
        ]
        for row_at in range(len(chosen))
    ]
    rates, basis = jacobi_eigen(scaled)
    eigen_basis = [
        [root_mass[row_at] * basis[row_at][col_at] for col_at in range(len(chosen))]
        for row_at in range(len(chosen))
    ]
    return (
        np.array(node_list),
        np.array(weight_list),
        np.array(stiff_list),
        np.array(eigen_basis),
        np.array(rates),
    )


def interp_table(fine_nodes, coarse_nodes):
    coarse_count = len(coarse_nodes)
    columns = []
    for column in range(coarse_count):
        factors_list = [
            (fine_nodes - coarse_nodes[other_node])
            / (coarse_nodes[column] - coarse_nodes[other_node])
            for other_node in range(coarse_count)
            if other_node != column
        ]
        columns.append(np.prod(np.stack(factors_list), axis=0))
    return np.stack(columns, axis=1)

BF = jnp.bfloat16
F32 = jnp.float32
RING = ((-1, 0), (1, 0), (0, -1), (-1, -1), (1, -1), (0, 1), (-1, 1), (1, 1))
GROUPS = ((0, 2), (2, 5), (5, 8))
AHEAD = (-1, 1, 2, 0)
FACE_ROWS = (16, 16, 16, 8, 8, 16, 8, 8)
BLOCK_ROWS = (16,) * 8
WIDE_ROWS = (80, 80, 80, 64, 64, 80, 64, 64)
LOW_SIDE = ((-1, 0), (-1, -1), (-1, 1), (0, -1), (0, 1))
HIGH_SIDE = ((1, 0), (1, -1), (1, 1), (0, -1), (0, 1))
MESH = pl.DeviceIdType.MESH


def offsets(rows):
    return tuple(int(at) for at in np.concatenate([[0], np.cumsum(rows)]))


def blocks(matrix, count):
    return np.kron(np.eye(count), matrix)


def line_extension(points, elements, periodic):
    size = elements * points
    width = size if periodic else size + 4
    table = np.zeros((elements, points + 2, width))

    def column(at):
        if periodic:
            return at % size
        if at < 0:
            return {-2: size, -1: size + 1}[at]
        if at >= size:
            return {size: size + 2, size + 1: size + 3}[at]
        return at

    for element in range(elements):
        start = element * points
        table[element, 0, column(start - 2)] += 1
        for at in range(points):
            table[element, 1 + at, start + at] += 1
        table[element, 1, column(start - 1)] += 1
        table[element, points, column(start + points)] += 1
        table[element, points + 1, column(start + points + 1)] += 1
    return table.reshape(elements * (points + 2), width)


def line_weights(points, elements):
    position = np.arange(points * elements) % points
    return np.where((position == 0) | (position == points - 1), 0.5, 1.0)


def z_back(inner, points, elements):
    table = blocks(inner, elements)
    total = np.array(table)
    size = points * elements
    for element in range(elements):
        low, high = element * points, (element * points - 1) % size
        total[low] = table[low] + table[high]
        total[high] = total[low]
    return (total * line_weights(points, elements)[:, None]).T


RIGHT = (
    "az", "bz", "bzra", "jz", "kz7", "rp", "pz", "azm", "bzm", "rb", "rj", "rk3", "ra3", "cz", "s16", "rcj",
    "s64", "s32", "s256", "s80", "sl80", "s48", "sl48", "select",
)


def fitted(table, right):
    rows, columns = table.shape[-2:]
    more = ((0, -rows % 128 if right else 0), (0, -columns % 128))
    return np.pad(table, ((0, 0),) * (table.ndim - 2) + more)


def side_by_side(*parts):
    return np.concatenate([np.pad(part, ((0, 0), (0, -part.shape[1] % 128))) for part in parts], 1)


def corner_columns(inner_table, elements):
    points = inner_table.shape[0]
    table = np.zeros((elements * points, 256))
    for corner in range(2):
        for lane in range(128):
            element = (lane % elements - corner) % elements
            table[element * points : (element + 1) * points, corner * 128 + lane] = inner_table[:, corner]
    return table


def build_tables(n_gy, ez):
    p, q = ORDER + 1, MID_ORDER + 1
    fine, mid, low = gll_tables(ORDER), gll_tables(MID_ORDER), gll_tables(1)
    jf = interp_table(fine[0], mid[0])
    jm = interp_table(mid[0], low[0])
    k7, w7, s7, l7 = fine[2], np.diag(fine[1]), fine[3], fine[4]
    k3, w3, s3, l3 = mid[2], np.diag(mid[1]), mid[3], mid[4]
    pair, plain = {}, {}
    modes = p + 2
    a1 = blocks(s7.T, 2) @ line_extension(p, 2, False)
    own, sides = a1[:, : 2 * p], {-1: a1[:, 2 * p : 2 * p + 2], 1: a1[:, 2 * p + 2 :]}
    pair["wo"] = np.kron(own, own)
    halves = []
    for half in range(2):
        layer = slice(half, half + 1)
        parts = []
        for dx, dy in RING:
            if dy == 0:
                parts.append(np.kron(sides[dx][:, layer], own))
            elif dx == 0:
                parts.append(np.kron(own, sides[dy][:, layer]))
            else:
                parts.append(np.pad(np.kron(sides[dx], sides[dy][:, layer]), ((0, 0), (0, 6))))
        halves.append(np.concatenate(parts, 1))
    pair["wh"] = side_by_side(*halves)
    pair["az"] = (blocks(s7.T, ez) @ line_extension(p, ez, True)).T
    inner = s7[1:-1]
    raw = blocks(inner, 2)
    back = np.array(raw)
    back[p - 1] = back[p] = raw[p - 1] + raw[p]
    face = {-1: raw[:1], 1: raw[-1:]}
    pair["bo"] = np.kron(back, back)
    parts, rows = [], []
    edge = {-1: 0, 1: 2 * p - 1}
    for tx, ty in RING:
        scatter = np.zeros((16, 256)) if 0 in (tx, ty) else np.zeros((8, 256))
        if ty == 0:
            parts.append(np.kron(face[tx], back))
            for at in range(16):
                scatter[at, edge[tx] * 16 + at] = 1
        elif tx == 0:
            parts.append(np.kron(back, face[ty]))
            for at in range(16):
                scatter[at, at * 16 + edge[ty]] = 1
        else:
            parts.append(np.pad(np.kron(face[tx], face[ty]), ((0, 7), (0, 0))))
            scatter[0, edge[tx] * 16 + edge[ty]] = 1
        rows.append(scatter)
    pair["bf"] = np.concatenate(parts, 0)
    scat = np.concatenate(rows, 0).T
    plain["scat"] = (scat, BF)
    bz = z_back(inner, p, ez)
    pair["bz"] = bz

    count = 4 * modes
    ext = np.zeros((4, modes, 36))
    for element in range(4):
        start = 2 + p * element
        ext[element, 0, start - 2] += 1
        for at in range(p):
            ext[element, 1 + at, start + at] += 1
        ext[element, 1, start - 1] += 1
        ext[element, p, start + p] += 1
        ext[element, p + 1, start + p + 1] += 1
    a1w = blocks(s7.T, 4) @ ext.reshape(count, 36)
    middle = a1w[:, 10:26]
    beside = {-1: a1w[:, 0:10], 1: a1w[:, 26:36]}
    for name, group, rows in (("vl", LOW_SIDE, slice(0, 2 * modes)), ("vr", HIGH_SIDE, slice(2 * modes, None))):
        parts = []
        for half in range(2):
            for dx, dy in group:
                pieces = []
                for at in range(half, 10, 2):
                    if dy == 0:
                        pieces.append(np.kron(beside[dx][rows, at : at + 1], middle))
                    elif dx == 0:
                        pieces.append(np.kron(middle[rows], beside[dy][:, at : at + 1]))
                    else:
                        pieces.append(np.kron(beside[dx][rows], beside[dy][:, at : at + 1]))
                piece = np.concatenate(pieces, 1)
                parts.append(np.pad(piece, ((0, 0), (0, -piece.shape[1] % 16))))
        plain[name] = (np.concatenate(parts, 1), BF)
    plain["vo"] = (np.kron(middle, middle), BF)
    raw = blocks(inner, 4)
    around = np.array(raw[p : 3 * p])
    for at in (p - 1, 2 * p - 1, 3 * p - 1):
        for row in (at, at + 1):
            if p <= row < 3 * p:
                around[row - p] = raw[at] + raw[at + 1]
    plain["vb"] = (np.kron(around, around), BF)

    def weights(points):
        line = line_weights(points, 2)
        low_side, high_side = np.zeros(2 * points), np.zeros(2 * points)
        low_side[0], high_side[-1] = 0.5, 0.5
        return np.stack([np.kron(line, line), np.kron(line, low_side), np.kron(line, high_side)], 1)

    wt7, wt3 = weights(p), weights(q)
    columns = np.zeros((256, 128))
    columns[:, 0:3] = wt7
    columns[:96, 3:6] = scat.T @ wt7
    columns[:64, 6:9] = wt3
    columns[:, 9] = np.kron(np.tile(fine[1], 2), np.tile(fine[1], 2))
    plain["columns"] = (columns, F32)

    def three(stiff, mass, count):
        stiff, mass = blocks(stiff, count), blocks(mass, count)
        return np.kron(stiff, mass), np.kron(mass, stiff), np.kron(mass, mass)

    la = np.concatenate(three(jf.T @ k7, jf.T @ w7, 2), 0)
    ra = side_by_side(blocks(w7 @ jf, ez), blocks(k7 @ jf, ez))
    pair["la"] = la
    pair["lar"] = la @ scat
    pair["bzra"] = bz @ ra
    pair["jxy"] = np.kron(blocks(jf.T, 2), blocks(jf.T, 2))
    pair["jz"] = blocks(jf, ez)
    k7x, k7y, _ = three(k7, w7, 2)
    pair["k7"] = np.concatenate([k7x, k7y], 0)
    pair["kz7"] = blocks(k7, ez)
    plain["wz7"] = (np.tile(np.tile(fine[1], ez)[None], (8, 1)), F32)
    pair["lp"] = np.concatenate(three(k7 @ jf, w7 @ jf, 2), 0)
    pair["rp"] = side_by_side(blocks((w7 @ jf).T, ez), blocks((k7 @ jf).T, ez))
    pair["pxy"] = np.kron(blocks(jf, 2), blocks(jf, 2))
    pair["pz"] = blocks(jf.T, ez)

    def factor_rows(elements, scale):
        table = np.zeros((len(elements), 16))
        for at, (ex, ey) in enumerate(elements):
            for d in range(3):
                if scale[d] is not None:
                    table[at, d * 4 + ex * 2 + ey] = scale[d][at]
        return table

    def grid_elements(per):
        return [(x // per, y // per) for x in range(2 * per) for y in range(2 * per)]

    def direction_rows(elements):
        one = np.ones(len(elements))
        return np.concatenate([factor_rows(elements, [one if d == e else None for e in range(3)]) for d in range(3)], 0)

    spread = lambda per: np.kron(np.eye(ez), np.ones((1, per)))
    plain["e7"] = (direction_rows(grid_elements(p)), BF)
    plain["e3"] = (direction_rows(grid_elements(q)), BF)
    plain["e1"] = (direction_rows(grid_elements(2)), BF)
    plain["s64"] = (spread(p), BF)
    plain["s32"] = (spread(q), BF)
    plain["s256"] = (corner_columns(np.ones((1, 2)), ez), BF)
    grid = grid_elements(modes)
    li = np.array([l7[x % modes] for x in range(2 * modes) for y in range(2 * modes)])
    lj = np.array([l7[y % modes] for x in range(2 * modes) for y in range(2 * modes)])
    pair["ld7"] = factor_rows(grid, [li, lj, None])
    plain["le7"] = (factor_rows(grid, [None, None, np.ones(len(grid))]), BF)
    plain["s80"] = (spread(modes), BF)
    pair["sl80"] = spread(modes) * np.tile(l7, ez)[None]

    m3 = q + 2
    ext = np.zeros((4, m3, 6 * q))
    for element in range(4):
        start = q * (element + 1)
        ext[element, 0, start - 2] += 1
        for at in range(q):
            ext[element, 1 + at, start + at] += 1
        ext[element, 1, start - 1] += 1
        ext[element, q, start + q] += 1
        ext[element, q + 1, start + q + 1] += 1
    a1m = blocks(s3.T, 4) @ ext.reshape(4 * m3, 6 * q)
    order = RING + ((0, 0),)
    span = lambda d: slice((d + 1) * 2 * q, (d + 2) * 2 * q)
    wm = [np.kron(a1m[:, span(dx)], a1m[:, span(dy)]) for dx, dy in order]
    pair["wmn"] = np.concatenate(wm[:8], 1)
    pair["wmo"] = wm[8]
    pair["azm"] = (blocks(s3.T, ez) @ line_extension(q, ez, True)).T
    inner3 = s3[1:-1]
    raw3 = blocks(inner3, 4)
    back3 = np.array(raw3[q : 3 * q])
    for at in (q - 1, 2 * q - 1, 3 * q - 1):
        total = raw3[at] + raw3[at + 1]
        for row in (at, at + 1):
            if q <= row < 3 * q:
                back3[row - q] = total
    bm = np.kron(back3, back3)
    pair["bm"] = bm
    bzm = z_back(inner3, q, ez)
    pair["bzm"] = bzm
    ll = np.concatenate(three(jm.T @ k3, jm.T @ w3, 2), 0)
    pair["lb"] = np.concatenate([ll @ ((wt3[:, 0] + extra)[:, None] * bm) for extra in (0, wt3[:, 1], wt3[:, 2])], 0)
    pair["rb"] = bzm @ np.concatenate([corner_columns(w3 @ jm, ez), corner_columns(k3 @ jm, ez)], 1)
    pair["jl"] = np.kron(blocks(jm.T, 2), blocks(jm.T, 2))
    pair["rj"] = corner_columns(jm, ez)
    place = {direction: at for at, direction in enumerate(order)}

    def ring_row(ex, ey, d):
        dx, dy = ex // 2 - 1, ey // 2 - 1
        return place[(dx, dy)] * 16 + d * 4 + (ex % 2) * 2 + ey % 2

    ld3, le3 = np.zeros((576, 144)), np.zeros((576, 144))
    for x in range(24):
        for y in range(24):
            ex, ey = x // m3 + 1, y // m3 + 1
            ld3[x * 24 + y, ring_row(ex, ey, 0)] = l3[x % m3]
            ld3[x * 24 + y, ring_row(ex, ey, 1)] = l3[y % m3]
            le3[x * 24 + y, ring_row(ex, ey, 2)] = 1
    ld9, le9 = np.zeros((count * count, 144)), np.zeros((count * count, 144))
    for x in range(count):
        for y in range(count):
            ex, ey = x // modes + 1, y // modes + 1
            ld9[x * count + y, ring_row(ex, ey, 0)] = l7[x % modes]
            ld9[x * count + y, ring_row(ex, ey, 1)] = l7[y % modes]
            le9[x * count + y, ring_row(ex, ey, 2)] = 1
    pair["ld9"] = ld9
    plain["le9"] = (le9, BF)
    pair["ld3"] = ld3
    plain["le3"] = (le3, BF)
    plain["s48"] = (spread(m3), BF)
    pair["sl48"] = spread(m3) * np.tile(l3, ez)[None]
    er = np.zeros((3, 9, 2 * q, 2 * q, 144))
    for at in range(9):
        for x in range(2 * q):
            for y in range(2 * q):
                for d in range(3):
                    er[d, at, x, y, at * 16 + d * 4 + (x // q) * 2 + y // q] = 1
    plain["er"] = (er.reshape(3 * 576, 144), BF)
    pair["k3"] = np.concatenate(three(k3, w3, 2), 0)
    pair["rk3"] = side_by_side(blocks(w3, ez), blocks(k3, ez))
    corner_line = lambda table: np.kron(np.eye(6), table)
    modes_of = [a1m @ corner_line(table) for table in (k3 @ jm, w3 @ jm)]
    pair["wl"] = np.concatenate(
        [np.kron(modes_of[left], modes_of[right]) for left, right in ((0, 1), (1, 0), (1, 1))], 1
    )
    pair["ra3"] = side_by_side(
        blocks((w3 @ jm).T, ez) @ pair["azm"], blocks((k3 @ jm).T, ez) @ pair["azm"]
    )
    spread_vertices, spread_factors = np.zeros((144, 128)), np.zeros((3, 144, 144))
    for row in range(144):
        (ex, cx), (ey, cy) = divmod(row // 12, 2), divmod(row % 12, 2)
        vx, vy = ex + cx, ey + cy
        column = ((vy // 2) * 4 + AHEAD.index(vx // 2 - 1)) * 8 + (vx % 2) * 2 + vy % 2
        spread_vertices[row, column] = 1
        for d in range(3):
            at = order.index((ex // 2 - 1, ey // 2 - 1))
            spread_factors[d, row, at * 16 + d * 4 + (ex % 2) * 2 + ey % 2] = 1
    plain["ev"] = (spread_vertices, BF)
    plain["ef"] = (spread_factors.reshape(432, 144), BF)
    corner_z = np.zeros((ez, 2 * ez))
    for element in range(ez):
        for at in range(2):
            corner_z[(element + at) % ez, 2 * element + at] = 1
    plain["cz"] = (np.tile(corner_z, (4, 1)), BF)
    plain["s16"] = (spread(2), BF)
    vertex_line = lambda table: np.array(
        [[table[at % q, v - at // q] if 0 <= v - at // q <= 1 else 0.0 for v in range(8)] for at in range(6 * q)]
    )
    plain1 = vertex_line(jm)

    def vertex_columns(left, right, dx, dy):
        table = np.zeros((64, 4, 4, 8))
        for iy in range(4):
            for ix, ahead in enumerate(AHEAD):
                for x in range(2):
                    for y in range(2):
                        table[:, iy, ix, x * 2 + y] = np.kron(
                            left[span(dx), (ahead + 1) * 2 + x], right[span(dy), iy * 2 + y]
                        )
        return table.reshape(64, 128)

    pair["jc"] = vertex_columns(plain1, plain1, 0, 0)

    def z_vertices(table):
        result = np.zeros((ez, ez * q))
        for element in range(ez):
            for at in range(q):
                result[element, element * q + at] += table[at, 0]
                result[(element + 1) % ez, element * q + at] += table[at, 1]
        return np.tile(result, (4, 1))

    pair["rcj"] = z_vertices(jm)
    mask, left = np.zeros((n_gy, 16, 128)), np.zeros((n_gy, 16, 16))
    for gy in range(n_gy):
        for row in range(16):
            vx, vy = row // 8 + row // 4 % 2, row // 2 % 2 + row % 2
            owner = gy + vy // 2
            if owner < n_gy:
                first = owner * 32 + (vx % 2) * 16 + (vy % 2) * 8
                mask[gy, row, first % 128 : first % 128 + 8] = 1
                left[gy, first // 128 + 4 * (vx // 2), row] = 1
    plain["mask"] = (mask.reshape(-1, 128), F32)
    plain["left"] = (left.reshape(-1, 16), BF)
    chosen = np.zeros((8, 32))
    select = np.zeros((32, 8))
    for lane in range(32):
        chosen[lane // 8, lane] = 1
        select[lane, lane % 8] = 1
    plain["chosen"] = (chosen, F32)
    plain["select"] = (select, BF)
    tables = {}
    for name, table in pair.items():
        table = fitted(np.asarray(table, np.float64), name in RIGHT)
        high = table.astype(ml_dtypes.bfloat16)
        rest = (table - high.astype(np.float64)).astype(ml_dtypes.bfloat16)
        if name in RIGHT:
            tables[name] = np.block([[high, rest], [high, np.zeros_like(rest)]])[None]
        else:
            tables[name] = np.stack([high, rest])
    for name, (table, kind) in plain.items():
        table = fitted(np.asarray(table), name in RIGHT)
        table = np.concatenate([table, table], 0) if name in RIGHT else table
        tables[name] = table.astype(ml_dtypes.bfloat16 if kind is BF else np.float32)[None]
    return tables


STAGES = (
    (
        "columns", "wo", "jxy", "jz", "s80", "sl80", "ld7", "le7", "e7", "e3", "e1", "s64", "s32", "s256",
        "wz7", "chosen", "mask",
    ),
    ("wh", "az", "bf", "bo", "la", "bzra", "ld3", "le3", "s48", "sl48", "er", "lar"),
    (
        "wmo", "jl", "rj", "scat", "bz", "k7", "kz7", "wmn", "azm", "lb", "rb", "left", "bm", "bzm", "select",
        "rk3", "k3", "wl", "ra3", "ev", "ef", "cz", "s16", "jc", "rcj", "rp", "lp", "pxy", "pz",
    ),
    ("ld9", "le9", "vo", "vl", "vr", "vb"),
)


def pack(tables):
    stacks, places = {}, {}
    for stage, names in enumerate(STAGES):
        for name in names:
            table = tables[name]
            key = (stage, table.dtype.name, table.shape[-1])
            parts = stacks.setdefault(key, [])
            at = sum(part.shape[0] for part in parts)
            height = -(-table.shape[1] // 16) * 16
            for part in table:
                parts.append(np.pad(part, ((0, height - part.shape[0]), (0, 0))))
            places[name] = (key, at, height, table.shape[1])
    keys = tuple(stacks)
    return keys, [np.concatenate(stacks[key], 0) for key in keys], places


class Table:
    def __init__(self, ref, place):
        _, self.at, self.height, self.rows = place
        self.ref = ref
        self.shape = (2, self.rows, ref.shape[-1])

    def __getitem__(self, part):
        part = 0 if part is Ellipsis else part
        return self.ref[self.at + part * self.height : self.at + part * self.height + self.rows, :]

    def piece(self, part, start, rows):
        return self.ref[pl.ds(self.at + part * self.height + start, rows), :]


def dot(a, b):
    return jnp.dot(a, b, preferred_element_type=F32)


def split(x):
    high = x.astype(BF)
    return high, (x - high.astype(F32)).astype(BF)


def wide(x, lanes=128):
    if x.shape[1] == lanes:
        return x
    return jnp.concatenate([x, jnp.zeros((x.shape[0], lanes - x.shape[1]), x.dtype)], 1)


def tall(x, rows):
    if x.shape[0] == rows:
        return x
    return jnp.concatenate([x, jnp.zeros((rows - x.shape[0], x.shape[1]), x.dtype)], 0)


def halves(x):
    middle = x.shape[1] // 2
    return x[:, :middle] + x[:, middle:]


def exactly(main, small, x):
    high, rest = split(x)
    return halves(dot(main, jnp.concatenate([high, rest], 1))) + dot(small, high)


def left3(table, x):
    return exactly(table[0], table[1], tall(x, table.shape[-1]))


def left2(table, x):
    return halves(dot(table[...], jnp.concatenate(split(tall(x, table.shape[-1])), 1)))


def terms3(table, x):
    x = tall(x, table.shape[-1])
    rows = table.shape[1] // 3
    first = exactly(table.piece(0, 0, 2 * rows), table.piece(1, 0, 2 * rows), x[:, 0:128])
    third = exactly(table.piece(0, 2 * rows, rows), table.piece(1, 2 * rows, rows), x[:, 128:256])
    return first[0:rows], first[rows:], third


def right3(x, table):
    return halves(right2(x, table))


def right2(x, table):
    return dot(jnp.concatenate(split(wide(x)), 1), table[...])


KEPT = {
    "fine_f": (768, 128), "mid_f": (192, 128), "low_f": (48, 256), "ring_f": (1728, 128), "inverse7": (400, 128),
    "inverse3": (576, 128), "wt7": (256, 128), "wr7": (96, 128), "wt3": (64, 128), "base_mid": (64, 128),
    "base_low": (16, 256), "local": (256, 128), "first_fine": (256, 128), "base_fine": (256, 128),
    "first_mid": (64, 128), "modal": (400, 128), "modal3": (576, 128), "own_part": (192, 128), "base_ring": (576, 128),
    "ww7": (256, 128), "inverse9": (1600, 128), "corner_f": (432, 128), "modal9": (1600, 128),
}


def cycle_kernel(keys, places, n_gx, n_gy, *refs):
    r_hbm, len_hbm, inv_hbm = refs[:3]
    count = len(keys)
    packed = refs[3 : 3 + count]
    out_fine, out_mid, out_low = refs[3 + count : 6 + count]
    stores = refs[6 + count : 6 + 2 * count]
    (
        r_ref, len_ref, inv_ref, rs, fs, hb1, fb1, rm, fm, rp, fp, hb2, hs1, hs2, st1, corner, held, gs, gb, cb,
        send_sem, recv_sem, gsend, grecv, csend, crecv, in_sem, table_sem,
    ) = refs[6 + 2 * count : -len(KEPT)]
    gx, gy = lax.axis_index("gx"), lax.axis_index("gy")
    last = n_gy - 1
    barrier = pltpu.get_barrier_semaphore()

    def greet(ahead, row):
        pl.semaphore_signal(
            barrier, inc=1, device_id=(lax.rem(gx + (ahead + n_gx), n_gx), row), device_id_type=MESH
        )

    def greet_if(row, *columns):
        @pl.when((row >= 0) & (row <= last))
        def _():
            for ahead in columns:
                greet(ahead, row)

    greet_if(gy + 1, 0, 1, -1)
    greet_if(gy - 1, 0, 1, -1)
    greet(1, gy)
    greet(-1, gy)
    greet(2, gy)
    greet_if(gy + 1, 2)
    greet_if(gy - 1, 2)
    greet_if(gy + 2, 1, 2)
    for row in range(n_gy):
        @pl.when((row < gy - 1) | (row > gy + 1))
        def _():
            greet(0, row)
            greet(-1, row)
    inputs = [
        pltpu.make_async_copy(source, target, in_sem.at[at])
        for at, (source, target) in enumerate(((len_hbm, len_ref), (r_hbm, r_ref), (inv_hbm, inv_ref)))
    ]
    loads = [pltpu.make_async_copy(packed[at], stores[at], table_sem.at[at]) for at in range(count)]
    for load in inputs:
        load.start()

    def fetch(*stages):
        for key, load in zip(keys, loads):
            if key[0] in stages:
                load.start()

    fetch(0)

    def ready(stage):
        for key, load in zip(keys, loads):
            if key[0] == stage:
                load.wait()

    kept = dict(zip(KEPT, refs[-len(KEPT) :]))

    def keep(name, value):
        kept[name][...] = value
        return kept[name]

    t = {name: Table(stores[keys.index(place[0])], place) for name, place in places.items()}
    at_bottom, at_top = gy == 0, gy == last
    not_bottom, not_top = gy > 0, gy < last
    sent = {0: None, 1: not_bottom, 2: not_top}

    def guarded(condition, action):
        if condition is None:
            action()
        else:
            pl.when(condition)(action)

    def exchange(phase, source, buffer, rows):
        at = offsets(rows)

        def group(number):
            def action():
                for index in range(*GROUPS[number]):
                    tx, ty = RING[index]
                    slot = RING.index((-tx, -ty))
                    landing = (0, 2, 1)[number]
                    pltpu.make_async_remote_copy(
                        src_ref=source(index),
                        dst_ref=buffer.at[pl.ds(at[slot], rows[slot])],
                        send_sem=send_sem.at[phase, number],
                        recv_sem=recv_sem.at[phase, landing],
                        device_id=(lax.rem(gx + (tx + n_gx), n_gx), gy + ty),
                        device_id_type=MESH,
                    ).start()

            return action

        for number in (1, 2, 0):
            guarded(sent[number], group(number))

    def settle(phase, sems, buffer, rows):
        at = offsets(rows)
        for number in range(3):
            first, end = GROUPS[number]
            piece = buffer.at[pl.ds(at[first], at[end] - at[first])]
            guarded(sent[number], lambda: pltpu.make_async_copy(piece, piece, sems.at[phase, number]).wait())

    def clear(number):
        first, end = GROUPS[number]
        for buffer, rows in (
            (fs, BLOCK_ROWS), (hb1, FACE_ROWS), (fb1, FACE_ROWS), (rp, BLOCK_ROWS),
            (fp, BLOCK_ROWS), (hb2, WIDE_ROWS),
        ):
            at = offsets(rows)
            buffer[at[first] : at[end], :] = jnp.zeros((at[end] - at[first], buffer.shape[1]), buffer.dtype)

    @pl.when(at_bottom)
    def _():
        clear(1)
        cb[0:32, :] = jnp.zeros((32, 128), F32)

    @pl.when(at_top)
    def _():
        clear(2)
        cb[64:96, :] = jnp.zeros((32, 128), F32)

    @pl.when(gy >= last - 1)
    def _():
        cb[96:128, :] = jnp.zeros((32, 128), F32)

    def halo(field, stage):
        at = offsets(FACE_ROWS)
        for index, (tx, ty) in enumerate(RING):
            xs, ys = (14, 0)[tx < 0], (14, 0)[ty < 0]
            if ty == 0:
                layers = field[xs, :, :], field[xs + 1, :, :]
            elif tx == 0:
                layers = field[:, ys, :], field[:, ys + 1, :]
            else:
                layers = field[xs : xs + 2, ys, :], field[xs : xs + 2, ys + 1, :]
            stage[at[index] : at[index + 1], :] = tall(jnp.concatenate(layers, 1), at[index + 1] - at[index])

    at_wide = offsets(WIDE_ROWS)

    def wide_halo(field, stage):
        for index, (tx, ty) in enumerate(RING):
            xs, ys = (6, 0)[tx < 0], (6, 0)[ty < 0]
            if 0 not in (tx, ty):
                corner[48:64, :] = jnp.zeros((16, 128), F32)
            for pair in range(5):
                xa, ya = xs + 2 * pair, ys + 2 * pair
                at = at_wide[index] + pair * 16
                if ty == 0:
                    layers = field[xa, :, :], field[xa + 1, :, :]
                    stage[at : at + 16, :] = jnp.concatenate(layers, 1).astype(stage.dtype)
                elif tx == 0:
                    layers = field[:, ya, :], field[:, ya + 1, :]
                    stage[at : at + 16, :] = jnp.concatenate(layers, 1).astype(stage.dtype)
                else:
                    layers = field[xs : xs + 10, ya, :], field[xs : xs + 10, ya + 1, :]
                    corner[pair * 10 : pair * 10 + 10, :] = jnp.concatenate(layers, 1)
            if 0 not in (tx, ty):
                stage[at_wide[index] : at_wide[index + 1], :] = corner[...].astype(stage.dtype)

    def side_values(buffer, group):
        pieces = []
        for direction in group:
            index = RING.index(direction)
            pieces.append(buffer[at_wide[index] : at_wide[index + 1], :])
        turned_back = [pltpu.roll(piece.astype(F32), 64, 1).astype(BF) for piece in pieces]
        return tall(jnp.concatenate(pieces + turned_back, 0), 768)

    def unfold(buffer):
        packed_rows = tall(buffer[...], 128)
        return jnp.concatenate([packed_rows, pltpu.roll(packed_rows, 64, 1)], 0)

    def fold(block):
        result = block[0:16]
        for part in range(1, 4):
            result = result + pltpu.roll(block[part * 16 : part * 16 + 16], part * 32, 1)
        return result

    def spread_blocks(folded, blocks_ref):
        for part in range(4):
            turned_back = pltpu.roll(folded[0:128, :], (128 - part * 32) % 128, 1) if part else folded[0:128, :]
            for slot in range(8):
                blocks_ref[slot * 64 + part * 16 : slot * 64 + part * 16 + 16, :] = turned_back[
                    slot * 16 : slot * 16 + 16
                ]

    at_face = offsets(FACE_ROWS)

    inputs[0].wait()
    own_f = 8 * 16
    for ex in range(2):
        a, b, c = len_ref[0, ex], len_ref[1, ex], len_ref[2, ex]
        fs[own_f + ex * 2 : own_f + ex * 2 + 2, :] = wide(b * c / (2.0 * a))
        fs[own_f + 4 + ex * 2 : own_f + 6 + ex * 2, :] = wide(a * c / (2.0 * b))
        fs[own_f + 8 + ex * 2 : own_f + 10 + ex * 2, :] = wide(a * b / (2.0 * c))
    fs[own_f + 12 : own_f + 16, :] = jnp.zeros((4, 128), F32)
    inputs[1].wait()
    halo(r_ref, hs1)
    near = jnp.minimum(gy + 1, last) - jnp.maximum(gy - 2, 0) + 1
    pl.semaphore_wait(barrier, 2 * n_gy - 1 + 2 * near)
    exchange(1, lambda index: hs1.at[pl.ds(at_face[index], FACE_ROWS[index])], hb1, FACE_ROWS)
    exchange(0, lambda index: fs.at[pl.ds(own_f, 16)], fs, BLOCK_ROWS)
    fetch(1, 2)

    bottom_on = jnp.where(at_bottom, 1.0, 0.0)
    top_on = jnp.where(at_top, 1.0, 0.0)

    ready(0)
    columns = t["columns"][...]

    def wall_weight(rows, at):
        piece = columns[0:rows]
        return piece[:, at : at + 1] + bottom_on * piece[:, at + 1 : at + 2] + top_on * piece[:, at + 2 : at + 3]

    wt7 = keep("wt7", jnp.broadcast_to(wall_weight(256, 0), (256, 128)))
    wr7 = keep("wr7", jnp.broadcast_to(wall_weight(96, 3), (96, 128)))
    wt3 = keep("wt3", jnp.broadcast_to(wall_weight(64, 6), (64, 128)))
    ww7 = keep("ww7", jnp.broadcast_to(columns[:, 9:10], (256, 128)))
    r = wide(r_ref[...].reshape(256, 64))
    f_own = wide(fs[own_f : own_f + 16, :])
    d7 = left3(t["ld7"], right2(f_own, t["s80"])) + left2(t["le7"], right3(f_own, t["sl80"]))
    inverse7 = keep("inverse7", jnp.where(d7 > 0.0, 1.0 / jnp.where(d7 > 0.0, d7, 1.0), 0.0))
    modal = keep("modal", left3(t["wo"], r))
    base_mid = keep("base_mid", right3(left3(t["jxy"], r), t["jz"]))
    fine_f = keep("fine_f", left2(t["e7"], right2(f_own, t["s64"])))
    mid_f = keep("mid_f", left2(t["e3"], right2(f_own, t["s32"])))
    low_f = keep("low_f", left2(t["e1"], right2(f_own, t["s256"])))

    def fine_back(modal, buffer, stage, phase):
        modal = right3(modal, t["az"]) * inverse7[...]
        stage[...] = left3(t["bf"], modal)
        exchange(phase, lambda index: stage.at[pl.ds(at_face[index], FACE_ROWS[index])], buffer, FACE_ROWS)
        return left3(t["bo"], modal)

    ready(1)
    settle(1, recv_sem, hb1, FACE_ROWS)
    modal = modal[...] + left3(t["wh"], unfold(hb1))
    fetch(3)
    local = keep("local", fine_back(modal, fb1, st1, 2) * wt7[...])
    own_part = keep("own_part", jnp.concatenate(terms3(t["la"], right3(local[...], t["bzra"])), 0))
    settle(0, recv_sem, fs, BLOCK_ROWS)
    ring_f = wide(fs[...])
    d3 = left3(t["ld3"], right2(ring_f, t["s48"])) + left2(t["le3"], right3(ring_f, t["sl48"]))
    inverse3 = keep("inverse3", jnp.where(d3 > 0.0, 1.0 / jnp.where(d3 > 0.0, d3, 1.0), 0.0))
    ring_f = keep("ring_f", left2(t["er"], right2(ring_f, t["s32"])))

    settle(2, recv_sem, fb1, FACE_ROWS)
    faces = wide(fb1[...]) * wr7[...]
    face_part = terms3(t["lar"], right3(faces, t["bzra"]))
    residual_mid = base_mid[...] - (
        mid_f[0:64] * (own_part[0:64] + face_part[0])
        + mid_f[64:128] * (own_part[64:128] + face_part[1])
        + mid_f[128:192] * (own_part[128:192] + face_part[2])
    )
    rp[128:144, :] = fold(residual_mid)
    exchange(3, lambda index: rp.at[pl.ds(128, 16)], rp, BLOCK_ROWS)
    rm[512:576, :] = residual_mid

    ready(2)
    own_modal = keep("modal3", left3(t["wmo"], residual_mid))
    base_low = keep("base_low", right3(left3(t["jl"], residual_mid), t["rj"]))
    first_fine = keep("first_fine", right3(local[...] + left2(t["scat"], faces), t["bz"]))
    massed = left3(t["k7"], first_fine[...] * t["wz7"][...][0:1])
    along_z = right3(first_fine[...], t["kz7"]) * ww7[...]
    base_fine = keep(
        "base_fine",
        wide(r_ref[...].reshape(256, 64))
        - (fine_f[0:256] * massed[0:256] + fine_f[256:512] * massed[256:512] + fine_f[512:768] * along_z),
    )

    settle(3, recv_sem, rp, BLOCK_ROWS)
    spread_blocks(rp, rm)
    modal3 = own_modal[...] + left3(t["wmn"], rm[0:512, :])
    modal3 = right3(modal3, t["azm"]) * inverse3[...]
    variant = jnp.where(at_bottom, 1, jnp.where(at_top, 2, 0))
    rows = pl.multiple_of(variant * 48, 16)
    low = exactly(t["lb"].piece(0, rows, 48), t["lb"].piece(1, rows, 48), tall(modal3, t["lb"].shape[-1]))
    low = right3(low, t["rb"])
    low = base_low[...] - (
        low_f[0:16] * low[0:16, 0:256] + low_f[16:32] * low[16:32, 0:256] + low_f[32:48] * low[32:48, 256:512]
    )
    wall = pl.multiple_of(gy * 16, 16)
    low = tall(halves(low) * t["mask"].piece(0, wall, 16), 128)
    message = halves(dot(t["left"].piece(0, wall, 16), jnp.concatenate(split(low), 1)))[0:8]
    gs[...] = message

    def send_slab(step, ahead):
        slot = step + jnp.where(ahead == 0, -1, n_gy - 1)
        pltpu.make_async_remote_copy(
            src_ref=gs,
            dst_ref=gb.at[slot],
            send_sem=gsend,
            recv_sem=grecv,
            device_id=(lax.rem(gx + ahead, n_gx), lax.rem(gy + step, n_gy)),
            device_id_type=MESH,
        ).start()

    for step in range(1, n_gy):
        send_slab(step, 0)
    for step in range(n_gy):
        send_slab(step, 1)

    first_mid = keep("first_mid", right3(left3(t["bm"], modal3) * wt3[...], t["bzm"]))
    fm[512:576, :] = first_mid[...]
    fp[128:144, :] = fold(first_mid[...])
    exchange(4, lambda index: fp.at[pl.ds(128, 16)], fp, BLOCK_ROWS)

    pltpu.make_async_copy(gb, gb, grecv).wait()
    here = gs[...] + jnp.sum(gb[0 : n_gy - 1], axis=0)
    behind = jnp.sum(gb[n_gy - 1 :], axis=0)
    inputs[2].wait()
    chunks = inv_ref.shape[2] // 128
    vector = here + pltpu.roll(behind, 4, 0)
    row = lax.broadcasted_iota(jnp.int32, (8, 128), 0)
    vector = jnp.concatenate([jnp.where(row == chunk, vector, 0.0) for chunk in range(chunks)], 1)
    vector = tall(vector, 16).astype(BF)
    inverse = tall(inv_ref[0], 128)
    solved = lax.dot_general(vector, inverse, (((1,), (1,)), ((), ())), preferred_element_type=F32)
    solved = jnp.sum(solved, axis=0, keepdims=True)
    solved = jnp.broadcast_to(solved, (8, 128)) * t["chosen"][...]
    own_c = (4 + 3) * 8
    cb[own_c : own_c + 8, :] = solved

    def send_correction(iy):
        def action():
            for ix, ahead in enumerate(AHEAD):
                if (ahead, iy - 1) != (0, 0):
                    pltpu.make_async_remote_copy(
                        src_ref=cb.at[pl.ds(own_c, 8)],
                        dst_ref=cb.at[pl.ds((iy * 4 + ix) * 8, 8)],
                        send_sem=csend.at[iy],
                        recv_sem=crecv.at[iy],
                        device_id=(lax.rem(gx - ahead + n_gx, n_gx), gy - (iy - 1)),
                        device_id_type=MESH,
                    ).start()

        return action

    to_group = (not_top, None, not_bottom, gy > 1)
    from_group = (not_bottom, None, not_top, gy < last - 1)
    for iy in range(4):
        guarded(to_group[iy], send_correction(iy))

    def settle_corrections(sems, conditions):
        for iy in range(4):
            piece = cb.at[pl.ds(iy * 32, 24 if iy == 1 else 32)]
            guarded(conditions[iy], lambda: pltpu.make_async_copy(piece, piece, sems.at[iy]).wait())

    ready(3)
    ring_l = wide(fs[...])
    d9 = left3(t["ld9"], right2(ring_l, t["s80"])) + left2(t["le9"], right3(ring_l, t["sl80"]))
    inverse9 = keep("inverse9", jnp.where(d9 > 0.0, 1.0 / jnp.where(d9 > 0.0, d9, 1.0), 0.0))
    corner_f = keep("corner_f", left2(t["ef"], right2(ring_l, t["s16"])))
    low_out = right2(tall(solved, 16), t["select"])
    out_low[0] = low_out[0:2, 0:8]
    out_low[1] = low_out[2:4, 0:8]
    settle(4, recv_sem, fp, BLOCK_ROWS)
    spread_blocks(fp, fm)
    turned = right3(fm[...], t["rk3"])
    parts = []
    for at in range(9):
        piece = terms3(t["k3"], turned[at * 64 : (at + 1) * 64])
        parts.append(
            rm[at * 64 : (at + 1) * 64, :]
            - (
                ring_f[at * 64 : (at + 1) * 64] * piece[0]
                + ring_f[576 + at * 64 : 576 + (at + 1) * 64] * piece[1]
                + ring_f[1152 + at * 64 : 1152 + (at + 1) * 64] * piece[2]
            )
        )
    base_ring = keep("base_ring", jnp.concatenate(parts, 0))
    modal3 = left3(t["wmn"], base_ring[0:512]) + left3(t["wmo"], base_ring[512:576])
    modal3 = keep("modal3", right3(modal3, t["azm"]))

    settle_corrections(crecv, from_group)
    corrections = wide(cb[...])
    change = left2(t["ev"], right2(corrections, t["cz"]))
    change = right3(jnp.concatenate([change * corner_f[at * 144 : at * 144 + 144] for at in range(3)], 0), t["ra3"])
    change = jnp.concatenate([change[0:288, 0:128], change[288:432, 128:256]], 0)
    modal3 = (modal3[...] - left3(t["wl"], change)) * inverse3[...]
    held[0:64, :] = first_mid[...] + right3(left3(t["jc"], corrections), t["rcj"])
    mid_result = held[0:64, :] + right3(left3(t["bm"], modal3) * wt3[...], t["bzm"])

    turned = right3(mid_result, t["rp"])
    turned = terms3(t["lp"], turned)
    residual = base_fine[...] - (
        fine_f[0:256] * turned[0]
        + fine_f[256:512] * turned[1]
        + fine_f[512:768] * turned[2]
    )
    rs[...] = residual[:, 0:64].reshape(16, 16, 64)
    wide_halo(rs, hs2)
    exchange(5, lambda index: hs2.at[pl.ds(at_wide[index], WIDE_ROWS[index])], hb2, WIDE_ROWS)
    out_mid[...] = mid_result[:, 0:32].reshape(8, 8, 32)
    modal9 = keep("modal9", dot(t["vo"][...], residual.astype(BF)))
    held[...] = first_fine[...] + right3(left3(t["pxy"], mid_result), t["pz"])
    settle(5, recv_sem, hb2, WIDE_ROWS)
    modal = jnp.concatenate(
        [
            modal9[0:800] + dot(t["vl"][...], side_values(hb2, LOW_SIDE)),
            modal9[800:1600] + dot(t["vr"][...], side_values(hb2, HIGH_SIDE)),
        ],
        0,
    )
    modal = right3(modal, t["az"]) * inverse9[...]
    local = dot(t["vb"][...], tall(modal, 1664).astype(BF)) * wt7[...]
    result = held[...] + right3(local, t["bz"])
    out_fine[...] = result[:, 0:64].reshape(16, 16, 64)

    for phase, buffer, rows in (
        (0, fs, BLOCK_ROWS), (1, hb1, FACE_ROWS), (2, fb1, FACE_ROWS), (3, rp, BLOCK_ROWS),
        (4, fp, BLOCK_ROWS), (5, hb2, WIDE_ROWS),
    ):
        settle(phase, send_sem, buffer, rows)
    pltpu.make_async_copy(gb, gb, gsend).wait()
    settle_corrections(csend, to_group)


def hand_over(*refs):
    copies = [pltpu.make_async_copy(refs[at], refs[3 + at], refs[6].at[at]) for at in range(3)]
    for copy in copies:
        copy.start()
    for copy in copies:
        copy.wait()


def shards(n_gx, n_gy, local_residual, lengths, coarse_inverse):
    keys, packed, places = pack(build_tables(n_gy, lengths.shape[3]))
    vmem = pl.BlockSpec(memory_space=pltpu.VMEM)
    scratch = [pltpu.VMEM(table.shape, BF if key[1] == "bfloat16" else F32) for key, table in zip(keys, packed)]
    scratch += [
        pltpu.VMEM(local_residual.shape, F32),
        pltpu.VMEM(lengths.shape, F32),
        pltpu.VMEM(coarse_inverse.shape, BF),
        pltpu.VMEM((16, 16, 64), F32),
        pltpu.VMEM((144, 128), F32),
        pltpu.VMEM((96, 128), F32),
        pltpu.VMEM((96, 128), F32),
        pltpu.VMEM((576, 128), F32),
        pltpu.VMEM((576, 128), F32),
        pltpu.VMEM((144, 128), F32),
        pltpu.VMEM((144, 128), F32),
        pltpu.VMEM((576, 128), BF),
        pltpu.VMEM((96, 128), F32),
        pltpu.VMEM((576, 128), BF),
        pltpu.VMEM((96, 128), F32),
        pltpu.VMEM((64, 128), F32),
        pltpu.VMEM((256, 128), F32),
        pltpu.VMEM((8, 128), F32),
        pltpu.VMEM((2 * n_gy - 1, 8, 128), F32),
        pltpu.VMEM((128, 128), F32),
        pltpu.SemaphoreType.DMA((6, 3)),
        pltpu.SemaphoreType.DMA((6, 3)),
        pltpu.SemaphoreType.DMA,
        pltpu.SemaphoreType.DMA,
        pltpu.SemaphoreType.DMA((4,)),
        pltpu.SemaphoreType.DMA((4,)),
        pltpu.SemaphoreType.DMA((3,)),
        pltpu.SemaphoreType.DMA((len(keys),)),
    ]
    scratch += [pltpu.VMEM(shape, F32) for shape in KEPT.values()]
    outs = pl.pallas_call(
        functools.partial(cycle_kernel, keys, places, n_gx, n_gy),
        out_shape=(
            jax.ShapeDtypeStruct((16, 16, 64), F32),
            jax.ShapeDtypeStruct((8, 8, 32), F32),
            jax.ShapeDtypeStruct((2, 2, 8), F32),
        ),
        in_specs=[pl.BlockSpec(memory_space=pl.ANY)] * (3 + len(keys)),
        out_specs=(vmem, vmem, vmem),
        scratch_shapes=scratch,
        compiler_params=pltpu.CompilerParams(collective_id=0, has_side_effects=True, vmem_limit_bytes=60 * 1024 * 1024),
    )(local_residual, lengths, coarse_inverse, *[jnp.asarray(table) for table in packed])
    return pl.pallas_call(
        hand_over,
        out_shape=tuple(jax.ShapeDtypeStruct(out.shape, out.dtype) for out in outs),
        in_specs=[vmem] * 3,
        out_specs=[pl.BlockSpec(memory_space=pl.ANY)] * 3,
        scratch_shapes=[pltpu.SemaphoreType.DMA((3,))],
    )(*outs)


def solution(mesh):
    in_specs = (P("gx", "gy", None), P(None, "gx", "gy", None), P("gx", "gy", None))
    out_specs = (P("gx", "gy", None), P("gx", "gy", None), P("gx", "gy", None))
    return jax.shard_map(
        functools.partial(shards, mesh.shape["gx"], mesh.shape["gy"]),
        mesh=mesh,
        in_specs=in_specs,
        out_specs=out_specs,
        check_vma=False,
    )
```

```python
import functools
import math

import jax
import jax.numpy as jnp
import ml_dtypes
import numpy as np
from jax import lax
from jax.experimental import pallas as pl
from jax.experimental.pallas import tpu as pltpu
from jax.sharding import PartitionSpec as P

ORDER = 7
MID_ORDER = 3


def legendre_pair(order, point):
    older = 1.0
    newer = point
    for degree in range(2, order + 1):
        nexter = ((2 * degree - 1) * point * newer - (degree - 1) * older) / degree
        older = newer
        newer = nexter
    return (newer, older)


def jacobi_eigen(matrix):
    count_n = len(matrix)
    work = [list(row_items) for row_items in matrix]
    vectors = [
        [1.0 if row_at == col_at else 0.0 for col_at in range(count_n)] for row_at in range(count_n)
    ]
    for sweep_count in range(60):
        for lower_at in range(count_n):
            for upper_at in range(lower_at + 1, count_n):
                off_value = work[lower_at][upper_at]
                if abs(off_value) < 1e-18 * (
                    abs(work[lower_at][lower_at]) + abs(work[upper_at][upper_at])
                ):
                    continue
                angle_ratio = (work[upper_at][upper_at] - work[lower_at][lower_at]) / (
                    2.0 * off_value
                )
                sign_value = 1.0 if angle_ratio >= 0 else -1.0
                tangent = sign_value / (
                    abs(angle_ratio) + math.sqrt(angle_ratio * angle_ratio + 1.0)
                )
                cosine = 1.0 / math.sqrt(tangent * tangent + 1.0)
                sine_value = tangent * cosine
                for other_at in range(count_n):
                    left_value = work[other_at][lower_at]
                    right_value = work[other_at][upper_at]
                    work[other_at][lower_at] = cosine * left_value - sine_value * right_value
                    work[other_at][upper_at] = sine_value * left_value + cosine * right_value
                for other_at in range(count_n):
                    left_value = work[lower_at][other_at]
                    right_value = work[upper_at][other_at]
                    work[lower_at][other_at] = cosine * left_value - sine_value * right_value
                    work[upper_at][other_at] = sine_value * left_value + cosine * right_value
                for other_at in range(count_n):
                    left_value = vectors[other_at][lower_at]
                    right_value = vectors[other_at][upper_at]
                    vectors[other_at][lower_at] = cosine * left_value - sine_value * right_value
                    vectors[other_at][upper_at] = sine_value * left_value + cosine * right_value
    eigen_list = [work[row_at][row_at] for row_at in range(count_n)]
    ordering = sorted(range(count_n), key=lambda index_at: eigen_list[index_at])
    rates = [eigen_list[index_at] for index_at in ordering]
    basis = [[vectors[row_at][index_at] for index_at in ordering] for row_at in range(count_n)]
    return (rates, basis)


def gll_tables(order):
    point_count = order + 1
    node_list = []
    for node_at in range(point_count):
        point = math.cos(math.pi * node_at / order)
        for newton_step in range(100):
            top_value, lower_value = legendre_pair(order, point)
            point = point - (point * top_value - lower_value) / ((order + 1) * top_value)
        node_list.append(point)
    node_list = node_list[::-1]
    node_list[0] = -1.0
    node_list[-1] = 1.0
    values = [legendre_pair(order, point)[0] for point in node_list]
    weight_list = [2.0 / (order * (order + 1) * value_at**2) for value_at in values]
    derivative = [[0.0] * point_count for row_at in range(point_count)]
    for row_at in range(point_count):
        for col_at in range(point_count):
            if row_at != col_at:
                derivative[row_at][col_at] = values[row_at] / (
                    values[col_at] * (node_list[row_at] - node_list[col_at])
                )
    derivative[0][0] = -order * (order + 1) / 4.0
    derivative[order][order] = order * (order + 1) / 4.0
    stiff_list = [
        [
            sum(
                (
                    derivative[inner_at][row_at]
                    * weight_list[inner_at]
                    * derivative[inner_at][col_at]
                    for inner_at in range(point_count)
                )
            )
            for col_at in range(point_count)
        ]
        for row_at in range(point_count)
    ]
    extent = 3 * order + 1
    big_stiff = [[0.0] * extent for row_at in range(extent)]
    big_mass = [0.0] * extent
    for offset_at in (0, order, 2 * order):
        for row_at in range(point_count):
            big_mass[offset_at + row_at] += weight_list[row_at]
            for col_at in range(point_count):
                big_stiff[offset_at + row_at][offset_at + col_at] += stiff_list[row_at][col_at]
    chosen = list(range(order - 1, 2 * order + 2))
    root_mass = [1.0 / math.sqrt(big_mass[index_at]) for index_at in chosen]
    scaled = [
        [
            root_mass[row_at] * big_stiff[chosen[row_at]][chosen[col_at]] * root_mass[col_at]
            for col_at in range(len(chosen))
        ]
        for row_at in range(len(chosen))
    ]
    rates, basis = jacobi_eigen(scaled)
    eigen_basis = [
        [root_mass[row_at] * basis[row_at][col_at] for col_at in range(len(chosen))]
        for row_at in range(len(chosen))
    ]
    return (
        np.array(node_list),
        np.array(weight_list),
        np.array(stiff_list),
        np.array(eigen_basis),
        np.array(rates),
    )


def interp_table(fine_nodes, coarse_nodes):
    coarse_count = len(coarse_nodes)
    columns = []
    for column in range(coarse_count):
        factors_list = [
            (fine_nodes - coarse_nodes[other_node])
            / (coarse_nodes[column] - coarse_nodes[other_node])
            for other_node in range(coarse_count)
            if other_node != column
        ]
        columns.append(np.prod(np.stack(factors_list), axis=0))
    return np.stack(columns, axis=1)

BF = jnp.bfloat16
F32 = jnp.float32
RING = ((-1, 0), (1, 0), (0, -1), (-1, -1), (1, -1), (0, 1), (-1, 1), (1, 1))
GROUPS = ((0, 2), (2, 5), (5, 8))
AHEAD = (-1, 1, 2, 0)
BLOCK_ROWS = (16,) * 8
WIDE_ROWS = (80, 80, 80, 64, 64, 80, 64, 64)
LOW_SIDE = ((-1, 0), (-1, -1), (-1, 1), (0, -1), (0, 1))
HIGH_SIDE = ((1, 0), (1, -1), (1, 1), (0, -1), (0, 1))
MESH = pl.DeviceIdType.MESH


def offsets(rows):
    return tuple(int(at) for at in np.concatenate([[0], np.cumsum(rows)]))


def blocks(matrix, count):
    return np.kron(np.eye(count), matrix)


def line_extension(points, elements, periodic):
    size = elements * points
    width = size if periodic else size + 4
    table = np.zeros((elements, points + 2, width))

    def column(at):
        if periodic:
            return at % size
        if at < 0:
            return {-2: size, -1: size + 1}[at]
        if at >= size:
            return {size: size + 2, size + 1: size + 3}[at]
        return at

    for element in range(elements):
        start = element * points
        table[element, 0, column(start - 2)] += 1
        for at in range(points):
            table[element, 1 + at, start + at] += 1
        table[element, 1, column(start - 1)] += 1
        table[element, points, column(start + points)] += 1
        table[element, points + 1, column(start + points + 1)] += 1
    return table.reshape(elements * (points + 2), width)


def line_weights(points, elements):
    position = np.arange(points * elements) % points
    return np.where((position == 0) | (position == points - 1), 0.5, 1.0)


def z_back(inner, points, elements):
    table = blocks(inner, elements)
    total = np.array(table)
    size = points * elements
    for element in range(elements):
        low, high = element * points, (element * points - 1) % size
        total[low] = table[low] + table[high]
        total[high] = total[low]
    return (total * line_weights(points, elements)[:, None]).T


RIGHT = (
    "az", "bz", "bzra", "jz", "kz7", "rp", "pz", "azm", "bzm", "rb", "rj", "rk3", "ra3", "bzrp", "cz", "s16", "rcj",
    "s64", "s32", "s256", "s80", "sl80", "s48", "sl48", "select",
)


def fitted(table, right):
    rows, columns = table.shape[-2:]
    more = ((0, -rows % 128 if right else 0), (0, -columns % 128))
    return np.pad(table, ((0, 0),) * (table.ndim - 2) + more)


def side_by_side(*parts):
    return np.concatenate([np.pad(part, ((0, 0), (0, -part.shape[1] % 128))) for part in parts], 1)


def corner_columns(inner_table, elements):
    points = inner_table.shape[0]
    table = np.zeros((elements * points, 256))
    for corner in range(2):
        for lane in range(128):
            element = (lane % elements - corner) % elements
            table[element * points : (element + 1) * points, corner * 128 + lane] = inner_table[:, corner]
    return table


def build_tables(n_gy, ez):
    p, q = ORDER + 1, MID_ORDER + 1
    fine, mid, low = gll_tables(ORDER), gll_tables(MID_ORDER), gll_tables(1)
    jf = interp_table(fine[0], mid[0])
    jm = interp_table(mid[0], low[0])
    k7, w7, s7, l7 = fine[2], np.diag(fine[1]), fine[3], fine[4]
    k3, w3, s3, l3 = mid[2], np.diag(mid[1]), mid[3], mid[4]
    pair, plain = {}, {}
    modes = p + 2
    pair["az"] = (blocks(s7.T, ez) @ line_extension(p, ez, True)).T
    inner = s7[1:-1]
    bz = z_back(inner, p, ez)
    pair["bz"] = bz

    count = 4 * modes
    ext = np.zeros((4, modes, 36))
    for element in range(4):
        start = 2 + p * element
        ext[element, 0, start - 2] += 1
        for at in range(p):
            ext[element, 1 + at, start + at] += 1
        ext[element, 1, start - 1] += 1
        ext[element, p, start + p] += 1
        ext[element, p + 1, start + p + 1] += 1
    a1w = blocks(s7.T, 4) @ ext.reshape(count, 36)
    middle = a1w[:, 10:26]
    beside = {-1: a1w[:, 0:10], 1: a1w[:, 26:36]}
    for name, group, rows in (("vl", LOW_SIDE, slice(0, 2 * modes)), ("vr", HIGH_SIDE, slice(2 * modes, None))):
        parts = []
        for half in range(2):
            for dx, dy in group:
                pieces = []
                for at in range(half, 10, 2):
                    if dy == 0:
                        pieces.append(np.kron(beside[dx][rows, at : at + 1], middle))
                    elif dx == 0:
                        pieces.append(np.kron(middle[rows], beside[dy][:, at : at + 1]))
                    else:
                        pieces.append(np.kron(beside[dx][rows], beside[dy][:, at : at + 1]))
                piece = np.concatenate(pieces, 1)
                parts.append(np.pad(piece, ((0, 0), (0, -piece.shape[1] % 16))))
        plain[name] = (np.concatenate(parts, 1), BF)
    pair["vo"] = np.kron(middle, middle)
    raw = blocks(inner, 4)
    around = np.array(raw[p : 3 * p])
    for at in (p - 1, 2 * p - 1, 3 * p - 1):
        for row in (at, at + 1):
            if p <= row < 3 * p:
                around[row - p] = raw[at] + raw[at + 1]
    pair["vb"] = np.kron(around, around)

    def weights(points):
        line = line_weights(points, 2)
        low_side, high_side = np.zeros(2 * points), np.zeros(2 * points)
        low_side[0], high_side[-1] = 0.5, 0.5
        return np.stack([np.kron(line, line), np.kron(line, low_side), np.kron(line, high_side)], 1)

    wt7, wt3 = weights(p), weights(q)
    columns = np.zeros((256, 128))
    columns[:, 0:3] = wt7
    columns[:64, 6:9] = wt3
    columns[:, 9] = np.kron(np.tile(fine[1], 2), np.tile(fine[1], 2))
    plain["columns"] = (columns, F32)

    def three(stiff, mass, count):
        stiff, mass = blocks(stiff, count), blocks(mass, count)
        return np.kron(stiff, mass), np.kron(mass, stiff), np.kron(mass, mass)

    la = np.concatenate(three(jf.T @ k7, jf.T @ w7, 2), 0)
    ra = side_by_side(blocks(w7 @ jf, ez), blocks(k7 @ jf, ez))
    pair["la"] = la
    pair["bzra"] = bz @ ra
    pair["jxy"] = np.kron(blocks(jf.T, 2), blocks(jf.T, 2))
    pair["jz"] = blocks(jf, ez)
    k7x, k7y, _ = three(k7, w7, 2)
    pair["k7"] = np.concatenate([k7x, k7y], 0)
    pair["kz7"] = blocks(k7, ez)
    plain["wz7"] = (np.tile(np.tile(fine[1], ez)[None], (8, 1)), F32)
    pair["lp"] = np.concatenate(three(k7 @ jf, w7 @ jf, 2), 0)
    pair["rp"] = side_by_side(blocks((w7 @ jf).T, ez), blocks((k7 @ jf).T, ez))
    pair["bzrp"] = z_back(s3[1:-1], q, ez) @ pair["rp"]
    pair["pxy"] = np.kron(blocks(jf, 2), blocks(jf, 2))
    pair["pz"] = blocks(jf.T, ez)

    def factor_rows(elements, scale):
        table = np.zeros((len(elements), 16))
        for at, (ex, ey) in enumerate(elements):
            for d in range(3):
                if scale[d] is not None:
                    table[at, d * 4 + ex * 2 + ey] = scale[d][at]
        return table

    def grid_elements(per):
        return [(x // per, y // per) for x in range(2 * per) for y in range(2 * per)]

    def direction_rows(elements):
        one = np.ones(len(elements))
        return np.concatenate([factor_rows(elements, [one if d == e else None for e in range(3)]) for d in range(3)], 0)

    spread = lambda per: np.kron(np.eye(ez), np.ones((1, per)))
    plain["e7"] = (direction_rows(grid_elements(p)), BF)
    plain["e3"] = (direction_rows(grid_elements(q)), BF)
    plain["e1"] = (direction_rows(grid_elements(2)), BF)
    plain["s64"] = (spread(p), BF)
    plain["s32"] = (spread(q), BF)
    plain["s256"] = (corner_columns(np.ones((1, 2)), ez), BF)
    plain["s80"] = (spread(modes), BF)
    pair["sl80"] = spread(modes) * np.tile(l7, ez)[None]

    m3 = q + 2
    ext = np.zeros((4, m3, 6 * q))
    for element in range(4):
        start = q * (element + 1)
        ext[element, 0, start - 2] += 1
        for at in range(q):
            ext[element, 1 + at, start + at] += 1
        ext[element, 1, start - 1] += 1
        ext[element, q, start + q] += 1
        ext[element, q + 1, start + q + 1] += 1
    a1m = blocks(s3.T, 4) @ ext.reshape(4 * m3, 6 * q)
    order = RING + ((0, 0),)
    span = lambda d: slice((d + 1) * 2 * q, (d + 2) * 2 * q)
    wm = [np.kron(a1m[:, span(dx)], a1m[:, span(dy)]) for dx, dy in order]
    pair["wmn"] = np.concatenate(wm[:8], 1)
    pair["wmo"] = wm[8]
    pair["azm"] = (blocks(s3.T, ez) @ line_extension(q, ez, True)).T
    inner3 = s3[1:-1]
    raw3 = blocks(inner3, 4)
    back3 = np.array(raw3[q : 3 * q])
    for at in (q - 1, 2 * q - 1, 3 * q - 1):
        total = raw3[at] + raw3[at + 1]
        for row in (at, at + 1):
            if q <= row < 3 * q:
                back3[row - q] = total
    bm = np.kron(back3, back3)
    pair["bm"] = bm
    bzm = z_back(inner3, q, ez)
    pair["bzm"] = bzm
    ll = np.concatenate(three(jm.T @ k3, jm.T @ w3, 2), 0)
    pair["lb"] = np.concatenate([ll @ ((wt3[:, 0] + extra)[:, None] * bm) for extra in (0, wt3[:, 1], wt3[:, 2])], 0)
    pair["rb"] = bzm @ np.concatenate([corner_columns(w3 @ jm, ez), corner_columns(k3 @ jm, ez)], 1)
    pair["jl"] = np.kron(blocks(jm.T, 2), blocks(jm.T, 2))
    pair["rj"] = corner_columns(jm, ez)
    place = {direction: at for at, direction in enumerate(order)}

    def ring_row(ex, ey, d):
        dx, dy = ex // 2 - 1, ey // 2 - 1
        return place[(dx, dy)] * 16 + d * 4 + (ex % 2) * 2 + ey % 2

    ld3, le3 = np.zeros((576, 144)), np.zeros((576, 144))
    for x in range(24):
        for y in range(24):
            ex, ey = x // m3 + 1, y // m3 + 1
            ld3[x * 24 + y, ring_row(ex, ey, 0)] = l3[x % m3]
            ld3[x * 24 + y, ring_row(ex, ey, 1)] = l3[y % m3]
            le3[x * 24 + y, ring_row(ex, ey, 2)] = 1
    ld9, le9 = np.zeros((count * count, 144)), np.zeros((count * count, 144))
    for x in range(count):
        for y in range(count):
            ex, ey = x // modes + 1, y // modes + 1
            ld9[x * count + y, ring_row(ex, ey, 0)] = l7[x % modes]
            ld9[x * count + y, ring_row(ex, ey, 1)] = l7[y % modes]
            le9[x * count + y, ring_row(ex, ey, 2)] = 1
    pair["ld9"] = ld9
    plain["le9"] = (le9, BF)
    pair["ld3"] = ld3
    plain["le3"] = (le3, BF)
    plain["s48"] = (spread(m3), BF)
    pair["sl48"] = spread(m3) * np.tile(l3, ez)[None]
    er = np.zeros((3, 9, 2 * q, 2 * q, 144))
    for at in range(9):
        for x in range(2 * q):
            for y in range(2 * q):
                for d in range(3):
                    er[d, at, x, y, at * 16 + d * 4 + (x // q) * 2 + y // q] = 1
    plain["er"] = (er.reshape(3 * 576, 144), BF)
    pair["k3"] = np.concatenate(three(k3, w3, 2), 0)
    pair["rk3"] = side_by_side(blocks(w3, ez), blocks(k3, ez))
    corner_line = lambda table: np.kron(np.eye(6), table)
    modes_of = [a1m @ corner_line(table) for table in (k3 @ jm, w3 @ jm)]
    pair["wl"] = np.concatenate(
        [np.kron(modes_of[left], modes_of[right]) for left, right in ((0, 1), (1, 0), (1, 1))], 1
    )
    pair["ra3"] = side_by_side(
        blocks((w3 @ jm).T, ez) @ pair["azm"], blocks((k3 @ jm).T, ez) @ pair["azm"]
    )
    spread_vertices, spread_factors = np.zeros((144, 128)), np.zeros((3, 144, 144))
    for row in range(144):
        (ex, cx), (ey, cy) = divmod(row // 12, 2), divmod(row % 12, 2)
        vx, vy = ex + cx, ey + cy
        column = (AHEAD.index(vx // 2 - 1) * 4 + vy // 2) * 8 + (vx % 2) * 2 + vy % 2
        spread_vertices[row, column] = 1
        for d in range(3):
            at = order.index((ex // 2 - 1, ey // 2 - 1))
            spread_factors[d, row, at * 16 + d * 4 + (ex % 2) * 2 + ey % 2] = 1
    plain["ev"] = (spread_vertices, BF)
    plain["ef"] = (spread_factors.reshape(432, 144), BF)
    corner_z = np.zeros((ez, 2 * ez))
    for element in range(ez):
        for at in range(2):
            corner_z[(element + at) % ez, 2 * element + at] = 1
    plain["cz"] = (np.tile(corner_z, (4, 1)), BF)
    plain["s16"] = (spread(2), BF)
    vertex_line = lambda table: np.array(
        [[table[at % q, v - at // q] if 0 <= v - at // q <= 1 else 0.0 for v in range(8)] for at in range(6 * q)]
    )
    plain1 = vertex_line(jm)

    def vertex_columns(left, right, dx, dy):
        table = np.zeros((64, 4, 4, 8))
        for iy in range(4):
            for ix, ahead in enumerate(AHEAD):
                for x in range(2):
                    for y in range(2):
                        table[:, ix, iy, x * 2 + y] = np.kron(
                            left[span(dx), (ahead + 1) * 2 + x], right[span(dy), iy * 2 + y]
                        )
        return table.reshape(64, 128)

    pair["jc"] = vertex_columns(plain1, plain1, 0, 0)

    def z_vertices(table):
        result = np.zeros((ez, ez * q))
        for element in range(ez):
            for at in range(q):
                result[element, element * q + at] += table[at, 0]
                result[(element + 1) % ez, element * q + at] += table[at, 1]
        return np.tile(result, (4, 1))

    pair["rcj"] = z_vertices(jm)
    mask, left = np.zeros((n_gy, 16, 128)), np.zeros((n_gy, 16, 16))
    for gy in range(n_gy):
        for row in range(16):
            vx, vy = row // 8 + row // 4 % 2, row // 2 % 2 + row % 2
            owner = gy + vy // 2
            if owner < n_gy:
                first = owner * 32 + (vx % 2) * 16 + (vy % 2) * 8
                mask[gy, row, first % 128 : first % 128 + 8] = 1
                left[gy, first // 128 + 4 * (vx // 2), row] = 1
    plain["mask"] = (mask.reshape(-1, 128), F32)
    plain["left"] = (left.reshape(-1, 16), BF)
    chosen = np.zeros((8, 32))
    select = np.zeros((32, 8))
    for lane in range(32):
        chosen[lane // 8, lane] = 1
        select[lane, lane % 8] = 1
    plain["chosen"] = (chosen, F32)
    plain["select"] = (select, BF)
    tables = {}
    for name, table in pair.items():
        table = fitted(np.asarray(table, np.float64), name in RIGHT)
        high = table.astype(ml_dtypes.bfloat16)
        rest = (table - high.astype(np.float64)).astype(ml_dtypes.bfloat16)
        if name in RIGHT:
            tables[name] = np.block([[high, rest], [high, np.zeros_like(rest)]])[None]
        else:
            tables[name] = np.stack([high, rest])
    for name, (table, kind) in plain.items():
        table = fitted(np.asarray(table), name in RIGHT)
        table = np.concatenate([table, table], 0) if name in RIGHT else table
        tables[name] = table.astype(ml_dtypes.bfloat16 if kind is BF else np.float32)[None]
    return tables


STAGES = (
    ("columns", "vo", "jxy", "jz", "s80", "sl80", "e7", "e3", "e1", "s64", "s32", "s256", "wz7", "chosen", "mask"),
    ("ld9", "le9", "vl", "vr", "az", "vb", "la", "bzra"),
    ("ld3", "le3", "s48", "sl48", "er"),
    (
        "wmo", "jl", "rj", "bz", "k7", "kz7", "wmn", "azm", "lb", "rb", "left", "bm", "bzm", "select",
        "rk3", "k3", "wl", "ra3", "ev", "ef", "cz", "s16", "jc", "rcj", "rp", "bzrp", "lp", "pxy", "pz",
    ),
)


def pack(tables):
    stacks, places = {}, {}
    for stage, names in enumerate(STAGES):
        for name in names:
            table = tables[name]
            key = (stage, table.dtype.name, table.shape[-1])
            parts = stacks.setdefault(key, [])
            at = sum(part.shape[0] for part in parts)
            height = -(-table.shape[1] // 16) * 16
            for part in table:
                parts.append(np.pad(part, ((0, height - part.shape[0]), (0, 0))))
            places[name] = (key, at, height, table.shape[1])
    keys = tuple(stacks)
    return keys, [np.concatenate(stacks[key], 0) for key in keys], places


class Table:
    def __init__(self, ref, place):
        _, self.at, self.height, self.rows = place
        self.ref = ref
        self.shape = (2, self.rows, ref.shape[-1])

    def __getitem__(self, part):
        part = 0 if part is Ellipsis else part
        return self.ref[self.at + part * self.height : self.at + part * self.height + self.rows, :]

    def piece(self, part, start, rows):
        return self.ref[pl.ds(self.at + part * self.height + start, rows), :]


def dot(a, b):
    return jnp.dot(a, b, preferred_element_type=F32)


def split(x):
    high = x.astype(BF)
    return high, (x - high.astype(F32)).astype(BF)


def wide(x, lanes=128):
    if x.shape[1] == lanes:
        return x
    return jnp.concatenate([x, jnp.zeros((x.shape[0], lanes - x.shape[1]), x.dtype)], 1)


def tall(x, rows):
    if x.shape[0] == rows:
        return x
    return jnp.concatenate([x, jnp.zeros((rows - x.shape[0], x.shape[1]), x.dtype)], 0)


def halves(x):
    middle = x.shape[1] // 2
    return x[:, :middle] + x[:, middle:]


def exactly(main, small, x):
    high, rest = split(x)
    return halves(dot(main, jnp.concatenate([high, rest], 1))) + dot(small, high)


def left3(table, x):
    return exactly(table[0], table[1], tall(x, table.shape[-1]))


def left2(table, x):
    return halves(dot(table[...], jnp.concatenate(split(tall(x, table.shape[-1])), 1)))


def terms3(table, x):
    x = tall(x, table.shape[-1])
    rows = table.shape[1] // 3
    first = exactly(table.piece(0, 0, 2 * rows), table.piece(1, 0, 2 * rows), x[:, 0:128])
    third = exactly(table.piece(0, 2 * rows, rows), table.piece(1, 2 * rows, rows), x[:, 128:256])
    return first[0:rows], first[rows:], third


def right3(x, table):
    return halves(right2(x, table))


def right2(x, table):
    return dot(jnp.concatenate(split(wide(x)), 1), table[...])


KEPT = {
    "fine_f": (768, 128), "mid_f": (192, 128), "low_f": (48, 256), "ring_f": (1728, 128), "inverse3": (576, 128), "wt7": (256, 128), "wt3": (64, 128), "base_mid": (64, 128),
    "base_low": (16, 256), "first_fine": (256, 128), "base_fine": (256, 128),
    "first_mid": (64, 128), "modal3": (576, 128), "base_ring": (576, 128),
    "ww7": (256, 128), "inverse9": (1600, 128), "corner_f": (432, 128), "modal9": (1600, 128),
}


def cycle_kernel(keys, places, n_gx, n_gy, *refs):
    r_hbm, len_hbm, inv_hbm = refs[:3]
    count = len(keys)
    packed = refs[3 : 3 + count]
    out_fine, out_mid, out_low = refs[3 + count : 6 + count]
    stores = refs[6 + count : 6 + 2 * count]
    (
        r_ref, len_ref, inv_ref, rs, fs, hb1, rm, fm, rp, fp, hb2, hs1, hs2, corner, held, gs, gb, cb, invs,
        send_sem, recv_sem, gsend, grecv, csend, crecv, isend, irecv, in_sem, table_sem,
    ) = refs[6 + 2 * count : -len(KEPT)]
    gx, gy = lax.axis_index("gx"), lax.axis_index("gy")
    last = n_gy - 1
    barrier = pltpu.get_barrier_semaphore()

    def greet(ahead, row):
        pl.semaphore_signal(
            barrier, inc=1, device_id=(lax.rem(gx + (ahead + n_gx), n_gx), row), device_id_type=MESH
        )

    def greet_if(row, *columns):
        @pl.when((row >= 0) & (row <= last))
        def _():
            for ahead in columns:
                greet(ahead, row)

    greet_if(gy + 1, 0, 1, -1)
    greet_if(gy - 1, 0, 1, -1)
    greet(1, gy)
    greet(-1, gy)
    greet(2, gy)
    for row in range(n_gy):
        @pl.when((row < gy - 1) | (row > gy + 1))
        def _():
            greet(0, row)
            greet(-1, row)
    inputs = [
        pltpu.make_async_copy(source, target, in_sem.at[at])
        for at, (source, target) in enumerate(((len_hbm, len_ref), (r_hbm, r_ref), (inv_hbm, inv_ref)))
    ]
    loads = [pltpu.make_async_copy(packed[at], stores[at], table_sem.at[at]) for at in range(count)]
    for load in inputs:
        load.start()

    def fetch(*stages):
        for key, load in zip(keys, loads):
            if key[0] in stages:
                load.start()

    fetch(0)

    def ready(stage):
        for key, load in zip(keys, loads):
            if key[0] == stage:
                load.wait()

    kept = dict(zip(KEPT, refs[-len(KEPT) :]))

    def keep(name, value):
        kept[name][...] = value
        return kept[name]

    t = {name: Table(stores[keys.index(place[0])], place) for name, place in places.items()}
    at_bottom, at_top = gy == 0, gy == last
    not_bottom, not_top = gy > 0, gy < last
    sent = {0: None, 1: not_bottom, 2: not_top}

    def guarded(condition, action):
        if condition is None:
            action()
        else:
            pl.when(condition)(action)

    def exchange(phase, source, buffer, rows):
        at = offsets(rows)

        def group(number):
            def action():
                for index in range(*GROUPS[number]):
                    tx, ty = RING[index]
                    slot = RING.index((-tx, -ty))
                    landing = (0, 2, 1)[number]
                    pltpu.make_async_remote_copy(
                        src_ref=source(index),
                        dst_ref=buffer.at[pl.ds(at[slot], rows[slot])],
                        send_sem=send_sem.at[phase, number],
                        recv_sem=recv_sem.at[phase, landing],
                        device_id=(lax.rem(gx + (tx + n_gx), n_gx), gy + ty),
                        device_id_type=MESH,
                    ).start()

            return action

        for number in (1, 2, 0):
            guarded(sent[number], group(number))

    def settle(phase, sems, buffer, rows):
        at = offsets(rows)
        for number in range(3):
            first, end = GROUPS[number]
            piece = buffer.at[pl.ds(at[first], at[end] - at[first])]
            guarded(sent[number], lambda: pltpu.make_async_copy(piece, piece, sems.at[phase, number]).wait())

    def clear(number):
        first, end = GROUPS[number]
        for buffer, rows in (
            (fs, BLOCK_ROWS), (hb1, WIDE_ROWS), (rp, BLOCK_ROWS), (fp, BLOCK_ROWS), (hb2, WIDE_ROWS),
        ):
            at = offsets(rows)
            buffer[at[first] : at[end], :] = jnp.zeros((at[end] - at[first], buffer.shape[1]), buffer.dtype)

    @pl.when(at_bottom)
    def _():
        clear(1)
        invs[0:32, :] = jnp.zeros((32, invs.shape[1]), BF)

    @pl.when(at_top)
    def _():
        clear(2)
        invs[64:96, :] = jnp.zeros((32, invs.shape[1]), BF)

    @pl.when(gy >= last - 1)
    def _():
        invs[96:128, :] = jnp.zeros((32, invs.shape[1]), BF)

    at_wide = offsets(WIDE_ROWS)

    def wide_halo(field, stage):
        for index, (tx, ty) in enumerate(RING):
            xs, ys = (6, 0)[tx < 0], (6, 0)[ty < 0]
            if 0 not in (tx, ty):
                corner[48:64, :] = jnp.zeros((16, 128), F32)
            for pair in range(5):
                xa, ya = xs + 2 * pair, ys + 2 * pair
                at = at_wide[index] + pair * 16
                if ty == 0:
                    layers = field[xa, :, :], field[xa + 1, :, :]
                    stage[at : at + 16, :] = jnp.concatenate(layers, 1).astype(stage.dtype)
                elif tx == 0:
                    layers = field[:, ya, :], field[:, ya + 1, :]
                    stage[at : at + 16, :] = jnp.concatenate(layers, 1).astype(stage.dtype)
                else:
                    layers = field[xs : xs + 10, ya, :], field[xs : xs + 10, ya + 1, :]
                    corner[pair * 10 : pair * 10 + 10, :] = jnp.concatenate(layers, 1)
            if 0 not in (tx, ty):
                stage[at_wide[index] : at_wide[index + 1], :] = corner[...].astype(stage.dtype)

    def side_values(buffer, group):
        pieces = []
        for direction in group:
            index = RING.index(direction)
            pieces.append(buffer[at_wide[index] : at_wide[index + 1], :])
        turned_back = [pltpu.roll(piece.astype(F32), 64, 1).astype(BF) for piece in pieces]
        return tall(jnp.concatenate(pieces + turned_back, 0), 768)

    def fold(block):
        result = block[0:16]
        for part in range(1, 4):
            result = result + pltpu.roll(block[part * 16 : part * 16 + 16], part * 32, 1)
        return result

    def spread_blocks(folded, blocks_ref):
        for part in range(4):
            turned_back = pltpu.roll(folded[0:128, :], (128 - part * 32) % 128, 1) if part else folded[0:128, :]
            for slot in range(8):
                blocks_ref[slot * 64 + part * 16 : slot * 64 + part * 16 + 16, :] = turned_back[
                    slot * 16 : slot * 16 + 16
                ]


    inputs[0].wait()
    own_f = 8 * 16
    for ex in range(2):
        a, b, c = len_ref[0, ex], len_ref[1, ex], len_ref[2, ex]
        fs[own_f + ex * 2 : own_f + ex * 2 + 2, :] = wide(b * c / (2.0 * a))
        fs[own_f + 4 + ex * 2 : own_f + 6 + ex * 2, :] = wide(a * c / (2.0 * b))
        fs[own_f + 8 + ex * 2 : own_f + 10 + ex * 2, :] = wide(a * b / (2.0 * c))
    fs[own_f + 12 : own_f + 16, :] = jnp.zeros((4, 128), F32)
    inputs[1].wait()
    wide_halo(r_ref, hs1)
    near = jnp.minimum(gy + 1, last) - jnp.maximum(gy - 1, 0) + 1
    pl.semaphore_wait(barrier, 2 * n_gy + near)
    exchange(0, lambda index: fs.at[pl.ds(own_f, 16)], fs, BLOCK_ROWS)
    exchange(1, lambda index: hs1.at[pl.ds(at_wide[index], WIDE_ROWS[index])], hb1, WIDE_ROWS)
    fetch(1, 2)
    inputs[2].wait()
    invs[32:64, :] = inv_ref[0]
    reach = ((1, 0, not_top, not_bottom), (-1, 2, not_bottom, not_top), (-2, 3, gy > 1, gy < last - 1))

    def inverse_copy(at):
        step, slot, _, _ = reach[at]
        return pltpu.make_async_remote_copy(
            src_ref=invs.at[pl.ds(32, 32)],
            dst_ref=invs.at[pl.ds(slot * 32, 32)],
            send_sem=isend.at[at],
            recv_sem=irecv.at[at],
            device_id=(gx, gy + step),
            device_id_type=MESH,
        )

    for at in range(3):
        pl.when(reach[at][2])(lambda: inverse_copy(at).start())

    bottom_on = jnp.where(at_bottom, 1.0, 0.0)
    top_on = jnp.where(at_top, 1.0, 0.0)

    ready(0)
    columns = t["columns"][...]

    def wall_weight(rows, at):
        piece = columns[0:rows]
        return piece[:, at : at + 1] + bottom_on * piece[:, at + 1 : at + 2] + top_on * piece[:, at + 2 : at + 3]

    wt7 = keep("wt7", jnp.broadcast_to(wall_weight(256, 0), (256, 128)))
    wt3 = keep("wt3", jnp.broadcast_to(wall_weight(64, 6), (64, 128)))
    ww7 = keep("ww7", jnp.broadcast_to(columns[:, 9:10], (256, 128)))
    r = wide(r_ref[...].reshape(256, 64))
    f_own = wide(fs[own_f : own_f + 16, :])
    modal9 = keep("modal9", left3(t["vo"], r))
    base_mid = keep("base_mid", right3(left3(t["jxy"], r), t["jz"]))
    fine_f = keep("fine_f", left2(t["e7"], right2(f_own, t["s64"])))
    mid_f = keep("mid_f", left2(t["e3"], right2(f_own, t["s32"])))
    low_f = keep("low_f", left2(t["e1"], right2(f_own, t["s256"])))

    def ring_modes(buffer):
        modal = jnp.concatenate(
            [
                modal9[0:800] + dot(t["vl"][...], side_values(buffer, LOW_SIDE)),
                modal9[800:1600] + dot(t["vr"][...], side_values(buffer, HIGH_SIDE)),
            ],
            0,
        )
        return right3(modal, t["az"]) * inverse9[...]

    ready(1)
    fetch(3)
    settle(0, recv_sem, fs, BLOCK_ROWS)
    ring_l = wide(fs[...])
    d9 = left3(t["ld9"], right2(ring_l, t["s80"])) + left2(t["le9"], right3(ring_l, t["sl80"]))
    inverse9 = keep("inverse9", jnp.where(d9 > 0.0, 1.0 / d9, 0.0))
    settle(1, recv_sem, hb1, WIDE_ROWS)
    local = left3(t["vb"], ring_modes(hb1)) * wt7[...]
    terms = terms3(t["la"], right3(local, t["bzra"]))
    residual_mid = base_mid[...] - (mid_f[0:64] * terms[0] + mid_f[64:128] * terms[1] + mid_f[128:192] * terms[2])
    rp[128:144, :] = fold(residual_mid)
    exchange(3, lambda index: rp.at[pl.ds(128, 16)], rp, BLOCK_ROWS)
    rm[512:576, :] = residual_mid

    ready(2)
    ready(3)
    ring_l = wide(fs[...])
    d3 = left3(t["ld3"], right2(ring_l, t["s48"])) + left2(t["le3"], right3(ring_l, t["sl48"]))
    inverse3 = keep("inverse3", jnp.where(d3 > 0.0, 1.0 / d3, 0.0))
    own_modal = keep("modal3", left3(t["wmo"], residual_mid))
    base_low = keep("base_low", right3(left3(t["jl"], residual_mid), t["rj"]))
    first_fine = keep("first_fine", right3(local, t["bz"]))
    massed = left3(t["k7"], first_fine[...] * t["wz7"][...][0:1])
    along_z = right3(first_fine[...], t["kz7"]) * ww7[...]
    base_fine = keep(
        "base_fine",
        wide(r_ref[...].reshape(256, 64))
        - (fine_f[0:256] * massed[0:256] + fine_f[256:512] * massed[256:512] + fine_f[512:768] * along_z),
    )

    settle(3, recv_sem, rp, BLOCK_ROWS)
    spread_blocks(rp, rm)
    modal3 = own_modal[...] + left3(t["wmn"], rm[0:512, :])
    modal3 = right3(modal3, t["azm"]) * inverse3[...]
    variant = jnp.where(at_bottom, 1, jnp.where(at_top, 2, 0))
    rows = pl.multiple_of(variant * 48, 16)
    low = exactly(t["lb"].piece(0, rows, 48), t["lb"].piece(1, rows, 48), tall(modal3, t["lb"].shape[-1]))
    low = right3(low, t["rb"])
    low = base_low[...] - (
        low_f[0:16] * low[0:16, 0:256] + low_f[16:32] * low[16:32, 0:256] + low_f[32:48] * low[32:48, 256:512]
    )
    wall = pl.multiple_of(gy * 16, 16)
    low = tall(halves(low) * t["mask"].piece(0, wall, 16), 128)
    message = halves(dot(t["left"].piece(0, wall, 16), jnp.concatenate(split(low), 1)))[0:8]
    gs[...] = message

    def send_slab(flips, ahead):
        row = gy
        for bit in (8, 4, 2, 1):
            if flips & bit:
                row = row + bit * (1 - 2 * (gy // bit % 2))
        pltpu.make_async_remote_copy(
            src_ref=gs,
            dst_ref=gb.at[flips + (n_gy - 1 if ahead else -1)],
            send_sem=gsend,
            recv_sem=grecv,
            device_id=(lax.rem(gx + ahead, n_gx), row),
            device_id_type=MESH,
        ).start()

    for flips in (12, 13, 10, 11, 14, 15, 8, 9, 4, 5, 2, 3, 6, 7, 1, 0):
        if flips < n_gy:
            send_slab(flips, 1)
            if flips:
                send_slab(flips, 0)

    first_mid = keep("first_mid", right3(left3(t["bm"], modal3) * wt3[...], t["bzm"]))
    fm[512:576, :] = first_mid[...]
    fp[128:144, :] = fold(first_mid[...])
    exchange(4, lambda index: fp.at[pl.ds(128, 16)], fp, BLOCK_ROWS)

    for at in range(3):
        pl.when(reach[at][3])(lambda: inverse_copy(at).wait_recv())
    pltpu.make_async_copy(gb, gb, grecv).wait()
    here = gs[...] + jnp.sum(gb[0 : n_gy - 1], axis=0)
    behind = jnp.sum(gb[n_gy - 1 :], axis=0)
    chunks = inv_ref.shape[2] // 128
    vector = here + pltpu.roll(behind, 4, 0)
    row = lax.broadcasted_iota(jnp.int32, (8, 128), 0)
    vector = jnp.concatenate([jnp.where(row == chunk, vector, 0.0) for chunk in range(chunks)], 1)
    vector = tall(vector, 16).astype(BF)
    solved = lax.dot_general(vector, invs[...], (((1,), (1,)), ((), ())), preferred_element_type=F32)
    solved = jnp.broadcast_to(jnp.sum(solved, axis=0, keepdims=True), (8, 128))
    chosen = t["chosen"][...]
    for iy in range(4):
        cb[96 + iy * 8 : 104 + iy * 8, :] = (pltpu.roll(solved, 128 - iy * 32, 1) if iy else solved) * chosen
    for ix in (2, 1, 0):
        pltpu.make_async_remote_copy(
            src_ref=cb.at[pl.ds(96, 32)],
            dst_ref=cb.at[pl.ds(ix * 32, 32)],
            send_sem=csend,
            recv_sem=crecv,
            device_id=(lax.rem(gx - AHEAD[ix] + n_gx, n_gx), gy),
            device_id_type=MESH,
        ).start()

    others = cb.at[pl.ds(0, 96)]

    ring_l = wide(fs[...])
    ring_f = keep("ring_f", left2(t["er"], right2(ring_l, t["s32"])))
    corner_f = keep("corner_f", left2(t["ef"], right2(ring_l, t["s16"])))
    low_out = right2(tall(cb[104:112, :], 16), t["select"])
    out_low[0] = low_out[0:2, 0:8]
    out_low[1] = low_out[2:4, 0:8]
    settle(4, recv_sem, fp, BLOCK_ROWS)
    spread_blocks(fp, fm)
    turned = right3(fm[...], t["rk3"])
    parts = []
    for at in range(9):
        piece = terms3(t["k3"], turned[at * 64 : (at + 1) * 64])
        parts.append(
            rm[at * 64 : (at + 1) * 64, :]
            - (
                ring_f[at * 64 : (at + 1) * 64] * piece[0]
                + ring_f[576 + at * 64 : 576 + (at + 1) * 64] * piece[1]
                + ring_f[1152 + at * 64 : 1152 + (at + 1) * 64] * piece[2]
            )
        )
    base_ring = keep("base_ring", jnp.concatenate(parts, 0))
    modal3 = left3(t["wmn"], base_ring[0:512]) + left3(t["wmo"], base_ring[512:576])
    modal3 = keep("modal3", right3(modal3, t["azm"]))

    pltpu.make_async_copy(others, others, crecv).wait()
    corrections = wide(cb[...])
    change = left2(t["ev"], right2(corrections, t["cz"]))
    change = right3(jnp.concatenate([change * corner_f[at * 144 : at * 144 + 144] for at in range(3)], 0), t["ra3"])
    change = jnp.concatenate([change[0:288, 0:128], change[288:432, 128:256]], 0)
    modal3 = (modal3[...] - left3(t["wl"], change)) * inverse3[...]
    held[0:64, :] = first_mid[...] + right3(left3(t["jc"], corrections), t["rcj"])
    smoothed = left3(t["bm"], modal3) * wt3[...]

    turned = terms3(t["lp"], right3(smoothed, t["bzrp"]) + right3(held[0:64, :], t["rp"]))
    residual = base_fine[...] - (
        fine_f[0:256] * turned[0]
        + fine_f[256:512] * turned[1]
        + fine_f[512:768] * turned[2]
    )
    rs[...] = residual[:, 0:64].reshape(16, 16, 64)
    wide_halo(rs, hs2)
    exchange(5, lambda index: hs2.at[pl.ds(at_wide[index], WIDE_ROWS[index])], hb2, WIDE_ROWS)
    mid_result = held[0:64, :] + right3(smoothed, t["bzm"])
    out_mid[...] = mid_result[:, 0:32].reshape(8, 8, 32)
    modal9 = keep("modal9", dot(t["vo"][0], residual.astype(BF)))
    held[...] = first_fine[...] + right3(left3(t["pxy"], mid_result), t["pz"])
    settle(5, recv_sem, hb2, WIDE_ROWS)
    local = dot(t["vb"][0], tall(ring_modes(hb2), 1664).astype(BF)) * wt7[...]
    result = held[...] + right3(local, t["bz"])
    out_fine[...] = result[:, 0:64].reshape(16, 16, 64)

    for phase, buffer, rows in (
        (0, fs, BLOCK_ROWS), (1, hb1, WIDE_ROWS), (3, rp, BLOCK_ROWS), (4, fp, BLOCK_ROWS), (5, hb2, WIDE_ROWS),
    ):
        settle(phase, send_sem, buffer, rows)
    pltpu.make_async_copy(gb, gb, gsend).wait()
    pltpu.make_async_copy(others, others, csend).wait()
    for at in range(3):
        pl.when(reach[at][2])(lambda: inverse_copy(at).wait_send())


def hand_over(*refs):
    copies = [pltpu.make_async_copy(refs[at], refs[3 + at], refs[6].at[at]) for at in range(3)]
    for copy in copies:
        copy.start()
    for copy in copies:
        copy.wait()


def shards(n_gx, n_gy, local_residual, lengths, coarse_inverse):
    keys, packed, places = pack(build_tables(n_gy, lengths.shape[3]))
    vmem = pl.BlockSpec(memory_space=pltpu.VMEM)
    scratch = [pltpu.VMEM(table.shape, BF if key[1] == "bfloat16" else F32) for key, table in zip(keys, packed)]
    scratch += [
        pltpu.VMEM(local_residual.shape, F32),
        pltpu.VMEM(lengths.shape, F32),
        pltpu.VMEM(coarse_inverse.shape, BF),
        pltpu.VMEM((16, 16, 64), F32),
        pltpu.VMEM((144, 128), F32),
        pltpu.VMEM((576, 128), BF),
        pltpu.VMEM((576, 128), F32),
        pltpu.VMEM((576, 128), F32),
        pltpu.VMEM((144, 128), F32),
        pltpu.VMEM((144, 128), F32),
        pltpu.VMEM((576, 128), BF),
        pltpu.VMEM((576, 128), BF),
        pltpu.VMEM((576, 128), BF),
        pltpu.VMEM((64, 128), F32),
        pltpu.VMEM((256, 128), F32),
        pltpu.VMEM((8, 128), F32),
        pltpu.VMEM((2 * n_gy - 1, 8, 128), F32),
        pltpu.VMEM((128, 128), F32),
        pltpu.VMEM((128, coarse_inverse.shape[2]), BF),
        pltpu.SemaphoreType.DMA((6, 3)),
        pltpu.SemaphoreType.DMA((6, 3)),
        pltpu.SemaphoreType.DMA,
        pltpu.SemaphoreType.DMA,
        pltpu.SemaphoreType.DMA,
        pltpu.SemaphoreType.DMA,
        pltpu.SemaphoreType.DMA((3,)),
        pltpu.SemaphoreType.DMA((3,)),
        pltpu.SemaphoreType.DMA((3,)),
        pltpu.SemaphoreType.DMA((len(keys),)),
    ]
    scratch += [pltpu.VMEM(shape, F32) for shape in KEPT.values()]
    outs = pl.pallas_call(
        functools.partial(cycle_kernel, keys, places, n_gx, n_gy),
        out_shape=(
            jax.ShapeDtypeStruct((16, 16, 64), F32),
            jax.ShapeDtypeStruct((8, 8, 32), F32),
            jax.ShapeDtypeStruct((2, 2, 8), F32),
        ),
        in_specs=[pl.BlockSpec(memory_space=pl.ANY)] * (3 + len(keys)),
        out_specs=(vmem, vmem, vmem),
        scratch_shapes=scratch,
        compiler_params=pltpu.CompilerParams(collective_id=0, has_side_effects=True, vmem_limit_bytes=60 * 1024 * 1024),
    )(local_residual, lengths, coarse_inverse, *[jnp.asarray(table) for table in packed])
    return pl.pallas_call(
        hand_over,
        out_shape=tuple(jax.ShapeDtypeStruct(out.shape, out.dtype) for out in outs),
        in_specs=[vmem] * 3,
        out_specs=[pl.BlockSpec(memory_space=pl.ANY)] * 3,
        scratch_shapes=[pltpu.SemaphoreType.DMA((3,))],
    )(*outs)


def solution(mesh):
    in_specs = (P("gx", "gy", None), P(None, "gx", "gy", None), P("gx", "gy", None))
    out_specs = (P("gx", "gy", None), P("gx", "gy", None), P("gx", "gy", None))
    return jax.shard_map(
        functools.partial(shards, mesh.shape["gx"], mesh.shape["gy"]),
        mesh=mesh,
        in_specs=in_specs,
        out_specs=out_specs,
        check_vma=False,
    )
```

```python
import functools
import math

import jax
import jax.numpy as jnp
import ml_dtypes
import numpy as np
from jax import lax
from jax.experimental import pallas as pl
from jax.experimental.pallas import tpu as pltpu
from jax.sharding import PartitionSpec as P

ORDER = 7
MID_ORDER = 3


def legendre_pair(order, point):
    older = 1.0
    newer = point
    for degree in range(2, order + 1):
        nexter = ((2 * degree - 1) * point * newer - (degree - 1) * older) / degree
        older = newer
        newer = nexter
    return (newer, older)


def jacobi_eigen(matrix):
    count_n = len(matrix)
    work = [list(row_items) for row_items in matrix]
    vectors = [
        [1.0 if row_at == col_at else 0.0 for col_at in range(count_n)] for row_at in range(count_n)
    ]
    for sweep_count in range(60):
        for lower_at in range(count_n):
            for upper_at in range(lower_at + 1, count_n):
                off_value = work[lower_at][upper_at]
                if abs(off_value) < 1e-18 * (
                    abs(work[lower_at][lower_at]) + abs(work[upper_at][upper_at])
                ):
                    continue
                angle_ratio = (work[upper_at][upper_at] - work[lower_at][lower_at]) / (
                    2.0 * off_value
                )
                sign_value = 1.0 if angle_ratio >= 0 else -1.0
                tangent = sign_value / (
                    abs(angle_ratio) + math.sqrt(angle_ratio * angle_ratio + 1.0)
                )
                cosine = 1.0 / math.sqrt(tangent * tangent + 1.0)
                sine_value = tangent * cosine
                for other_at in range(count_n):
                    left_value = work[other_at][lower_at]
                    right_value = work[other_at][upper_at]
                    work[other_at][lower_at] = cosine * left_value - sine_value * right_value
                    work[other_at][upper_at] = sine_value * left_value + cosine * right_value
                for other_at in range(count_n):
                    left_value = work[lower_at][other_at]
                    right_value = work[upper_at][other_at]
                    work[lower_at][other_at] = cosine * left_value - sine_value * right_value
                    work[upper_at][other_at] = sine_value * left_value + cosine * right_value
                for other_at in range(count_n):
                    left_value = vectors[other_at][lower_at]
                    right_value = vectors[other_at][upper_at]
                    vectors[other_at][lower_at] = cosine * left_value - sine_value * right_value
                    vectors[other_at][upper_at] = sine_value * left_value + cosine * right_value
    eigen_list = [work[row_at][row_at] for row_at in range(count_n)]
    ordering = sorted(range(count_n), key=lambda index_at: eigen_list[index_at])
    rates = [eigen_list[index_at] for index_at in ordering]
    basis = [[vectors[row_at][index_at] for index_at in ordering] for row_at in range(count_n)]
    return (rates, basis)


def gll_tables(order):
    point_count = order + 1
    node_list = []
    for node_at in range(point_count):
        point = math.cos(math.pi * node_at / order)
        for newton_step in range(100):
            top_value, lower_value = legendre_pair(order, point)
            point = point - (point * top_value - lower_value) / ((order + 1) * top_value)
        node_list.append(point)
    node_list = node_list[::-1]
    node_list[0] = -1.0
    node_list[-1] = 1.0
    values = [legendre_pair(order, point)[0] for point in node_list]
    weight_list = [2.0 / (order * (order + 1) * value_at**2) for value_at in values]
    derivative = [[0.0] * point_count for row_at in range(point_count)]
    for row_at in range(point_count):
        for col_at in range(point_count):
            if row_at != col_at:
                derivative[row_at][col_at] = values[row_at] / (
                    values[col_at] * (node_list[row_at] - node_list[col_at])
                )
    derivative[0][0] = -order * (order + 1) / 4.0
    derivative[order][order] = order * (order + 1) / 4.0
    stiff_list = [
        [
            sum(
                (
                    derivative[inner_at][row_at]
                    * weight_list[inner_at]
                    * derivative[inner_at][col_at]
                    for inner_at in range(point_count)
                )
            )
            for col_at in range(point_count)
        ]
        for row_at in range(point_count)
    ]
    extent = 3 * order + 1
    big_stiff = [[0.0] * extent for row_at in range(extent)]
    big_mass = [0.0] * extent
    for offset_at in (0, order, 2 * order):
        for row_at in range(point_count):
            big_mass[offset_at + row_at] += weight_list[row_at]
            for col_at in range(point_count):
                big_stiff[offset_at + row_at][offset_at + col_at] += stiff_list[row_at][col_at]
    chosen = list(range(order - 1, 2 * order + 2))
    root_mass = [1.0 / math.sqrt(big_mass[index_at]) for index_at in chosen]
    scaled = [
        [
            root_mass[row_at] * big_stiff[chosen[row_at]][chosen[col_at]] * root_mass[col_at]
            for col_at in range(len(chosen))
        ]
        for row_at in range(len(chosen))
    ]
    rates, basis = jacobi_eigen(scaled)
    eigen_basis = [
        [root_mass[row_at] * basis[row_at][col_at] for col_at in range(len(chosen))]
        for row_at in range(len(chosen))
    ]
    return (
        np.array(node_list),
        np.array(weight_list),
        np.array(stiff_list),
        np.array(eigen_basis),
        np.array(rates),
    )


def interp_table(fine_nodes, coarse_nodes):
    coarse_count = len(coarse_nodes)
    columns = []
    for column in range(coarse_count):
        factors_list = [
            (fine_nodes - coarse_nodes[other_node])
            / (coarse_nodes[column] - coarse_nodes[other_node])
            for other_node in range(coarse_count)
            if other_node != column
        ]
        columns.append(np.prod(np.stack(factors_list), axis=0))
    return np.stack(columns, axis=1)

BF = jnp.bfloat16
F32 = jnp.float32
RING = ((-1, 0), (1, 0), (0, -1), (-1, -1), (1, -1), (0, 1), (-1, 1), (1, 1))
GROUPS = ((0, 2), (2, 5), (5, 8))
AHEAD = (-1, 1, 2, 0)
BLOCK_ROWS = (16,) * 8
WIDE_ROWS = (80, 80, 80, 64, 64, 80, 64, 64)
LOW_SIDE = ((-1, 0), (-1, -1), (-1, 1), (0, -1), (0, 1))
MESH = pl.DeviceIdType.MESH


def offsets(rows):
    return tuple(int(at) for at in np.concatenate([[0], np.cumsum(rows)]))


def blocks(matrix, count):
    return np.kron(np.eye(count), matrix)


def line_extension(points, elements, periodic):
    size = elements * points
    width = size if periodic else size + 4
    table = np.zeros((elements, points + 2, width))

    def column(at):
        if periodic:
            return at % size
        if at < 0:
            return {-2: size, -1: size + 1}[at]
        if at >= size:
            return {size: size + 2, size + 1: size + 3}[at]
        return at

    for element in range(elements):
        start = element * points
        table[element, 0, column(start - 2)] += 1
        for at in range(points):
            table[element, 1 + at, start + at] += 1
        table[element, 1, column(start - 1)] += 1
        table[element, points, column(start + points)] += 1
        table[element, points + 1, column(start + points + 1)] += 1
    return table.reshape(elements * (points + 2), width)


def line_weights(points, elements):
    position = np.arange(points * elements) % points
    return np.where((position == 0) | (position == points - 1), 0.5, 1.0)


def z_back(inner, points, elements):
    table = blocks(inner, elements)
    total = np.array(table)
    size = points * elements
    for element in range(elements):
        low, high = element * points, (element * points - 1) % size
        total[low] = table[low] + table[high]
        total[high] = total[low]
    return (total * line_weights(points, elements)[:, None]).T


RIGHT = (
    "az", "bz", "bzra", "jz", "kz7", "rp", "pz", "azm", "bzm", "rb", "rj", "rk3", "ra3", "bzrp", "cz", "s16", "rcj",
    "s64", "s32", "s256", "s80", "sl80", "s48", "sl48", "select",
)


def fitted(table, right):
    rows, columns = table.shape[-2:]
    more = ((0, -rows % 128 if right else 0), (0, -columns % 128))
    return np.pad(table, ((0, 0),) * (table.ndim - 2) + more)


def side_by_side(*parts):
    return np.concatenate([np.pad(part, ((0, 0), (0, -part.shape[1] % 128))) for part in parts], 1)


def corner_columns(inner_table, elements):
    points = inner_table.shape[0]
    table = np.zeros((elements * points, 256))
    for corner in range(2):
        for lane in range(128):
            element = (lane % elements - corner) % elements
            table[element * points : (element + 1) * points, corner * 128 + lane] = inner_table[:, corner]
    return table


def build_tables(n_gy, ez):
    p, q = ORDER + 1, MID_ORDER + 1
    fine, mid, low = gll_tables(ORDER), gll_tables(MID_ORDER), gll_tables(1)
    jf = interp_table(fine[0], mid[0])
    jm = interp_table(mid[0], low[0])
    k7, w7, s7, l7 = fine[2], np.diag(fine[1]), fine[3], fine[4]
    k3, w3, s3, l3 = mid[2], np.diag(mid[1]), mid[3], mid[4]
    pair, plain = {}, {}
    modes = p + 2
    pair["az"] = (blocks(s7.T, ez) @ line_extension(p, ez, True)).T
    inner = s7[1:-1]
    bz = z_back(inner, p, ez)
    pair["bz"] = bz

    count = 4 * modes
    ext = np.zeros((4, modes, 36))
    for element in range(4):
        start = 2 + p * element
        ext[element, 0, start - 2] += 1
        for at in range(p):
            ext[element, 1 + at, start + at] += 1
        ext[element, 1, start - 1] += 1
        ext[element, p, start + p] += 1
        ext[element, p + 1, start + p + 1] += 1
    a1w = blocks(s7.T, 4) @ ext.reshape(count, 36)
    middle = a1w[:, 10:26]
    beside = {-1: a1w[:, 0:10], 1: a1w[:, 26:36]}
    near, parts = slice(0, 2 * modes), []
    for half in range(2):
        for dx, dy in LOW_SIDE:
            if dy == 0:
                pieces = [np.kron(beside[dx][near, at : at + 1], middle) for at in range(half, 10, 2)]
            elif dx == 0:
                columns = range(15, 7, -1) if half else range(8)
                pieces = [np.kron(middle[near][:, columns], beside[dy][:, at : at + 1]) for at in range(10)]
            else:
                pieces = [np.kron(beside[dx][near], beside[dy][:, at : at + 1]) for at in range(half, 10, 2)]
            piece = np.concatenate(pieces, 1)
            parts.append(np.pad(piece, ((0, 0), (0, -piece.shape[1] % 16))))
    plain["vl"] = (np.concatenate(parts, 1), BF)
    pair["vo"] = np.kron(middle[near], middle)
    raw = blocks(inner, 4)
    around = np.array(raw[p : 3 * p])
    for at in (p - 1, 2 * p - 1, 3 * p - 1):
        for row in (at, at + 1):
            if p <= row < 3 * p:
                around[row - p] = raw[at] + raw[at + 1]
    pair["vb"] = np.kron(around[:, near], around)

    def weights(points):
        line = line_weights(points, 2)
        low_side, high_side = np.zeros(2 * points), np.zeros(2 * points)
        low_side[0], high_side[-1] = 0.5, 0.5
        return np.stack([np.kron(line, line), np.kron(line, low_side), np.kron(line, high_side)], 1)

    wt7, wt3 = weights(p), weights(q)
    columns = np.zeros((256, 128))
    columns[:, 0:3] = wt7
    columns[:64, 6:9] = wt3
    columns[:, 9] = np.kron(np.tile(fine[1], 2), np.tile(fine[1], 2))
    plain["columns"] = (columns, F32)

    def three(stiff, mass, count):
        stiff, mass = blocks(stiff, count), blocks(mass, count)
        return np.kron(stiff, mass), np.kron(mass, stiff), np.kron(mass, mass)

    la = np.concatenate(three(jf.T @ k7, jf.T @ w7, 2), 0)
    ra = side_by_side(blocks(w7 @ jf, ez), blocks(k7 @ jf, ez))
    pair["la"] = la
    pair["bzra"] = bz @ ra
    pair["jxy"] = np.kron(blocks(jf.T, 2), blocks(jf.T, 2))
    pair["jz"] = blocks(jf, ez)
    k7x, k7y, _ = three(k7, w7, 2)
    pair["k7"] = np.concatenate([k7x, k7y], 0)
    pair["kz7"] = blocks(k7, ez)
    plain["wz7"] = (np.tile(np.tile(fine[1], ez)[None], (8, 1)), F32)
    pair["lp"] = np.concatenate(three(k7 @ jf, w7 @ jf, 2), 0)
    pair["rp"] = side_by_side(blocks((w7 @ jf).T, ez), blocks((k7 @ jf).T, ez))
    pair["bzrp"] = z_back(s3[1:-1], q, ez) @ pair["rp"]
    pair["pxy"] = np.kron(blocks(jf, 2), blocks(jf, 2))
    pair["pz"] = blocks(jf.T, ez)

    def factor_rows(elements, scale):
        table = np.zeros((len(elements), 16))
        for at, (ex, ey) in enumerate(elements):
            for d in range(3):
                if scale[d] is not None:
                    table[at, d * 4 + ex * 2 + ey] = scale[d][at]
        return table

    def grid_elements(per):
        return [(x // per, y // per) for x in range(2 * per) for y in range(2 * per)]

    def direction_rows(elements):
        one = np.ones(len(elements))
        return np.concatenate([factor_rows(elements, [one if d == e else None for e in range(3)]) for d in range(3)], 0)

    spread = lambda per: np.kron(np.eye(ez), np.ones((1, per)))
    plain["e7"] = (direction_rows(grid_elements(p)), BF)
    plain["e3"] = (direction_rows(grid_elements(q)), BF)
    plain["e1"] = (direction_rows(grid_elements(2)), BF)
    plain["s64"] = (spread(p), BF)
    plain["s32"] = (spread(q), BF)
    plain["s256"] = (corner_columns(np.ones((1, 2)), ez), BF)
    plain["s80"] = (spread(modes), BF)
    pair["sl80"] = spread(modes) * np.tile(l7, ez)[None]

    m3 = q + 2
    ext = np.zeros((4, m3, 6 * q))
    for element in range(4):
        start = q * (element + 1)
        ext[element, 0, start - 2] += 1
        for at in range(q):
            ext[element, 1 + at, start + at] += 1
        ext[element, 1, start - 1] += 1
        ext[element, q, start + q] += 1
        ext[element, q + 1, start + q + 1] += 1
    a1m = blocks(s3.T, 4) @ ext.reshape(4 * m3, 6 * q)
    order = RING + ((0, 0),)
    span = lambda d: slice((d + 1) * 2 * q, (d + 2) * 2 * q)
    wm = [np.kron(a1m[:, span(dx)], a1m[:, span(dy)]) for dx, dy in order]
    pair["wmn"] = np.concatenate(wm[:8], 1)
    pair["wmo"] = wm[8]
    pair["azm"] = (blocks(s3.T, ez) @ line_extension(q, ez, True)).T
    inner3 = s3[1:-1]
    raw3 = blocks(inner3, 4)
    back3 = np.array(raw3[q : 3 * q])
    for at in (q - 1, 2 * q - 1, 3 * q - 1):
        total = raw3[at] + raw3[at + 1]
        for row in (at, at + 1):
            if q <= row < 3 * q:
                back3[row - q] = total
    bm = np.kron(back3, back3)
    pair["bm"] = bm
    bzm = z_back(inner3, q, ez)
    pair["bzm"] = bzm
    ll = np.concatenate(three(jm.T @ k3, jm.T @ w3, 2), 0)
    pair["lb"] = np.concatenate([ll @ ((wt3[:, 0] + extra)[:, None] * bm) for extra in (0, wt3[:, 1], wt3[:, 2])], 0)
    pair["rb"] = bzm @ np.concatenate([corner_columns(w3 @ jm, ez), corner_columns(k3 @ jm, ez)], 1)
    pair["jl"] = np.kron(blocks(jm.T, 2), blocks(jm.T, 2))
    pair["rj"] = corner_columns(jm, ez)
    place = {direction: at for at, direction in enumerate(order)}

    def ring_row(ex, ey, d):
        dx, dy = ex // 2 - 1, ey // 2 - 1
        return place[(dx, dy)] * 16 + d * 4 + (ex % 2) * 2 + ey % 2

    ld3, le3 = np.zeros((576, 144)), np.zeros((576, 144))
    for x in range(24):
        for y in range(24):
            ex, ey = x // m3 + 1, y // m3 + 1
            ld3[x * 24 + y, ring_row(ex, ey, 0)] = l3[x % m3]
            ld3[x * 24 + y, ring_row(ex, ey, 1)] = l3[y % m3]
            le3[x * 24 + y, ring_row(ex, ey, 2)] = 1
    ld9, le9 = np.zeros((count * count, 144)), np.zeros((count * count, 144))
    for x in range(count):
        for y in range(count):
            ex, ey = x // modes + 1, y // modes + 1
            ex = ex if ex < 3 else 7 - ex
            ld9[x * count + y, ring_row(ex, ey, 0)] = l7[x % modes]
            ld9[x * count + y, ring_row(ex, ey, 1)] = l7[y % modes]
            le9[x * count + y, ring_row(ex, ey, 2)] = 1
    pair["ld9"] = ld9
    plain["le9"] = (le9, BF)
    pair["ld3"] = ld3
    plain["le3"] = (le3, BF)
    plain["s48"] = (spread(m3), BF)
    pair["sl48"] = spread(m3) * np.tile(l3, ez)[None]
    er = np.zeros((3, 9, 2 * q, 2 * q, 144))
    for at in range(9):
        for x in range(2 * q):
            for y in range(2 * q):
                for d in range(3):
                    er[d, at, x, y, at * 16 + d * 4 + (x // q) * 2 + y // q] = 1
    plain["er"] = (er.reshape(3 * 576, 144), BF)
    pair["k3"] = np.concatenate(three(k3, w3, 2), 0)
    pair["rk3"] = side_by_side(blocks(w3, ez), blocks(k3, ez))
    corner_line = lambda table: np.kron(np.eye(6), table)
    modes_of = [a1m @ corner_line(table) for table in (k3 @ jm, w3 @ jm)]
    pair["wl"] = np.concatenate(
        [np.kron(modes_of[left], modes_of[right]) for left, right in ((0, 1), (1, 0), (1, 1))], 1
    )
    pair["ra3"] = side_by_side(
        blocks((w3 @ jm).T, ez) @ pair["azm"], blocks((k3 @ jm).T, ez) @ pair["azm"]
    )
    spread_vertices, spread_factors = np.zeros((144, 128)), np.zeros((3, 144, 144))
    for row in range(144):
        (ex, cx), (ey, cy) = divmod(row // 12, 2), divmod(row % 12, 2)
        vx, vy = ex + cx, ey + cy
        column = (AHEAD.index(vx // 2 - 1) * 4 + vy // 2) * 8 + (vx % 2) * 2 + vy % 2
        spread_vertices[row, column] = 1
        for d in range(3):
            at = order.index((ex // 2 - 1, ey // 2 - 1))
            spread_factors[d, row, at * 16 + d * 4 + (ex % 2) * 2 + ey % 2] = 1
    plain["ev"] = (spread_vertices, BF)
    plain["ef"] = (spread_factors.reshape(432, 144), BF)
    corner_z = np.zeros((ez, 2 * ez))
    for element in range(ez):
        for at in range(2):
            corner_z[(element + at) % ez, 2 * element + at] = 1
    plain["cz"] = (np.tile(corner_z, (4, 1)), BF)
    plain["s16"] = (spread(2), BF)
    vertex_line = lambda table: np.array(
        [[table[at % q, v - at // q] if 0 <= v - at // q <= 1 else 0.0 for v in range(8)] for at in range(6 * q)]
    )
    plain1 = vertex_line(jm)

    def vertex_columns(left, right, dx, dy):
        table = np.zeros((64, 4, 4, 8))
        for iy in range(4):
            for ix, ahead in enumerate(AHEAD):
                for x in range(2):
                    for y in range(2):
                        table[:, ix, iy, x * 2 + y] = np.kron(
                            left[span(dx), (ahead + 1) * 2 + x], right[span(dy), iy * 2 + y]
                        )
        return table.reshape(64, 128)

    pair["jc"] = vertex_columns(plain1, plain1, 0, 0)

    def z_vertices(table):
        result = np.zeros((ez, ez * q))
        for element in range(ez):
            for at in range(q):
                result[element, element * q + at] += table[at, 0]
                result[(element + 1) % ez, element * q + at] += table[at, 1]
        return np.tile(result, (4, 1))

    pair["rcj"] = z_vertices(jm)
    mask, left = np.zeros((n_gy, 16, 128)), np.zeros((n_gy, 16, 16))
    for gy in range(n_gy):
        for row in range(16):
            vx, vy = row // 8 + row // 4 % 2, row // 2 % 2 + row % 2
            owner = gy + vy // 2
            if owner < n_gy:
                first = owner * 32 + (vx % 2) * 16 + (vy % 2) * 8
                mask[gy, row, first % 128 : first % 128 + 8] = 1
                left[gy, first // 128 + 4 * (vx // 2), row] = 1
    plain["mask"] = (mask.reshape(-1, 128), F32)
    plain["left"] = (left.reshape(-1, 16), BF)
    chosen = np.zeros((8, 32))
    select = np.zeros((32, 8))
    for lane in range(32):
        chosen[lane // 8, lane] = 1
        select[lane, lane % 8] = 1
    plain["chosen"] = (chosen, F32)
    plain["select"] = (select, BF)
    tables = {}
    for name, table in pair.items():
        table = fitted(np.asarray(table, np.float64), name in RIGHT)
        high = table.astype(ml_dtypes.bfloat16)
        rest = (table - high.astype(np.float64)).astype(ml_dtypes.bfloat16)
        if name in RIGHT:
            tables[name] = np.block([[high, rest], [high, np.zeros_like(rest)]])[None]
        else:
            tables[name] = np.stack([high, rest])
    for name, (table, kind) in plain.items():
        table = fitted(np.asarray(table), name in RIGHT)
        table = np.concatenate([table, table], 0) if name in RIGHT else table
        tables[name] = table.astype(ml_dtypes.bfloat16 if kind is BF else np.float32)[None]
    return tables


STAGES = (
    ("columns", "vo", "jxy", "jz", "s80", "sl80", "e7", "e3", "e1", "s64", "s32", "s256", "wz7", "chosen", "mask"),
    ("ld9", "le9", "vl", "az", "vb", "la", "bzra"),
    ("ld3", "le3", "s48", "sl48", "er"),
    (
        "wmo", "jl", "rj", "bz", "k7", "kz7", "wmn", "azm", "lb", "rb", "left", "bm", "bzm", "select",
        "rk3", "k3", "wl", "ra3", "ev", "ef", "cz", "s16", "jc", "rcj", "rp", "bzrp", "lp", "pxy", "pz",
    ),
)


def pack(tables):
    stacks, places = {}, {}
    for stage, names in enumerate(STAGES):
        for name in names:
            table = tables[name]
            key = (stage, table.dtype.name, table.shape[-1])
            parts = stacks.setdefault(key, [])
            at = sum(part.shape[0] for part in parts)
            height = -(-table.shape[1] // 16) * 16
            for part in table:
                parts.append(np.pad(part, ((0, height - part.shape[0]), (0, 0))))
            places[name] = (key, at, height, table.shape[1])
    keys = tuple(stacks)
    return keys, [np.concatenate(stacks[key], 0) for key in keys], places


class Table:
    def __init__(self, ref, place):
        _, self.at, self.height, self.rows = place
        self.ref = ref
        self.shape = (2, self.rows, ref.shape[-1])

    def __getitem__(self, part):
        part = 0 if part is Ellipsis else part
        return self.ref[self.at + part * self.height : self.at + part * self.height + self.rows, :]

    def piece(self, part, start, rows):
        return self.ref[pl.ds(self.at + part * self.height + start, rows), :]


def dot(a, b):
    return jnp.dot(a, b, preferred_element_type=F32)


def split(x):
    high = x.astype(BF)
    return high, (x - high.astype(F32)).astype(BF)


def wide(x, lanes=128):
    if x.shape[1] == lanes:
        return x
    return jnp.concatenate([x, jnp.zeros((x.shape[0], lanes - x.shape[1]), x.dtype)], 1)


def tall(x, rows):
    if x.shape[0] == rows:
        return x
    return jnp.concatenate([x, jnp.zeros((rows - x.shape[0], x.shape[1]), x.dtype)], 0)


def halves(x):
    middle = x.shape[1] // 2
    return x[:, :middle] + x[:, middle:]


def exactly(main, small, x):
    high, rest = split(x)
    return halves(dot(main, jnp.concatenate([high, rest], 1))) + dot(small, high)


def left3(table, x):
    return exactly(table[0], table[1], tall(x, table.shape[-1]))


def left2(table, x):
    return halves(dot(table[...], jnp.concatenate(split(tall(x, table.shape[-1])), 1)))


def terms3(table, x):
    x = tall(x, table.shape[-1])
    rows = table.shape[1] // 3
    first = exactly(table.piece(0, 0, 2 * rows), table.piece(1, 0, 2 * rows), x[:, 0:128])
    third = exactly(table.piece(0, 2 * rows, rows), table.piece(1, 2 * rows, rows), x[:, 128:256])
    return first[0:rows], first[rows:], third


def right3(x, table):
    return halves(right2(x, table))


def right2(x, table):
    return dot(jnp.concatenate(split(wide(x)), 1), table[...])


KEPT = {
    "fine_f": (768, 128), "mid_f": (192, 128), "low_f": (48, 256), "ring_f": (1728, 128), "inverse3": (576, 128), "wt7": (256, 128), "wt3": (64, 128), "base_mid": (64, 128),
    "base_low": (16, 256), "first_fine": (256, 128), "base_fine": (256, 128),
    "first_mid": (64, 128), "modal3": (576, 128), "base_ring": (576, 128),
    "ww7": (256, 128), "inverse9": (1600, 128), "corner_f": (432, 128), "modal9": (800, 256),
}


def cycle_kernel(keys, places, n_gx, n_gy, *refs):
    r_hbm, len_hbm, inv_hbm = refs[:3]
    count = len(keys)
    packed = refs[3 : 3 + count]
    out_fine, out_mid, out_low = refs[3 + count : 6 + count]
    stores = refs[6 + count : 6 + 2 * count]
    (
        r_ref, len_ref, inv_ref, rs, fs, hb1, rm, fm, rp, fp, hb2, hs1, hs2, rb, corner, held, gs, gb, cb, invs,
        send_sem, recv_sem, gsend, grecv, csend, crecv, isend, irecv, in_sem, table_sem,
    ) = refs[6 + 2 * count : -len(KEPT)]
    gx, gy = lax.axis_index("gx"), lax.axis_index("gy")
    last = n_gy - 1
    barrier = pltpu.get_barrier_semaphore()

    def greet(ahead, row):
        pl.semaphore_signal(
            barrier, inc=1, device_id=(lax.rem(gx + (ahead + n_gx), n_gx), row), device_id_type=MESH
        )

    def greet_if(row, *columns):
        @pl.when((row >= 0) & (row <= last))
        def _():
            for ahead in columns:
                greet(ahead, row)

    greet_if(gy + 1, 0, 1, -1)
    greet_if(gy - 1, 0, 1, -1)
    greet(1, gy)
    greet(-1, gy)
    greet(2, gy)
    for row in range(n_gy):
        @pl.when((row < gy - 1) | (row > gy + 1))
        def _():
            greet(0, row)
            greet(-1, row)
    inputs = [
        pltpu.make_async_copy(source, target, in_sem.at[at])
        for at, (source, target) in enumerate(((len_hbm, len_ref), (r_hbm, r_ref), (inv_hbm, inv_ref)))
    ]
    loads = [pltpu.make_async_copy(packed[at], stores[at], table_sem.at[at]) for at in range(count)]
    for load in inputs:
        load.start()

    def fetch(*stages):
        for key, load in zip(keys, loads):
            if key[0] in stages:
                load.start()

    fetch(0)

    def ready(stage):
        for key, load in zip(keys, loads):
            if key[0] == stage:
                load.wait()

    kept = dict(zip(KEPT, refs[-len(KEPT) :]))

    def keep(name, value):
        kept[name][...] = value
        return kept[name]

    t = {name: Table(stores[keys.index(place[0])], place) for name, place in places.items()}
    at_bottom, at_top = gy == 0, gy == last
    not_bottom, not_top = gy > 0, gy < last
    sent = {0: None, 1: not_bottom, 2: not_top}

    def guarded(condition, action):
        if condition is None:
            action()
        else:
            pl.when(condition)(action)

    def exchange(phase, source, buffer, rows):
        at = offsets(rows)

        def group(number):
            def action():
                for index in range(*GROUPS[number]):
                    tx, ty = RING[index]
                    slot = RING.index((-tx, -ty))
                    landing = (0, 2, 1)[number]
                    pltpu.make_async_remote_copy(
                        src_ref=source(index),
                        dst_ref=buffer.at[pl.ds(at[slot], rows[slot])],
                        send_sem=send_sem.at[phase, number],
                        recv_sem=recv_sem.at[phase, landing],
                        device_id=(lax.rem(gx + (tx + n_gx), n_gx), gy + ty),
                        device_id_type=MESH,
                    ).start()

            return action

        for number in (1, 2, 0):
            guarded(sent[number], group(number))

    def settle(phase, sems, buffer, rows):
        at = offsets(rows)
        for number in range(3):
            first, end = GROUPS[number]
            piece = buffer.at[pl.ds(at[first], at[end] - at[first])]
            guarded(sent[number], lambda: pltpu.make_async_copy(piece, piece, sems.at[phase, number]).wait())

    def clear(number):
        first, end = GROUPS[number]
        for buffer, rows in (
            (fs, BLOCK_ROWS), (hb1, WIDE_ROWS), (rp, BLOCK_ROWS), (fp, BLOCK_ROWS), (hb2, WIDE_ROWS),
        ):
            at = offsets(rows)
            buffer[at[first] : at[end], :] = jnp.zeros((at[end] - at[first], buffer.shape[1]), buffer.dtype)

    @pl.when(at_bottom)
    def _():
        clear(1)
        invs[0:32, :] = jnp.zeros((32, invs.shape[1]), BF)

    @pl.when(at_top)
    def _():
        clear(2)
        invs[64:96, :] = jnp.zeros((32, invs.shape[1]), BF)

    @pl.when(gy >= last - 1)
    def _():
        invs[96:128, :] = jnp.zeros((32, invs.shape[1]), BF)

    at_wide = offsets(WIDE_ROWS)

    def mirrored(values):
        return jnp.concatenate([values[(15 - x) * 16 : (16 - x) * 16] for x in range(16)], 0)

    def wide_halo(field, stage):
        for x in range(16):
            rb[x] = field[15 - x]
        for index, (tx, ty) in enumerate(RING):
            source, ys = (rb if tx < 0 else field), (6, 0)[ty < 0]
            if 0 not in (tx, ty):
                corner[48:64, :] = jnp.zeros((16, 128), F32)
            for pair in range(5):
                xa, ya = 6 + 2 * pair, ys + 2 * pair
                at = at_wide[index] + pair * 16
                if ty == 0:
                    layers = source[xa, :, :], source[xa + 1, :, :]
                    stage[at : at + 16, :] = jnp.concatenate(layers, 1).astype(stage.dtype)
                elif tx == 0:
                    rows = [jnp.concatenate([field[0:8, y, :], rb[0:8, y, :]], 1) for y in (ya, ya + 1)]
                    stage[at : at + 16, :] = jnp.concatenate(rows, 0).astype(stage.dtype)
                else:
                    layers = source[6:16, ya, :], source[6:16, ya + 1, :]
                    corner[pair * 10 : pair * 10 + 10, :] = jnp.concatenate(layers, 1)
            if 0 not in (tx, ty):
                stage[at_wide[index] : at_wide[index + 1], :] = corner[...].astype(stage.dtype)

    def side_values(buffer):
        plain, turned_back = {}, {}
        for index, direction in enumerate(RING):
            piece = buffer[at_wide[index] : at_wide[index + 1], :]
            plain[direction] = piece
            turned_back[direction] = pltpu.roll(piece.astype(F32), 64, 1).astype(BF)
        ends, flanks = LOW_SIDE[:3], LOW_SIDE[3:]
        opposite = [(-dx, dy) for dx, dy in ends]
        low_part = [plain[d] for d in ends + flanks] + [turned_back[d] for d in ends + flanks]
        high_part = [plain[d] for d in opposite] + [turned_back[d] for d in flanks]
        high_part += [turned_back[d] for d in opposite] + [plain[d] for d in flanks]
        return jnp.concatenate([tall(jnp.concatenate(part, 0), 768) for part in (low_part, high_part)], 1)

    def fold(block):
        result = block[0:16]
        for part in range(1, 4):
            result = result + pltpu.roll(block[part * 16 : part * 16 + 16], part * 32, 1)
        return result

    def spread_blocks(folded, blocks_ref):
        for part in range(4):
            turned_back = pltpu.roll(folded[0:128, :], (128 - part * 32) % 128, 1) if part else folded[0:128, :]
            for slot in range(8):
                blocks_ref[slot * 64 + part * 16 : slot * 64 + part * 16 + 16, :] = turned_back[
                    slot * 16 : slot * 16 + 16
                ]


    inputs[0].wait()
    own_f = 8 * 16
    for ex in range(2):
        a, b, c = len_ref[0, ex], len_ref[1, ex], len_ref[2, ex]
        fs[own_f + ex * 2 : own_f + ex * 2 + 2, :] = wide(b * c / (2.0 * a))
        fs[own_f + 4 + ex * 2 : own_f + 6 + ex * 2, :] = wide(a * c / (2.0 * b))
        fs[own_f + 8 + ex * 2 : own_f + 10 + ex * 2, :] = wide(a * b / (2.0 * c))
    fs[own_f + 12 : own_f + 16, :] = jnp.zeros((4, 128), F32)
    inputs[1].wait()
    wide_halo(r_ref, hs1)
    near = jnp.minimum(gy + 1, last) - jnp.maximum(gy - 1, 0) + 1
    pl.semaphore_wait(barrier, 2 * n_gy + near)
    exchange(0, lambda index: fs.at[pl.ds(own_f, 16)], fs, BLOCK_ROWS)
    exchange(1, lambda index: hs1.at[pl.ds(at_wide[index], WIDE_ROWS[index])], hb1, WIDE_ROWS)
    fetch(1, 2)
    inputs[2].wait()
    invs[32:64, :] = inv_ref[0]
    reach = ((1, 0, not_top, not_bottom), (-1, 2, not_bottom, not_top), (-2, 3, gy > 1, gy < last - 1))

    def inverse_copy(at):
        step, slot, _, _ = reach[at]
        return pltpu.make_async_remote_copy(
            src_ref=invs.at[pl.ds(32, 32)],
            dst_ref=invs.at[pl.ds(slot * 32, 32)],
            send_sem=isend.at[at],
            recv_sem=irecv.at[at],
            device_id=(gx, gy + step),
            device_id_type=MESH,
        )

    for at in range(3):
        pl.when(reach[at][2])(lambda: inverse_copy(at).start())

    bottom_on = jnp.where(at_bottom, 1.0, 0.0)
    top_on = jnp.where(at_top, 1.0, 0.0)

    ready(0)
    columns = t["columns"][...]

    def wall_weight(rows, at):
        piece = columns[0:rows]
        return piece[:, at : at + 1] + bottom_on * piece[:, at + 1 : at + 2] + top_on * piece[:, at + 2 : at + 3]

    wt7 = keep("wt7", jnp.broadcast_to(wall_weight(256, 0), (256, 128)))
    wt3 = keep("wt3", jnp.broadcast_to(wall_weight(64, 6), (64, 128)))
    ww7 = keep("ww7", jnp.broadcast_to(columns[:, 9:10], (256, 128)))
    r = wide(r_ref[...].reshape(256, 64))
    f_own = wide(fs[own_f : own_f + 16, :])
    modal9 = keep("modal9", left3(t["vo"], jnp.concatenate([r, mirrored(r)], 1)))
    base_mid = keep("base_mid", right3(left3(t["jxy"], r), t["jz"]))
    fine_f = keep("fine_f", left2(t["e7"], right2(f_own, t["s64"])))
    mid_f = keep("mid_f", left2(t["e3"], right2(f_own, t["s32"])))
    low_f = keep("low_f", left2(t["e1"], right2(f_own, t["s256"])))

    def ring_modes(buffer):
        modal = modal9[...] + dot(t["vl"][...], side_values(buffer))
        modal = right3(jnp.concatenate([modal[:, 0:128], modal[:, 128:256]], 0), t["az"]) * inverse9[...]
        return jnp.concatenate([modal[0:800], modal[800:1600]], 1)

    def joined(values):
        return values[:, 0:128] + mirrored(values[:, 128:256])

    ready(1)
    fetch(3)
    settle(0, recv_sem, fs, BLOCK_ROWS)
    ring_l = wide(fs[...])
    d9 = left3(t["ld9"], right2(ring_l, t["s80"])) + left2(t["le9"], right3(ring_l, t["sl80"]))
    inverse9 = keep("inverse9", jnp.where(d9 > 0.0, 1.0 / d9, 0.0))
    settle(1, recv_sem, hb1, WIDE_ROWS)
    local = joined(left3(t["vb"], ring_modes(hb1))) * wt7[...]
    terms = terms3(t["la"], right3(local, t["bzra"]))
    residual_mid = base_mid[...] - (mid_f[0:64] * terms[0] + mid_f[64:128] * terms[1] + mid_f[128:192] * terms[2])
    rp[128:144, :] = fold(residual_mid)
    exchange(3, lambda index: rp.at[pl.ds(128, 16)], rp, BLOCK_ROWS)
    rm[512:576, :] = residual_mid

    ready(2)
    ready(3)
    ring_l = wide(fs[...])
    d3 = left3(t["ld3"], right2(ring_l, t["s48"])) + left2(t["le3"], right3(ring_l, t["sl48"]))
    inverse3 = keep("inverse3", jnp.where(d3 > 0.0, 1.0 / d3, 0.0))
    own_modal = keep("modal3", left3(t["wmo"], residual_mid))
    base_low = keep("base_low", right3(left3(t["jl"], residual_mid), t["rj"]))
    first_fine = keep("first_fine", right3(local, t["bz"]))
    massed = left3(t["k7"], first_fine[...] * t["wz7"][...][0:1])
    along_z = right3(first_fine[...], t["kz7"]) * ww7[...]
    base_fine = keep(
        "base_fine",
        wide(r_ref[...].reshape(256, 64))
        - (fine_f[0:256] * massed[0:256] + fine_f[256:512] * massed[256:512] + fine_f[512:768] * along_z),
    )

    settle(3, recv_sem, rp, BLOCK_ROWS)
    spread_blocks(rp, rm)
    modal3 = own_modal[...] + left3(t["wmn"], rm[0:512, :])
    modal3 = right3(modal3, t["azm"]) * inverse3[...]
    variant = jnp.where(at_bottom, 1, jnp.where(at_top, 2, 0))
    rows = pl.multiple_of(variant * 48, 16)
    low = exactly(t["lb"].piece(0, rows, 48), t["lb"].piece(1, rows, 48), tall(modal3, t["lb"].shape[-1]))
    low = right3(low, t["rb"])
    low = base_low[...] - (
        low_f[0:16] * low[0:16, 0:256] + low_f[16:32] * low[16:32, 0:256] + low_f[32:48] * low[32:48, 256:512]
    )
    wall = pl.multiple_of(gy * 16, 16)
    low = tall(halves(low) * t["mask"].piece(0, wall, 16), 128)
    message = halves(dot(t["left"].piece(0, wall, 16), jnp.concatenate(split(low), 1)))[0:8]
    gs[...] = message

    def send_slab(flips, ahead):
        row = gy
        for bit in (8, 4, 2, 1):
            if flips & bit:
                row = row + bit * (1 - 2 * (gy // bit % 2))
        pltpu.make_async_remote_copy(
            src_ref=gs,
            dst_ref=gb.at[flips + (n_gy - 1 if ahead else -1)],
            send_sem=gsend,
            recv_sem=grecv,
            device_id=(lax.rem(gx + ahead, n_gx), row),
            device_id_type=MESH,
        ).start()

    for flips in (12, 13, 10, 11, 14, 15, 8, 9, 4, 5, 2, 3, 6, 7, 1, 0):
        if flips < n_gy:
            send_slab(flips, 1)
            if flips:
                send_slab(flips, 0)

    first_mid = keep("first_mid", right3(left3(t["bm"], modal3) * wt3[...], t["bzm"]))
    fm[512:576, :] = first_mid[...]
    fp[128:144, :] = fold(first_mid[...])
    exchange(4, lambda index: fp.at[pl.ds(128, 16)], fp, BLOCK_ROWS)

    for at in range(3):
        pl.when(reach[at][3])(lambda: inverse_copy(at).wait_recv())
    pltpu.make_async_copy(gb, gb, grecv).wait()
    here = gs[...] + jnp.sum(gb[0 : n_gy - 1], axis=0)
    behind = jnp.sum(gb[n_gy - 1 :], axis=0)
    chunks = inv_ref.shape[2] // 128
    vector = here + pltpu.roll(behind, 4, 0)
    row = lax.broadcasted_iota(jnp.int32, (8, 128), 0)
    vector = jnp.concatenate([jnp.where(row == chunk, vector, 0.0) for chunk in range(chunks)], 1)
    vector = tall(vector, 16).astype(BF)
    solved = lax.dot_general(vector, invs[...], (((1,), (1,)), ((), ())), preferred_element_type=F32)
    solved = jnp.broadcast_to(jnp.sum(solved, axis=0, keepdims=True), (8, 128))
    chosen = t["chosen"][...]
    for iy in range(4):
        cb[96 + iy * 8 : 104 + iy * 8, :] = (pltpu.roll(solved, 128 - iy * 32, 1) if iy else solved) * chosen
    for ix in (2, 1, 0):
        pltpu.make_async_remote_copy(
            src_ref=cb.at[pl.ds(96, 32)],
            dst_ref=cb.at[pl.ds(ix * 32, 32)],
            send_sem=csend,
            recv_sem=crecv,
            device_id=(lax.rem(gx - AHEAD[ix] + n_gx, n_gx), gy),
            device_id_type=MESH,
        ).start()

    others = cb.at[pl.ds(0, 96)]

    ring_l = wide(fs[...])
    ring_f = keep("ring_f", left2(t["er"], right2(ring_l, t["s32"])))
    corner_f = keep("corner_f", left2(t["ef"], right2(ring_l, t["s16"])))
    low_out = right2(tall(cb[104:112, :], 16), t["select"])
    out_low[0] = low_out[0:2, 0:8]
    out_low[1] = low_out[2:4, 0:8]
    settle(4, recv_sem, fp, BLOCK_ROWS)
    spread_blocks(fp, fm)
    turned = right3(fm[...], t["rk3"])
    parts = []
    for at in range(9):
        piece = terms3(t["k3"], turned[at * 64 : (at + 1) * 64])
        parts.append(
            rm[at * 64 : (at + 1) * 64, :]
            - (
                ring_f[at * 64 : (at + 1) * 64] * piece[0]
                + ring_f[576 + at * 64 : 576 + (at + 1) * 64] * piece[1]
                + ring_f[1152 + at * 64 : 1152 + (at + 1) * 64] * piece[2]
            )
        )
    base_ring = keep("base_ring", jnp.concatenate(parts, 0))
    modal3 = left3(t["wmn"], base_ring[0:512]) + left3(t["wmo"], base_ring[512:576])
    modal3 = keep("modal3", right3(modal3, t["azm"]))

    pltpu.make_async_copy(others, others, crecv).wait()
    corrections = wide(cb[...])
    change = left2(t["ev"], right2(corrections, t["cz"]))
    change = right3(jnp.concatenate([change * corner_f[at * 144 : at * 144 + 144] for at in range(3)], 0), t["ra3"])
    change = jnp.concatenate([change[0:288, 0:128], change[288:432, 128:256]], 0)
    modal3 = (modal3[...] - left3(t["wl"], change)) * inverse3[...]
    held[0:64, :] = first_mid[...] + right3(left3(t["jc"], corrections), t["rcj"])
    smoothed = left3(t["bm"], modal3) * wt3[...]

    turned = terms3(t["lp"], right3(smoothed, t["bzrp"]) + right3(held[0:64, :], t["rp"]))
    residual = base_fine[...] - (
        fine_f[0:256] * turned[0]
        + fine_f[256:512] * turned[1]
        + fine_f[512:768] * turned[2]
    )
    rs[...] = residual[:, 0:64].reshape(16, 16, 64)
    wide_halo(rs, hs2)
    exchange(5, lambda index: hs2.at[pl.ds(at_wide[index], WIDE_ROWS[index])], hb2, WIDE_ROWS)
    mid_result = held[0:64, :] + right3(smoothed, t["bzm"])
    out_mid[...] = mid_result[:, 0:32].reshape(8, 8, 32)
    modal9 = keep("modal9", dot(t["vo"][0], jnp.concatenate([residual, mirrored(residual)], 1).astype(BF)))
    held[...] = first_fine[...] + right3(left3(t["pxy"], mid_result), t["pz"])
    settle(5, recv_sem, hb2, WIDE_ROWS)
    local = joined(dot(t["vb"][0], tall(ring_modes(hb2), 896).astype(BF))) * wt7[...]
    result = held[...] + right3(local, t["bz"])
    out_fine[...] = result[:, 0:64].reshape(16, 16, 64)

    for phase, buffer, rows in (
        (0, fs, BLOCK_ROWS), (1, hb1, WIDE_ROWS), (3, rp, BLOCK_ROWS), (4, fp, BLOCK_ROWS), (5, hb2, WIDE_ROWS),
    ):
        settle(phase, send_sem, buffer, rows)
    pltpu.make_async_copy(gb, gb, gsend).wait()
    pltpu.make_async_copy(others, others, csend).wait()
    for at in range(3):
        pl.when(reach[at][2])(lambda: inverse_copy(at).wait_send())


def hand_over(*refs):
    copies = [pltpu.make_async_copy(refs[at], refs[3 + at], refs[6].at[at]) for at in range(3)]
    for copy in copies:
        copy.start()
    for copy in copies:
        copy.wait()


def shards(n_gx, n_gy, local_residual, lengths, coarse_inverse):
    keys, packed, places = pack(build_tables(n_gy, lengths.shape[3]))
    vmem = pl.BlockSpec(memory_space=pltpu.VMEM)
    scratch = [pltpu.VMEM(table.shape, BF if key[1] == "bfloat16" else F32) for key, table in zip(keys, packed)]
    scratch += [
        pltpu.VMEM(local_residual.shape, F32),
        pltpu.VMEM(lengths.shape, F32),
        pltpu.VMEM(coarse_inverse.shape, BF),
        pltpu.VMEM((16, 16, 64), F32),
        pltpu.VMEM((144, 128), F32),
        pltpu.VMEM((576, 128), BF),
        pltpu.VMEM((576, 128), F32),
        pltpu.VMEM((576, 128), F32),
        pltpu.VMEM((144, 128), F32),
        pltpu.VMEM((144, 128), F32),
        pltpu.VMEM((576, 128), BF),
        pltpu.VMEM((576, 128), BF),
        pltpu.VMEM((576, 128), BF),
        pltpu.VMEM((16, 16, 64), F32),
        pltpu.VMEM((64, 128), F32),
        pltpu.VMEM((256, 128), F32),
        pltpu.VMEM((8, 128), F32),
        pltpu.VMEM((2 * n_gy - 1, 8, 128), F32),
        pltpu.VMEM((128, 128), F32),
        pltpu.VMEM((128, coarse_inverse.shape[2]), BF),
        pltpu.SemaphoreType.DMA((6, 3)),
        pltpu.SemaphoreType.DMA((6, 3)),
        pltpu.SemaphoreType.DMA,
        pltpu.SemaphoreType.DMA,
        pltpu.SemaphoreType.DMA,
        pltpu.SemaphoreType.DMA,
        pltpu.SemaphoreType.DMA((3,)),
        pltpu.SemaphoreType.DMA((3,)),
        pltpu.SemaphoreType.DMA((3,)),
        pltpu.SemaphoreType.DMA((len(keys),)),
    ]
    scratch += [pltpu.VMEM(shape, F32) for shape in KEPT.values()]
    outs = pl.pallas_call(
        functools.partial(cycle_kernel, keys, places, n_gx, n_gy),
        out_shape=(
            jax.ShapeDtypeStruct((16, 16, 64), F32),
            jax.ShapeDtypeStruct((8, 8, 32), F32),
            jax.ShapeDtypeStruct((2, 2, 8), F32),
        ),
        in_specs=[pl.BlockSpec(memory_space=pl.ANY)] * (3 + len(keys)),
        out_specs=(vmem, vmem, vmem),
        scratch_shapes=scratch,
        compiler_params=pltpu.CompilerParams(collective_id=0, has_side_effects=True, vmem_limit_bytes=60 * 1024 * 1024),
    )(local_residual, lengths, coarse_inverse, *[jnp.asarray(table) for table in packed])
    return pl.pallas_call(
        hand_over,
        out_shape=tuple(jax.ShapeDtypeStruct(out.shape, out.dtype) for out in outs),
        in_specs=[vmem] * 3,
        out_specs=[pl.BlockSpec(memory_space=pl.ANY)] * 3,
        scratch_shapes=[pltpu.SemaphoreType.DMA((3,))],
    )(*outs)


def solution(mesh):
    in_specs = (P("gx", "gy", None), P(None, "gx", "gy", None), P("gx", "gy", None))
    out_specs = (P("gx", "gy", None), P("gx", "gy", None), P("gx", "gy", None))
    return jax.shard_map(
        functools.partial(shards, mesh.shape["gx"], mesh.shape["gy"]),
        mesh=mesh,
        in_specs=in_specs,
        out_specs=out_specs,
        check_vma=False,
    )
```

```python
import functools
import math

import jax
import jax.numpy as jnp
import ml_dtypes
import numpy as np
from jax import lax
from jax.experimental import pallas as pl
from jax.experimental.pallas import tpu as pltpu
from jax.sharding import PartitionSpec as P

ORDER = 7
MID_ORDER = 3


def legendre_pair(order, point):
    older = 1.0
    newer = point
    for degree in range(2, order + 1):
        nexter = ((2 * degree - 1) * point * newer - (degree - 1) * older) / degree
        older = newer
        newer = nexter
    return (newer, older)


def jacobi_eigen(matrix):
    count_n = len(matrix)
    work = [list(row_items) for row_items in matrix]
    vectors = [
        [1.0 if row_at == col_at else 0.0 for col_at in range(count_n)] for row_at in range(count_n)
    ]
    for sweep_count in range(60):
        for lower_at in range(count_n):
            for upper_at in range(lower_at + 1, count_n):
                off_value = work[lower_at][upper_at]
                if abs(off_value) < 1e-18 * (
                    abs(work[lower_at][lower_at]) + abs(work[upper_at][upper_at])
                ):
                    continue
                angle_ratio = (work[upper_at][upper_at] - work[lower_at][lower_at]) / (
                    2.0 * off_value
                )
                sign_value = 1.0 if angle_ratio >= 0 else -1.0
                tangent = sign_value / (
                    abs(angle_ratio) + math.sqrt(angle_ratio * angle_ratio + 1.0)
                )
                cosine = 1.0 / math.sqrt(tangent * tangent + 1.0)
                sine_value = tangent * cosine
                for other_at in range(count_n):
                    left_value = work[other_at][lower_at]
                    right_value = work[other_at][upper_at]
                    work[other_at][lower_at] = cosine * left_value - sine_value * right_value
                    work[other_at][upper_at] = sine_value * left_value + cosine * right_value
                for other_at in range(count_n):
                    left_value = work[lower_at][other_at]
                    right_value = work[upper_at][other_at]
                    work[lower_at][other_at] = cosine * left_value - sine_value * right_value
                    work[upper_at][other_at] = sine_value * left_value + cosine * right_value
                for other_at in range(count_n):
                    left_value = vectors[other_at][lower_at]
                    right_value = vectors[other_at][upper_at]
                    vectors[other_at][lower_at] = cosine * left_value - sine_value * right_value
                    vectors[other_at][upper_at] = sine_value * left_value + cosine * right_value
    eigen_list = [work[row_at][row_at] for row_at in range(count_n)]
    ordering = sorted(range(count_n), key=lambda index_at: eigen_list[index_at])
    rates = [eigen_list[index_at] for index_at in ordering]
    basis = [[vectors[row_at][index_at] for index_at in ordering] for row_at in range(count_n)]
    return (rates, basis)


def gll_tables(order):
    point_count = order + 1
    node_list = []
    for node_at in range(point_count):
        point = math.cos(math.pi * node_at / order)
        for newton_step in range(100):
            top_value, lower_value = legendre_pair(order, point)
            point = point - (point * top_value - lower_value) / ((order + 1) * top_value)
        node_list.append(point)
    node_list = node_list[::-1]
    node_list[0] = -1.0
    node_list[-1] = 1.0
    values = [legendre_pair(order, point)[0] for point in node_list]
    weight_list = [2.0 / (order * (order + 1) * value_at**2) for value_at in values]
    derivative = [[0.0] * point_count for row_at in range(point_count)]
    for row_at in range(point_count):
        for col_at in range(point_count):
            if row_at != col_at:
                derivative[row_at][col_at] = values[row_at] / (
                    values[col_at] * (node_list[row_at] - node_list[col_at])
                )
    derivative[0][0] = -order * (order + 1) / 4.0
    derivative[order][order] = order * (order + 1) / 4.0
    stiff_list = [
        [
            sum(
                (
                    derivative[inner_at][row_at]
                    * weight_list[inner_at]
                    * derivative[inner_at][col_at]
                    for inner_at in range(point_count)
                )
            )
            for col_at in range(point_count)
        ]
        for row_at in range(point_count)
    ]
    extent = 3 * order + 1
    big_stiff = [[0.0] * extent for row_at in range(extent)]
    big_mass = [0.0] * extent
    for offset_at in (0, order, 2 * order):
        for row_at in range(point_count):
            big_mass[offset_at + row_at] += weight_list[row_at]
            for col_at in range(point_count):
                big_stiff[offset_at + row_at][offset_at + col_at] += stiff_list[row_at][col_at]
    chosen = list(range(order - 1, 2 * order + 2))
    root_mass = [1.0 / math.sqrt(big_mass[index_at]) for index_at in chosen]
    scaled = [
        [
            root_mass[row_at] * big_stiff[chosen[row_at]][chosen[col_at]] * root_mass[col_at]
            for col_at in range(len(chosen))
        ]
        for row_at in range(len(chosen))
    ]
    rates, basis = jacobi_eigen(scaled)
    eigen_basis = [
        [root_mass[row_at] * basis[row_at][col_at] for col_at in range(len(chosen))]
        for row_at in range(len(chosen))
    ]
    return (
        np.array(node_list),
        np.array(weight_list),
        np.array(stiff_list),
        np.array(eigen_basis),
        np.array(rates),
    )


def interp_table(fine_nodes, coarse_nodes):
    coarse_count = len(coarse_nodes)
    columns = []
    for column in range(coarse_count):
        factors_list = [
            (fine_nodes - coarse_nodes[other_node])
            / (coarse_nodes[column] - coarse_nodes[other_node])
            for other_node in range(coarse_count)
            if other_node != column
        ]
        columns.append(np.prod(np.stack(factors_list), axis=0))
    return np.stack(columns, axis=1)

BF = jnp.bfloat16
F32 = jnp.float32
RING = ((-1, 0), (1, 0), (0, -1), (-1, -1), (1, -1), (0, 1), (-1, 1), (1, 1))
GROUPS = ((0, 2), (2, 5), (5, 8))
AHEAD = (-1, 1, 2, 0)
BLOCK_ROWS = (16,) * 8
WIDE_ROWS = (80, 80, 80, 64, 64, 80, 64, 64)
LOW_SIDE = ((-1, 0), (-1, -1), (-1, 1), (0, -1), (0, 1))
MESH = pl.DeviceIdType.MESH


def offsets(rows):
    return tuple(int(at) for at in np.concatenate([[0], np.cumsum(rows)]))


def blocks(matrix, count):
    return np.kron(np.eye(count), matrix)


def line_extension(points, elements, periodic):
    size = elements * points
    width = size if periodic else size + 4
    table = np.zeros((elements, points + 2, width))

    def column(at):
        if periodic:
            return at % size
        if at < 0:
            return {-2: size, -1: size + 1}[at]
        if at >= size:
            return {size: size + 2, size + 1: size + 3}[at]
        return at

    for element in range(elements):
        start = element * points
        table[element, 0, column(start - 2)] += 1
        for at in range(points):
            table[element, 1 + at, start + at] += 1
        table[element, 1, column(start - 1)] += 1
        table[element, points, column(start + points)] += 1
        table[element, points + 1, column(start + points + 1)] += 1
    return table.reshape(elements * (points + 2), width)


def line_weights(points, elements):
    position = np.arange(points * elements) % points
    return np.where((position == 0) | (position == points - 1), 0.5, 1.0)


def z_back(inner, points, elements):
    table = blocks(inner, elements)
    total = np.array(table)
    size = points * elements
    for element in range(elements):
        low, high = element * points, (element * points - 1) % size
        total[low] = table[low] + table[high]
        total[high] = total[low]
    return (total * line_weights(points, elements)[:, None]).T


RIGHT = (
    "az", "bz", "bzra", "jz", "kz7", "rp", "pz", "azm", "bzm", "rb", "rj", "rk3", "ra3", "bzrp", "cz", "s16", "rcj",
    "s64", "s32", "s256", "s80", "sl80", "s48", "sl48", "select",
)


def fitted(table, right):
    rows, columns = table.shape[-2:]
    more = ((0, -rows % 128 if right else 0), (0, -columns % 128))
    return np.pad(table, ((0, 0),) * (table.ndim - 2) + more)


def side_by_side(*parts):
    return np.concatenate([np.pad(part, ((0, 0), (0, -part.shape[1] % 128))) for part in parts], 1)


def corner_columns(inner_table, elements):
    points = inner_table.shape[0]
    table = np.zeros((elements * points, 256))
    for corner in range(2):
        for lane in range(128):
            element = (lane % elements - corner) % elements
            table[element * points : (element + 1) * points, corner * 128 + lane] = inner_table[:, corner]
    return table


def build_tables(n_gy, ez):
    p, q = ORDER + 1, MID_ORDER + 1
    fine, mid, low = gll_tables(ORDER), gll_tables(MID_ORDER), gll_tables(1)
    jf = interp_table(fine[0], mid[0])
    jm = interp_table(mid[0], low[0])
    k7, w7, s7, l7 = fine[2], np.diag(fine[1]), fine[3], fine[4]
    k3, w3, s3, l3 = mid[2], np.diag(mid[1]), mid[3], mid[4]
    pair, plain = {}, {}
    modes = p + 2
    pair["az"] = (blocks(s7.T, ez) @ line_extension(p, ez, True)).T
    inner = s7[1:-1]
    bz = z_back(inner, p, ez)
    pair["bz"] = bz

    count = 4 * modes
    ext = np.zeros((4, modes, 36))
    for element in range(4):
        start = 2 + p * element
        ext[element, 0, start - 2] += 1
        for at in range(p):
            ext[element, 1 + at, start + at] += 1
        ext[element, 1, start - 1] += 1
        ext[element, p, start + p] += 1
        ext[element, p + 1, start + p + 1] += 1
    a1w = blocks(s7.T, 4) @ ext.reshape(count, 36)
    middle = a1w[:, 10:26]
    beside = {-1: a1w[:, 0:10], 1: a1w[:, 26:36]}
    near, parts = slice(0, 2 * modes), []
    for half in range(2):
        for dx, dy in LOW_SIDE:
            if dy == 0:
                pieces = [np.kron(beside[dx][near, at : at + 1], middle) for at in range(half, 10, 2)]
            elif dx == 0:
                columns = range(15, 7, -1) if half else range(8)
                pieces = [np.kron(middle[near][:, columns], beside[dy][:, at : at + 1]) for at in range(10)]
            else:
                pieces = [np.kron(beside[dx][near], beside[dy][:, at : at + 1]) for at in range(half, 10, 2)]
            piece = np.concatenate(pieces, 1)
            parts.append(np.pad(piece, ((0, 0), (0, -piece.shape[1] % 16))))
    plain["vl"] = (np.concatenate(parts, 1), BF)
    pair["vo"] = np.kron(middle[near], middle)
    raw = blocks(inner, 4)
    around = np.array(raw[p : 3 * p])
    for at in (p - 1, 2 * p - 1, 3 * p - 1):
        for row in (at, at + 1):
            if p <= row < 3 * p:
                around[row - p] = raw[at] + raw[at + 1]
    pair["vb"] = np.kron(around[:, near], around)

    def weights(points):
        line = line_weights(points, 2)
        low_side, high_side = np.zeros(2 * points), np.zeros(2 * points)
        low_side[0], high_side[-1] = 0.5, 0.5
        return np.stack([np.kron(line, line), np.kron(line, low_side), np.kron(line, high_side)], 1)

    wt7, wt3 = weights(p), weights(q)
    columns = np.zeros((256, 128))
    columns[:, 0:3] = wt7
    columns[:64, 6:9] = wt3
    columns[:, 9] = np.kron(np.tile(fine[1], 2), np.tile(fine[1], 2))
    plain["columns"] = (columns, F32)

    def three(stiff, mass, count):
        stiff, mass = blocks(stiff, count), blocks(mass, count)
        return np.kron(stiff, mass), np.kron(mass, stiff), np.kron(mass, mass)

    la = np.concatenate(three(jf.T @ k7, jf.T @ w7, 2), 0)
    ra = side_by_side(blocks(w7 @ jf, ez), blocks(k7 @ jf, ez))
    pair["la"] = la
    pair["bzra"] = bz @ ra
    pair["jxy"] = np.kron(blocks(jf.T, 2), blocks(jf.T, 2))
    pair["jz"] = blocks(jf, ez)
    k7x, k7y, _ = three(k7, w7, 2)
    pair["k7"] = np.concatenate([k7x, k7y], 0)
    pair["kz7"] = blocks(k7, ez)
    plain["wz7"] = (np.tile(np.tile(fine[1], ez)[None], (8, 1)), F32)
    pair["lp"] = np.concatenate(three(k7 @ jf, w7 @ jf, 2), 0)
    pair["rp"] = side_by_side(blocks((w7 @ jf).T, ez), blocks((k7 @ jf).T, ez))
    pair["bzrp"] = z_back(s3[1:-1], q, ez) @ pair["rp"]
    pair["pxy"] = np.kron(blocks(jf, 2), blocks(jf, 2))
    pair["pz"] = blocks(jf.T, ez)

    def factor_rows(elements, scale):
        table = np.zeros((len(elements), 16))
        for at, (ex, ey) in enumerate(elements):
            for d in range(3):
                if scale[d] is not None:
                    table[at, d * 4 + ex * 2 + ey] = scale[d][at]
        return table

    def grid_elements(per):
        return [(x // per, y // per) for x in range(2 * per) for y in range(2 * per)]

    def direction_rows(elements):
        one = np.ones(len(elements))
        return np.concatenate([factor_rows(elements, [one if d == e else None for e in range(3)]) for d in range(3)], 0)

    spread = lambda per: np.kron(np.eye(ez), np.ones((1, per)))
    plain["e7"] = (direction_rows(grid_elements(p)), BF)
    plain["e3"] = (direction_rows(grid_elements(q)), BF)
    plain["e1"] = (direction_rows(grid_elements(2)), BF)
    plain["s64"] = (spread(p), BF)
    plain["s32"] = (spread(q), BF)
    plain["s256"] = (corner_columns(np.ones((1, 2)), ez), BF)
    plain["s80"] = (spread(modes), BF)
    pair["sl80"] = spread(modes) * np.tile(l7, ez)[None]

    m3 = q + 2
    ext = np.zeros((4, m3, 6 * q))
    for element in range(4):
        start = q * (element + 1)
        ext[element, 0, start - 2] += 1
        for at in range(q):
            ext[element, 1 + at, start + at] += 1
        ext[element, 1, start - 1] += 1
        ext[element, q, start + q] += 1
        ext[element, q + 1, start + q + 1] += 1
    a1m = blocks(s3.T, 4) @ ext.reshape(4 * m3, 6 * q)
    order = RING + ((0, 0),)
    span = lambda d: slice((d + 1) * 2 * q, (d + 2) * 2 * q)
    wm = [np.kron(a1m[:, span(dx)], a1m[:, span(dy)]) for dx, dy in order]
    pair["wmn"] = np.concatenate(wm[:8], 1)
    pair["wmo"] = wm[8]
    pair["azm"] = (blocks(s3.T, ez) @ line_extension(q, ez, True)).T
    inner3 = s3[1:-1]
    raw3 = blocks(inner3, 4)
    back3 = np.array(raw3[q : 3 * q])
    for at in (q - 1, 2 * q - 1, 3 * q - 1):
        total = raw3[at] + raw3[at + 1]
        for row in (at, at + 1):
            if q <= row < 3 * q:
                back3[row - q] = total
    bm = np.kron(back3, back3)
    pair["bm"] = bm
    bzm = z_back(inner3, q, ez)
    pair["bzm"] = bzm
    ll = np.concatenate(three(jm.T @ k3, jm.T @ w3, 2), 0)
    pair["lb"] = np.concatenate([ll @ ((wt3[:, 0] + extra)[:, None] * bm) for extra in (0, wt3[:, 1], wt3[:, 2])], 0)
    pair["rb"] = bzm @ np.concatenate([corner_columns(w3 @ jm, ez), corner_columns(k3 @ jm, ez)], 1)
    pair["jl"] = np.kron(blocks(jm.T, 2), blocks(jm.T, 2))
    pair["rj"] = corner_columns(jm, ez)
    place = {direction: at for at, direction in enumerate(order)}

    def ring_row(ex, ey, d):
        dx, dy = ex // 2 - 1, ey // 2 - 1
        return place[(dx, dy)] * 16 + d * 4 + (ex % 2) * 2 + ey % 2

    ld3, le3 = np.zeros((576, 144)), np.zeros((576, 144))
    for x in range(24):
        for y in range(24):
            ex, ey = x // m3 + 1, y // m3 + 1
            ld3[x * 24 + y, ring_row(ex, ey, 0)] = l3[x % m3]
            ld3[x * 24 + y, ring_row(ex, ey, 1)] = l3[y % m3]
            le3[x * 24 + y, ring_row(ex, ey, 2)] = 1
    ld9, le9 = np.zeros((count * count, 144)), np.zeros((count * count, 144))
    for x in range(count):
        for y in range(count):
            ex, ey = x // modes + 1, y // modes + 1
            ex = ex if ex < 3 else 7 - ex
            ld9[x * count + y, ring_row(ex, ey, 0)] = l7[x % modes]
            ld9[x * count + y, ring_row(ex, ey, 1)] = l7[y % modes]
            le9[x * count + y, ring_row(ex, ey, 2)] = 1
    pair["ld9"] = ld9 + le9
    pair["ld3"] = ld3 + le3
    plain["s48"] = (spread(m3), BF)
    pair["sl48"] = spread(m3) * np.tile(l3, ez)[None]
    er = np.zeros((3, 9, 2 * q, 2 * q, 144))
    for at in range(9):
        for x in range(2 * q):
            for y in range(2 * q):
                for d in range(3):
                    er[d, at, x, y, at * 16 + d * 4 + (x // q) * 2 + y // q] = 1
    plain["er"] = (er.reshape(3 * 576, 144), BF)
    pair["k3"] = np.concatenate(three(k3, w3, 2), 0)
    pair["rk3"] = side_by_side(blocks(w3, ez), blocks(k3, ez))
    corner_line = lambda table: np.kron(np.eye(6), table)
    modes_of = [a1m @ corner_line(table) for table in (k3 @ jm, w3 @ jm)]
    pair["wl"] = np.concatenate(
        [np.kron(modes_of[left], modes_of[right]) for left, right in ((0, 1), (1, 0), (1, 1))], 1
    )
    pair["ra3"] = side_by_side(
        blocks((w3 @ jm).T, ez) @ pair["azm"], blocks((k3 @ jm).T, ez) @ pair["azm"]
    )
    spread_vertices, spread_factors = np.zeros((144, 128)), np.zeros((3, 144, 144))
    for row in range(144):
        (ex, cx), (ey, cy) = divmod(row // 12, 2), divmod(row % 12, 2)
        vx, vy = ex + cx, ey + cy
        column = (AHEAD.index(vx // 2 - 1) * 4 + vy // 2) * 8 + (vx % 2) * 2 + vy % 2
        spread_vertices[row, column] = 1
        for d in range(3):
            at = order.index((ex // 2 - 1, ey // 2 - 1))
            spread_factors[d, row, at * 16 + d * 4 + (ex % 2) * 2 + ey % 2] = 1
    plain["ev"] = (spread_vertices, BF)
    plain["ef"] = (spread_factors.reshape(432, 144), BF)
    corner_z = np.zeros((ez, 2 * ez))
    for element in range(ez):
        for at in range(2):
            corner_z[(element + at) % ez, 2 * element + at] = 1
    plain["cz"] = (np.tile(corner_z, (4, 1)), BF)
    plain["s16"] = (spread(2), BF)
    vertex_line = lambda table: np.array(
        [[table[at % q, v - at // q] if 0 <= v - at // q <= 1 else 0.0 for v in range(8)] for at in range(6 * q)]
    )
    plain1 = vertex_line(jm)

    def vertex_columns(left, right, dx, dy):
        table = np.zeros((64, 4, 4, 8))
        for iy in range(4):
            for ix, ahead in enumerate(AHEAD):
                for x in range(2):
                    for y in range(2):
                        table[:, ix, iy, x * 2 + y] = np.kron(
                            left[span(dx), (ahead + 1) * 2 + x], right[span(dy), iy * 2 + y]
                        )
        return table.reshape(64, 128)

    pair["jc"] = vertex_columns(plain1, plain1, 0, 0)

    def z_vertices(table):
        result = np.zeros((ez, ez * q))
        for element in range(ez):
            for at in range(q):
                result[element, element * q + at] += table[at, 0]
                result[(element + 1) % ez, element * q + at] += table[at, 1]
        return np.tile(result, (4, 1))

    pair["rcj"] = z_vertices(jm)
    mask, left = np.zeros((n_gy, 16, 128)), np.zeros((n_gy, 16, 16))
    for gy in range(n_gy):
        for row in range(16):
            vx, vy = row // 8 + row // 4 % 2, row // 2 % 2 + row % 2
            owner = gy + vy // 2
            if owner < n_gy:
                first = owner * 32 + (vx % 2) * 16 + (vy % 2) * 8
                mask[gy, row, first % 128 : first % 128 + 8] = 1
                left[gy, first // 128 + 4 * (vx // 2), row] = 1
    plain["mask"] = (mask.reshape(-1, 128), F32)
    plain["left"] = (left.reshape(-1, 16), BF)
    chosen = np.zeros((8, 32))
    select = np.zeros((32, 8))
    for lane in range(32):
        chosen[lane // 8, lane] = 1
        select[lane, lane % 8] = 1
    plain["chosen"] = (chosen, F32)
    plain["select"] = (select, BF)
    tables = {}
    for name, table in pair.items():
        table = fitted(np.asarray(table, np.float64), name in RIGHT)
        high = table.astype(ml_dtypes.bfloat16)
        rest = (table - high.astype(np.float64)).astype(ml_dtypes.bfloat16)
        if name in RIGHT:
            tables[name] = np.block([[high, rest], [high, np.zeros_like(rest)]])[None]
        else:
            tables[name] = np.stack([high, rest])
    for name, (table, kind) in plain.items():
        table = fitted(np.asarray(table), name in RIGHT)
        table = np.concatenate([table, table], 0) if name in RIGHT else table
        tables[name] = table.astype(ml_dtypes.bfloat16 if kind is BF else np.float32)[None]
    return tables


STAGES = (
    ("columns", "vo", "jxy", "jz", "s80", "sl80", "e7", "e3", "e1", "s64", "s32", "s256", "wz7", "chosen", "mask"),
    ("ld9", "vl", "az", "vb", "la", "bzra"),
    ("ld3", "s48", "sl48", "er"),
    (
        "wmo", "jl", "rj", "bz", "k7", "kz7", "wmn", "azm", "lb", "rb", "left", "bm", "bzm", "select",
        "rk3", "k3", "wl", "ra3", "ev", "ef", "cz", "s16", "jc", "rcj", "rp", "bzrp", "lp", "pxy", "pz",
    ),
)


def pack(tables):
    stacks, places = {}, {}
    for stage, names in enumerate(STAGES):
        for name in names:
            table = tables[name]
            key = (stage, table.dtype.name, table.shape[-1])
            parts = stacks.setdefault(key, [])
            at = sum(part.shape[0] for part in parts)
            height = -(-table.shape[1] // 16) * 16
            for part in table:
                parts.append(np.pad(part, ((0, height - part.shape[0]), (0, 0))))
            places[name] = (key, at, height, table.shape[1])
    keys = tuple(stacks)
    return keys, [np.concatenate(stacks[key], 0) for key in keys], places


class Table:
    def __init__(self, ref, place):
        _, self.at, self.height, self.rows = place
        self.ref = ref
        self.shape = (2, self.rows, ref.shape[-1])

    def __getitem__(self, part):
        part = 0 if part is Ellipsis else part
        return self.ref[self.at + part * self.height : self.at + part * self.height + self.rows, :]

    def piece(self, part, start, rows):
        return self.ref[pl.ds(self.at + part * self.height + start, rows), :]


def dot(a, b):
    return jnp.dot(a, b, preferred_element_type=F32)


def split(x):
    high = x.astype(BF)
    return high, (x - high.astype(F32)).astype(BF)


def wide(x, lanes=128):
    if x.shape[1] == lanes:
        return x
    return jnp.concatenate([x, jnp.zeros((x.shape[0], lanes - x.shape[1]), x.dtype)], 1)


def tall(x, rows):
    if x.shape[0] == rows:
        return x
    return jnp.concatenate([x, jnp.zeros((rows - x.shape[0], x.shape[1]), x.dtype)], 0)


def halves(x):
    middle = x.shape[1] // 2
    return x[:, :middle] + x[:, middle:]


def exactly(main, small, x):
    high, rest = split(x)
    return halves(dot(main, jnp.concatenate([high, rest], 1))) + dot(small, high)


def left3(table, x):
    return exactly(table[0], table[1], tall(x, table.shape[-1]))


def left2(table, x):
    return halves(dot(table[...], jnp.concatenate(split(tall(x, table.shape[-1])), 1)))


def terms3(table, x):
    x = tall(x, table.shape[-1])
    rows = table.shape[1] // 3
    first = exactly(table.piece(0, 0, 2 * rows), table.piece(1, 0, 2 * rows), x[:, 0:128])
    third = exactly(table.piece(0, 2 * rows, rows), table.piece(1, 2 * rows, rows), x[:, 128:256])
    return first[0:rows], first[rows:], third


def right3(x, table):
    return halves(right2(x, table))


def right2(x, table):
    return dot(jnp.concatenate(split(wide(x)), 1), table[...])


KEPT = {
    "fine_f": (768, 128), "mid_f": (192, 128), "low_f": (48, 256), "ring_f": (1728, 128), "inverse3": (576, 128), "wt7": (256, 128), "wt3": (64, 128), "base_mid": (64, 128),
    "base_low": (16, 256), "first_fine": (256, 128), "base_fine": (256, 128),
    "first_mid": (64, 128), "modal3": (576, 128), "base_ring": (576, 128),
    "ww7": (256, 128), "inverse9": (1600, 128), "corner_f": (432, 128), "modal9": (800, 256),
}


def cycle_kernel(keys, places, n_gx, n_gy, *refs):
    r_hbm, len_hbm, inv_hbm = refs[:3]
    count = len(keys)
    packed = refs[3 : 3 + count]
    out_fine, out_mid, out_low = refs[3 + count : 6 + count]
    stores = refs[6 + count : 6 + 2 * count]
    (
        r_ref, len_ref, inv_ref, rs, fs, hb1, rm, fm, rp, fp, hb2, hs1, hs2, rb, corner, held, gs, gb, cb, invs,
        send_sem, recv_sem, gsend, grecv, csend, crecv, isend, irecv, in_sem, table_sem,
    ) = refs[6 + 2 * count : -len(KEPT)]
    gx, gy = lax.axis_index("gx"), lax.axis_index("gy")
    last = n_gy - 1
    barrier = pltpu.get_barrier_semaphore()

    def greet(ahead, row):
        pl.semaphore_signal(
            barrier, inc=1, device_id=(lax.rem(gx + (ahead + n_gx), n_gx), row), device_id_type=MESH
        )

    def greet_if(row, *columns):
        @pl.when((row >= 0) & (row <= last))
        def _():
            for ahead in columns:
                greet(ahead, row)

    def other_row(flips):
        row = gy
        for bit in (8, 4, 2, 1):
            if flips & bit:
                row = row + bit * (1 - 2 * (gy // bit % 2))
        return row

    def greet_rows(*several):
        for flips in several:
            if flips < n_gy:
                greet(-1, other_row(flips))
                if flips:
                    greet(0, other_row(flips))

    greet_rows(12, 13, 10, 11, 14, 15, 8, 9)
    greet_if(gy + 1, 1)
    greet_if(gy - 1, 1)
    greet(1, gy)
    greet(2, gy)
    greet_rows(4, 5, 2, 3, 6, 7, 1, 0)
    inputs = [
        pltpu.make_async_copy(source, target, in_sem.at[at])
        for at, (source, target) in enumerate(((len_hbm, len_ref), (r_hbm, r_ref), (inv_hbm, inv_ref)))
    ]
    loads = [pltpu.make_async_copy(packed[at], stores[at], table_sem.at[at]) for at in range(count)]
    for load in inputs:
        load.start()

    def fetch(*stages):
        for key, load in zip(keys, loads):
            if key[0] in stages:
                load.start()

    fetch(0)

    def ready(stage):
        for key, load in zip(keys, loads):
            if key[0] == stage:
                load.wait()

    kept = dict(zip(KEPT, refs[-len(KEPT) :]))

    def keep(name, value):
        kept[name][...] = value
        return kept[name]

    t = {name: Table(stores[keys.index(place[0])], place) for name, place in places.items()}
    at_bottom, at_top = gy == 0, gy == last
    not_bottom, not_top = gy > 0, gy < last
    sent = {0: None, 1: not_bottom, 2: not_top}

    def guarded(condition, action):
        if condition is None:
            action()
        else:
            pl.when(condition)(action)

    def exchange(phase, source, buffer, rows):
        at = offsets(rows)

        def group(number):
            def action():
                for index in range(*GROUPS[number]):
                    tx, ty = RING[index]
                    slot = RING.index((-tx, -ty))
                    landing = (0, 2, 1)[number]
                    pltpu.make_async_remote_copy(
                        src_ref=source(index),
                        dst_ref=buffer.at[pl.ds(at[slot], rows[slot])],
                        send_sem=send_sem.at[phase, number],
                        recv_sem=recv_sem.at[phase, landing],
                        device_id=(lax.rem(gx + (tx + n_gx), n_gx), gy + ty),
                        device_id_type=MESH,
                    ).start()

            return action

        for number in (1, 2, 0):
            guarded(sent[number], group(number))

    def settle(phase, sems, buffer, rows):
        at = offsets(rows)
        for number in range(3):
            first, end = GROUPS[number]
            piece = buffer.at[pl.ds(at[first], at[end] - at[first])]
            guarded(sent[number], lambda: pltpu.make_async_copy(piece, piece, sems.at[phase, number]).wait())

    def clear(number):
        first, end = GROUPS[number]
        for buffer, rows in (
            (fs, BLOCK_ROWS), (hb1, WIDE_ROWS), (rp, BLOCK_ROWS), (fp, BLOCK_ROWS), (hb2, WIDE_ROWS),
        ):
            at = offsets(rows)
            buffer[at[first] : at[end], :] = jnp.zeros((at[end] - at[first], buffer.shape[1]), buffer.dtype)

    @pl.when(at_bottom)
    def _():
        clear(1)
        invs[0:32, :] = jnp.zeros((32, invs.shape[1]), BF)

    @pl.when(at_top)
    def _():
        clear(2)
        invs[64:96, :] = jnp.zeros((32, invs.shape[1]), BF)

    @pl.when(gy >= last - 1)
    def _():
        invs[96:128, :] = jnp.zeros((32, invs.shape[1]), BF)

    at_wide = offsets(WIDE_ROWS)

    def mirrored(values):
        return jnp.concatenate([values[(15 - x) * 16 : (16 - x) * 16] for x in range(16)], 0)

    def wide_halo(field, stage):
        for x in range(16):
            rb[x] = field[15 - x]
        for index, (tx, ty) in enumerate(RING):
            source, ys = (rb if tx < 0 else field), (6, 0)[ty < 0]
            if 0 not in (tx, ty):
                corner[48:64, :] = jnp.zeros((16, 128), F32)
            for pair in range(5):
                xa, ya = 6 + 2 * pair, ys + 2 * pair
                at = at_wide[index] + pair * 16
                if ty == 0:
                    layers = source[xa, :, :], source[xa + 1, :, :]
                    stage[at : at + 16, :] = jnp.concatenate(layers, 1).astype(stage.dtype)
                elif tx == 0:
                    rows = [jnp.concatenate([field[0:8, y, :], rb[0:8, y, :]], 1) for y in (ya, ya + 1)]
                    stage[at : at + 16, :] = jnp.concatenate(rows, 0).astype(stage.dtype)
                else:
                    layers = source[6:16, ya, :], source[6:16, ya + 1, :]
                    corner[pair * 10 : pair * 10 + 10, :] = jnp.concatenate(layers, 1)
            if 0 not in (tx, ty):
                stage[at_wide[index] : at_wide[index + 1], :] = corner[...].astype(stage.dtype)

    def side_values(buffer):
        plain, turned_back = {}, {}
        for index, direction in enumerate(RING):
            piece = buffer[at_wide[index] : at_wide[index + 1], :]
            plain[direction] = piece
            turned_back[direction] = pltpu.roll(piece.astype(F32), 64, 1).astype(BF)
        ends, flanks = LOW_SIDE[:3], LOW_SIDE[3:]
        opposite = [(-dx, dy) for dx, dy in ends]
        low_part = [plain[d] for d in ends + flanks] + [turned_back[d] for d in ends + flanks]
        high_part = [plain[d] for d in opposite] + [turned_back[d] for d in flanks]
        high_part += [turned_back[d] for d in opposite] + [plain[d] for d in flanks]
        return jnp.concatenate([tall(jnp.concatenate(part, 0), 768) for part in (low_part, high_part)], 1)

    def fold(block):
        result = block[0:16]
        for part in range(1, 4):
            result = result + pltpu.roll(block[part * 16 : part * 16 + 16], part * 32, 1)
        return result

    def spread_blocks(folded, blocks_ref):
        for part in range(4):
            turned_back = pltpu.roll(folded[0:128, :], (128 - part * 32) % 128, 1) if part else folded[0:128, :]
            for slot in range(8):
                blocks_ref[slot * 64 + part * 16 : slot * 64 + part * 16 + 16, :] = turned_back[
                    slot * 16 : slot * 16 + 16
                ]


    inputs[0].wait()
    own_f = 8 * 16
    for ex in range(2):
        a, b, c = len_ref[0, ex], len_ref[1, ex], len_ref[2, ex]
        fs[own_f + ex * 2 : own_f + ex * 2 + 2, :] = wide(b * c / (2.0 * a))
        fs[own_f + 4 + ex * 2 : own_f + 6 + ex * 2, :] = wide(a * c / (2.0 * b))
        fs[own_f + 8 + ex * 2 : own_f + 10 + ex * 2, :] = wide(a * b / (2.0 * c))
    fs[own_f + 12 : own_f + 16, :] = jnp.zeros((4, 128), F32)
    inputs[1].wait()
    wide_halo(r_ref, hs1)
    near = jnp.minimum(gy + 1, last) - jnp.maximum(gy - 1, 0) + 1
    pl.semaphore_wait(barrier, 2 * n_gy + near)
    exchange(0, lambda index: fs.at[pl.ds(own_f, 16)], fs, BLOCK_ROWS)
    exchange(1, lambda index: hs1.at[pl.ds(at_wide[index], WIDE_ROWS[index])], hb1, WIDE_ROWS)
    fetch(1, 2)
    inputs[2].wait()
    invs[32:64, :] = inv_ref[0]
    reach = ((1, 0, not_top, not_bottom), (-1, 2, not_bottom, not_top), (-2, 3, gy > 1, gy < last - 1))

    def inverse_copy(at):
        step, slot, _, _ = reach[at]
        return pltpu.make_async_remote_copy(
            src_ref=invs.at[pl.ds(32, 32)],
            dst_ref=invs.at[pl.ds(slot * 32, 32)],
            send_sem=isend.at[at],
            recv_sem=irecv.at[at],
            device_id=(gx, gy + step),
            device_id_type=MESH,
        )

    for at in range(3):
        pl.when(reach[at][2])(lambda: inverse_copy(at).start())

    bottom_on = jnp.where(at_bottom, 1.0, 0.0)
    top_on = jnp.where(at_top, 1.0, 0.0)

    ready(0)
    columns = t["columns"][...]

    def wall_weight(rows, at):
        piece = columns[0:rows]
        return piece[:, at : at + 1] + bottom_on * piece[:, at + 1 : at + 2] + top_on * piece[:, at + 2 : at + 3]

    wt7 = keep("wt7", jnp.broadcast_to(wall_weight(256, 0), (256, 128)))
    wt3 = keep("wt3", jnp.broadcast_to(wall_weight(64, 6), (64, 128)))
    ww7 = keep("ww7", jnp.broadcast_to(columns[:, 9:10], (256, 128)))
    r = wide(r_ref[...].reshape(256, 64))
    f_own = wide(fs[own_f : own_f + 16, :])
    modal9 = keep("modal9", left3(t["vo"], jnp.concatenate([r, mirrored(r)], 1)))
    base_mid = keep("base_mid", right3(left3(t["jxy"], r), t["jz"]))
    fine_f = keep("fine_f", left2(t["e7"], right2(f_own, t["s64"])))
    mid_f = keep("mid_f", left2(t["e3"], right2(f_own, t["s32"])))
    low_f = keep("low_f", left2(t["e1"], right2(f_own, t["s256"])))

    def ring_modes(buffer):
        modal = modal9[...] + dot(t["vl"][...], side_values(buffer))
        modal = right3(jnp.concatenate([modal[:, 0:128], modal[:, 128:256]], 0), t["az"]) * inverse9[...]
        return jnp.concatenate([modal[0:800], modal[800:1600]], 1)

    def joined(values):
        return values[:, 0:128] + mirrored(values[:, 128:256])

    ready(1)
    fetch(3)
    settle(0, recv_sem, fs, BLOCK_ROWS)
    ring_l = wide(fs[...])
    kind = lax.broadcasted_iota(jnp.int32, (144, 128), 0) % 16 // 4
    d9 = left3(t["ld9"], jnp.where(kind == 2, right3(ring_l, t["sl80"]), right2(ring_l, t["s80"])))
    inverse9 = keep("inverse9", jnp.where(d9 > 0.0, 1.0 / d9, 0.0))
    settle(1, recv_sem, hb1, WIDE_ROWS)
    local = joined(left3(t["vb"], ring_modes(hb1))) * wt7[...]
    terms = terms3(t["la"], right3(local, t["bzra"]))
    residual_mid = base_mid[...] - (mid_f[0:64] * terms[0] + mid_f[64:128] * terms[1] + mid_f[128:192] * terms[2])
    rp[128:144, :] = fold(residual_mid)
    exchange(3, lambda index: rp.at[pl.ds(128, 16)], rp, BLOCK_ROWS)
    rm[512:576, :] = residual_mid

    ready(2)
    ready(3)
    ring_l = wide(fs[...])
    d3 = left3(t["ld3"], jnp.where(kind == 2, right3(ring_l, t["sl48"]), right2(ring_l, t["s48"])))
    inverse3 = keep("inverse3", jnp.where(d3 > 0.0, 1.0 / d3, 0.0))
    own_modal = keep("modal3", left3(t["wmo"], residual_mid))
    base_low = keep("base_low", right3(left3(t["jl"], residual_mid), t["rj"]))
    first_fine = keep("first_fine", right3(local, t["bz"]))
    massed = left3(t["k7"], first_fine[...] * t["wz7"][...][0:1])
    along_z = right3(first_fine[...], t["kz7"]) * ww7[...]
    base_fine = keep(
        "base_fine",
        wide(r_ref[...].reshape(256, 64))
        - (fine_f[0:256] * massed[0:256] + fine_f[256:512] * massed[256:512] + fine_f[512:768] * along_z),
    )

    settle(3, recv_sem, rp, BLOCK_ROWS)
    spread_blocks(rp, rm)
    modal3 = own_modal[...] + left3(t["wmn"], rm[0:512, :])
    modal3 = right3(modal3, t["azm"]) * inverse3[...]
    variant = jnp.where(at_bottom, 1, jnp.where(at_top, 2, 0))
    rows = pl.multiple_of(variant * 48, 16)
    low = exactly(t["lb"].piece(0, rows, 48), t["lb"].piece(1, rows, 48), tall(modal3, t["lb"].shape[-1]))
    low = right3(low, t["rb"])
    low = base_low[...] - (
        low_f[0:16] * low[0:16, 0:256] + low_f[16:32] * low[16:32, 0:256] + low_f[32:48] * low[32:48, 256:512]
    )
    wall = pl.multiple_of(gy * 16, 16)
    low = tall(halves(low) * t["mask"].piece(0, wall, 16), 128)
    message = halves(dot(t["left"].piece(0, wall, 16), jnp.concatenate(split(low), 1)))[0:8]
    gs[...] = message

    def send_slab(flips, ahead):
        row = other_row(flips)
        pltpu.make_async_remote_copy(
            src_ref=gs,
            dst_ref=gb.at[flips + (n_gy - 1 if ahead else -1)],
            send_sem=gsend,
            recv_sem=grecv,
            device_id=(lax.rem(gx + ahead, n_gx), row),
            device_id_type=MESH,
        ).start()

    for flips in (12, 13, 10, 11, 14, 15, 8, 9, 4, 5, 2, 3, 6, 7, 1, 0):
        if flips < n_gy:
            send_slab(flips, 1)
            if flips:
                send_slab(flips, 0)

    first_mid = keep("first_mid", right3(left3(t["bm"], modal3) * wt3[...], t["bzm"]))
    fm[512:576, :] = first_mid[...]
    fp[128:144, :] = fold(first_mid[...])
    exchange(4, lambda index: fp.at[pl.ds(128, 16)], fp, BLOCK_ROWS)

    for at in range(3):
        pl.when(reach[at][3])(lambda: inverse_copy(at).wait_recv())
    pltpu.make_async_copy(gb, gb, grecv).wait()
    here = gs[...] + jnp.sum(gb[0 : n_gy - 1], axis=0)
    behind = jnp.sum(gb[n_gy - 1 :], axis=0)
    chunks = inv_ref.shape[2] // 128
    vector = here + pltpu.roll(behind, 4, 0)
    row = lax.broadcasted_iota(jnp.int32, (8, 128), 0)
    vector = jnp.concatenate([jnp.where(row == chunk, vector, 0.0) for chunk in range(chunks)], 1)
    vector = tall(vector, 16).astype(BF)
    solved = lax.dot_general(vector, invs[...], (((1,), (1,)), ((), ())), preferred_element_type=F32)
    solved = jnp.broadcast_to(jnp.sum(solved, axis=0, keepdims=True), (8, 128))
    chosen = t["chosen"][...]
    for iy in range(4):
        cb[96 + iy * 8 : 104 + iy * 8, :] = (pltpu.roll(solved, 128 - iy * 32, 1) if iy else solved) * chosen
    for ix in (2, 1, 0):
        pltpu.make_async_remote_copy(
            src_ref=cb.at[pl.ds(96, 32)],
            dst_ref=cb.at[pl.ds(ix * 32, 32)],
            send_sem=csend,
            recv_sem=crecv,
            device_id=(lax.rem(gx - AHEAD[ix] + n_gx, n_gx), gy),
            device_id_type=MESH,
        ).start()

    others = cb.at[pl.ds(0, 96)]

    ring_l = wide(fs[...])
    ring_f = keep("ring_f", left2(t["er"], right2(ring_l, t["s32"])))
    corner_f = keep("corner_f", left2(t["ef"], right2(ring_l, t["s16"])))
    low_out = right2(tall(cb[104:112, :], 16), t["select"])
    out_low[0] = low_out[0:2, 0:8]
    out_low[1] = low_out[2:4, 0:8]
    settle(4, recv_sem, fp, BLOCK_ROWS)
    spread_blocks(fp, fm)
    turned = right3(fm[...], t["rk3"])
    parts = []
    for at in range(9):
        piece = terms3(t["k3"], turned[at * 64 : (at + 1) * 64])
        parts.append(
            rm[at * 64 : (at + 1) * 64, :]
            - (
                ring_f[at * 64 : (at + 1) * 64] * piece[0]
                + ring_f[576 + at * 64 : 576 + (at + 1) * 64] * piece[1]
                + ring_f[1152 + at * 64 : 1152 + (at + 1) * 64] * piece[2]
            )
        )
    base_ring = keep("base_ring", jnp.concatenate(parts, 0))
    modal3 = left3(t["wmn"], base_ring[0:512]) + left3(t["wmo"], base_ring[512:576])
    modal3 = keep("modal3", right3(modal3, t["azm"]))

    pltpu.make_async_copy(others, others, crecv).wait()
    corrections = wide(cb[...])
    change = left2(t["ev"], right2(corrections, t["cz"]))
    change = right3(jnp.concatenate([change * corner_f[at * 144 : at * 144 + 144] for at in range(3)], 0), t["ra3"])
    change = jnp.concatenate([change[0:288, 0:128], change[288:432, 128:256]], 0)
    modal3 = (modal3[...] - left3(t["wl"], change)) * inverse3[...]
    held[0:64, :] = first_mid[...] + right3(left3(t["jc"], corrections), t["rcj"])
    smoothed = left3(t["bm"], modal3) * wt3[...]

    turned = terms3(t["lp"], right3(smoothed, t["bzrp"]) + right3(held[0:64, :], t["rp"]))
    residual = base_fine[...] - (
        fine_f[0:256] * turned[0]
        + fine_f[256:512] * turned[1]
        + fine_f[512:768] * turned[2]
    )
    rs[...] = residual[:, 0:64].reshape(16, 16, 64)
    wide_halo(rs, hs2)
    exchange(5, lambda index: hs2.at[pl.ds(at_wide[index], WIDE_ROWS[index])], hb2, WIDE_ROWS)
    mid_result = held[0:64, :] + right3(smoothed, t["bzm"])
    out_mid[...] = mid_result[:, 0:32].reshape(8, 8, 32)
    modal9 = keep("modal9", dot(t["vo"][0], jnp.concatenate([residual, mirrored(residual)], 1).astype(BF)))
    held[...] = first_fine[...] + right3(left3(t["pxy"], mid_result), t["pz"])
    settle(5, recv_sem, hb2, WIDE_ROWS)
    local = joined(dot(t["vb"][0], tall(ring_modes(hb2), 896).astype(BF))) * wt7[...]
    result = held[...] + right3(local, t["bz"])
    out_fine[...] = result[:, 0:64].reshape(16, 16, 64)

    for phase, buffer, rows in (
        (0, fs, BLOCK_ROWS), (1, hb1, WIDE_ROWS), (3, rp, BLOCK_ROWS), (4, fp, BLOCK_ROWS), (5, hb2, WIDE_ROWS),
    ):
        settle(phase, send_sem, buffer, rows)
    pltpu.make_async_copy(gb, gb, gsend).wait()
    pltpu.make_async_copy(others, others, csend).wait()
    for at in range(3):
        pl.when(reach[at][2])(lambda: inverse_copy(at).wait_send())


def hand_over(*refs):
    copies = [pltpu.make_async_copy(refs[at], refs[3 + at], refs[6].at[at]) for at in range(3)]
    for copy in copies:
        copy.start()
    for copy in copies:
        copy.wait()


def shards(n_gx, n_gy, local_residual, lengths, coarse_inverse):
    keys, packed, places = pack(build_tables(n_gy, lengths.shape[3]))
    vmem = pl.BlockSpec(memory_space=pltpu.VMEM)
    scratch = [pltpu.VMEM(table.shape, BF if key[1] == "bfloat16" else F32) for key, table in zip(keys, packed)]
    scratch += [
        pltpu.VMEM(local_residual.shape, F32),
        pltpu.VMEM(lengths.shape, F32),
        pltpu.VMEM(coarse_inverse.shape, BF),
        pltpu.VMEM((16, 16, 64), F32),
        pltpu.VMEM((144, 128), F32),
        pltpu.VMEM((576, 128), BF),
        pltpu.VMEM((576, 128), F32),
        pltpu.VMEM((576, 128), F32),
        pltpu.VMEM((144, 128), F32),
        pltpu.VMEM((144, 128), F32),
        pltpu.VMEM((576, 128), BF),
        pltpu.VMEM((576, 128), BF),
        pltpu.VMEM((576, 128), BF),
        pltpu.VMEM((16, 16, 64), F32),
        pltpu.VMEM((64, 128), F32),
        pltpu.VMEM((256, 128), F32),
        pltpu.VMEM((8, 128), F32),
        pltpu.VMEM((2 * n_gy - 1, 8, 128), F32),
        pltpu.VMEM((128, 128), F32),
        pltpu.VMEM((128, coarse_inverse.shape[2]), BF),
        pltpu.SemaphoreType.DMA((6, 3)),
        pltpu.SemaphoreType.DMA((6, 3)),
        pltpu.SemaphoreType.DMA,
        pltpu.SemaphoreType.DMA,
        pltpu.SemaphoreType.DMA,
        pltpu.SemaphoreType.DMA,
        pltpu.SemaphoreType.DMA((3,)),
        pltpu.SemaphoreType.DMA((3,)),
        pltpu.SemaphoreType.DMA((3,)),
        pltpu.SemaphoreType.DMA((len(keys),)),
    ]
    scratch += [pltpu.VMEM(shape, F32) for shape in KEPT.values()]
    outs = pl.pallas_call(
        functools.partial(cycle_kernel, keys, places, n_gx, n_gy),
        out_shape=(
            jax.ShapeDtypeStruct((16, 16, 64), F32),
            jax.ShapeDtypeStruct((8, 8, 32), F32),
            jax.ShapeDtypeStruct((2, 2, 8), F32),
        ),
        in_specs=[pl.BlockSpec(memory_space=pl.ANY)] * (3 + len(keys)),
        out_specs=(vmem, vmem, vmem),
        scratch_shapes=scratch,
        compiler_params=pltpu.CompilerParams(collective_id=0, has_side_effects=True, vmem_limit_bytes=60 * 1024 * 1024),
    )(local_residual, lengths, coarse_inverse, *[jnp.asarray(table) for table in packed])
    return pl.pallas_call(
        hand_over,
        out_shape=tuple(jax.ShapeDtypeStruct(out.shape, out.dtype) for out in outs),
        in_specs=[vmem] * 3,
        out_specs=[pl.BlockSpec(memory_space=pl.ANY)] * 3,
        scratch_shapes=[pltpu.SemaphoreType.DMA((3,))],
    )(*outs)


def solution(mesh):
    in_specs = (P("gx", "gy", None), P(None, "gx", "gy", None), P("gx", "gy", None))
    out_specs = (P("gx", "gy", None), P("gx", "gy", None), P("gx", "gy", None))
    return jax.shard_map(
        functools.partial(shards, mesh.shape["gx"], mesh.shape["gy"]),
        mesh=mesh,
        in_specs=in_specs,
        out_specs=out_specs,
        check_vma=False,
    )
```

```python
import functools
import math

import jax
import jax.numpy as jnp
import ml_dtypes
import numpy as np
from jax import lax
from jax.experimental import pallas as pl
from jax.experimental.pallas import tpu as pltpu
from jax.sharding import PartitionSpec as P

ORDER = 7
MID_ORDER = 3


def legendre_pair(order, point):
    older = 1.0
    newer = point
    for degree in range(2, order + 1):
        nexter = ((2 * degree - 1) * point * newer - (degree - 1) * older) / degree
        older = newer
        newer = nexter
    return (newer, older)


def jacobi_eigen(matrix):
    count_n = len(matrix)
    work = [list(row_items) for row_items in matrix]
    vectors = [
        [1.0 if row_at == col_at else 0.0 for col_at in range(count_n)] for row_at in range(count_n)
    ]
    for sweep_count in range(60):
        for lower_at in range(count_n):
            for upper_at in range(lower_at + 1, count_n):
                off_value = work[lower_at][upper_at]
                if abs(off_value) < 1e-18 * (
                    abs(work[lower_at][lower_at]) + abs(work[upper_at][upper_at])
                ):
                    continue
                angle_ratio = (work[upper_at][upper_at] - work[lower_at][lower_at]) / (
                    2.0 * off_value
                )
                sign_value = 1.0 if angle_ratio >= 0 else -1.0
                tangent = sign_value / (
                    abs(angle_ratio) + math.sqrt(angle_ratio * angle_ratio + 1.0)
                )
                cosine = 1.0 / math.sqrt(tangent * tangent + 1.0)
                sine_value = tangent * cosine
                for other_at in range(count_n):
                    left_value = work[other_at][lower_at]
                    right_value = work[other_at][upper_at]
                    work[other_at][lower_at] = cosine * left_value - sine_value * right_value
                    work[other_at][upper_at] = sine_value * left_value + cosine * right_value
                for other_at in range(count_n):
                    left_value = work[lower_at][other_at]
                    right_value = work[upper_at][other_at]
                    work[lower_at][other_at] = cosine * left_value - sine_value * right_value
                    work[upper_at][other_at] = sine_value * left_value + cosine * right_value
                for other_at in range(count_n):
                    left_value = vectors[other_at][lower_at]
                    right_value = vectors[other_at][upper_at]
                    vectors[other_at][lower_at] = cosine * left_value - sine_value * right_value
                    vectors[other_at][upper_at] = sine_value * left_value + cosine * right_value
    eigen_list = [work[row_at][row_at] for row_at in range(count_n)]
    ordering = sorted(range(count_n), key=lambda index_at: eigen_list[index_at])
    rates = [eigen_list[index_at] for index_at in ordering]
    basis = [[vectors[row_at][index_at] for index_at in ordering] for row_at in range(count_n)]
    return (rates, basis)


def gll_tables(order):
    point_count = order + 1
    node_list = []
    for node_at in range(point_count):
        point = math.cos(math.pi * node_at / order)
        for newton_step in range(100):
            top_value, lower_value = legendre_pair(order, point)
            point = point - (point * top_value - lower_value) / ((order + 1) * top_value)
        node_list.append(point)
    node_list = node_list[::-1]
    node_list[0] = -1.0
    node_list[-1] = 1.0
    values = [legendre_pair(order, point)[0] for point in node_list]
    weight_list = [2.0 / (order * (order + 1) * value_at**2) for value_at in values]
    derivative = [[0.0] * point_count for row_at in range(point_count)]
    for row_at in range(point_count):
        for col_at in range(point_count):
            if row_at != col_at:
                derivative[row_at][col_at] = values[row_at] / (
                    values[col_at] * (node_list[row_at] - node_list[col_at])
                )
    derivative[0][0] = -order * (order + 1) / 4.0
    derivative[order][order] = order * (order + 1) / 4.0
    stiff_list = [
        [
            sum(
                (
                    derivative[inner_at][row_at]
                    * weight_list[inner_at]
                    * derivative[inner_at][col_at]
                    for inner_at in range(point_count)
                )
            )
            for col_at in range(point_count)
        ]
        for row_at in range(point_count)
    ]
    extent = 3 * order + 1
    big_stiff = [[0.0] * extent for row_at in range(extent)]
    big_mass = [0.0] * extent
    for offset_at in (0, order, 2 * order):
        for row_at in range(point_count):
            big_mass[offset_at + row_at] += weight_list[row_at]
            for col_at in range(point_count):
                big_stiff[offset_at + row_at][offset_at + col_at] += stiff_list[row_at][col_at]
    chosen = list(range(order - 1, 2 * order + 2))
    root_mass = [1.0 / math.sqrt(big_mass[index_at]) for index_at in chosen]
    scaled = [
        [
            root_mass[row_at] * big_stiff[chosen[row_at]][chosen[col_at]] * root_mass[col_at]
            for col_at in range(len(chosen))
        ]
        for row_at in range(len(chosen))
    ]
    rates, basis = jacobi_eigen(scaled)
    eigen_basis = [
        [root_mass[row_at] * basis[row_at][col_at] for col_at in range(len(chosen))]
        for row_at in range(len(chosen))
    ]
    return (
        np.array(node_list),
        np.array(weight_list),
        np.array(stiff_list),
        np.array(eigen_basis),
        np.array(rates),
    )


def interp_table(fine_nodes, coarse_nodes):
    coarse_count = len(coarse_nodes)
    columns = []
    for column in range(coarse_count):
        factors_list = [
            (fine_nodes - coarse_nodes[other_node])
            / (coarse_nodes[column] - coarse_nodes[other_node])
            for other_node in range(coarse_count)
            if other_node != column
        ]
        columns.append(np.prod(np.stack(factors_list), axis=0))
    return np.stack(columns, axis=1)

BF = jnp.bfloat16
F32 = jnp.float32
RING = ((-1, 0), (1, 0), (0, -1), (-1, -1), (1, -1), (0, 1), (-1, 1), (1, 1))
GROUPS = ((0, 2), (2, 5), (5, 8))
AHEAD = (-1, 1, 2, 0)
BLOCK_ROWS = (16,) * 8
WIDE_ROWS = (80, 80, 80, 64, 64, 80, 64, 64)
LOW_SIDE = ((-1, 0), (-1, -1), (-1, 1), (0, -1), (0, 1))
MESH = pl.DeviceIdType.MESH


def offsets(rows):
    return tuple(int(at) for at in np.concatenate([[0], np.cumsum(rows)]))


def blocks(matrix, count):
    return np.kron(np.eye(count), matrix)


def line_extension(points, elements, periodic):
    size = elements * points
    width = size if periodic else size + 4
    table = np.zeros((elements, points + 2, width))

    def column(at):
        if periodic:
            return at % size
        if at < 0:
            return {-2: size, -1: size + 1}[at]
        if at >= size:
            return {size: size + 2, size + 1: size + 3}[at]
        return at

    for element in range(elements):
        start = element * points
        table[element, 0, column(start - 2)] += 1
        for at in range(points):
            table[element, 1 + at, start + at] += 1
        table[element, 1, column(start - 1)] += 1
        table[element, points, column(start + points)] += 1
        table[element, points + 1, column(start + points + 1)] += 1
    return table.reshape(elements * (points + 2), width)


def line_weights(points, elements):
    position = np.arange(points * elements) % points
    return np.where((position == 0) | (position == points - 1), 0.5, 1.0)


def z_back(inner, points, elements):
    table = blocks(inner, elements)
    total = np.array(table)
    size = points * elements
    for element in range(elements):
        low, high = element * points, (element * points - 1) % size
        total[low] = table[low] + table[high]
        total[high] = total[low]
    return (total * line_weights(points, elements)[:, None]).T


RIGHT = (
    "az", "bz", "bzra", "jz", "kz7", "rp", "pz", "azm", "bzm", "rb", "rj", "rk3", "ra3", "bzrp", "cz", "s16", "rcj",
    "s64", "s32", "s256", "s80", "sl80", "s48", "sl48", "select",
)


def fitted(table, right):
    rows, columns = table.shape[-2:]
    more = ((0, -rows % 128 if right else 0), (0, -columns % 128))
    return np.pad(table, ((0, 0),) * (table.ndim - 2) + more)


def side_by_side(*parts):
    return np.concatenate([np.pad(part, ((0, 0), (0, -part.shape[1] % 128))) for part in parts], 1)


def corner_columns(inner_table, elements):
    points = inner_table.shape[0]
    table = np.zeros((elements * points, 256))
    for corner in range(2):
        for lane in range(128):
            element = (lane % elements - corner) % elements
            table[element * points : (element + 1) * points, corner * 128 + lane] = inner_table[:, corner]
    return table


def build_tables(n_gy, ez):
    p, q = ORDER + 1, MID_ORDER + 1
    fine, mid, low = gll_tables(ORDER), gll_tables(MID_ORDER), gll_tables(1)
    jf = interp_table(fine[0], mid[0])
    jm = interp_table(mid[0], low[0])
    k7, w7, s7, l7 = fine[2], np.diag(fine[1]), fine[3], fine[4]
    k3, w3, s3, l3 = mid[2], np.diag(mid[1]), mid[3], mid[4]
    pair, plain = {}, {}
    modes = p + 2
    pair["az"] = (blocks(s7.T, ez) @ line_extension(p, ez, True)).T
    inner = s7[1:-1]
    bz = z_back(inner, p, ez)
    pair["bz"] = bz

    count = 4 * modes
    ext = np.zeros((4, modes, 36))
    for element in range(4):
        start = 2 + p * element
        ext[element, 0, start - 2] += 1
        for at in range(p):
            ext[element, 1 + at, start + at] += 1
        ext[element, 1, start - 1] += 1
        ext[element, p, start + p] += 1
        ext[element, p + 1, start + p + 1] += 1
    a1w = blocks(s7.T, 4) @ ext.reshape(count, 36)
    middle = a1w[:, 10:26]
    beside = {-1: a1w[:, 0:10], 1: a1w[:, 26:36]}
    near, parts = slice(0, 2 * modes), []
    for half in range(2):
        for dx, dy in LOW_SIDE:
            if dy == 0:
                pieces = [np.kron(beside[dx][near, at : at + 1], middle) for at in range(half, 10, 2)]
            elif dx == 0:
                columns = range(15, 7, -1) if half else range(8)
                pieces = [np.kron(middle[near][:, columns], beside[dy][:, at : at + 1]) for at in range(10)]
            else:
                pieces = [np.kron(beside[dx][near], beside[dy][:, at : at + 1]) for at in range(half, 10, 2)]
            piece = np.concatenate(pieces, 1)
            parts.append(np.pad(piece, ((0, 0), (0, -piece.shape[1] % 16))))
    plain["vl"] = (np.concatenate(parts, 1), BF)
    pair["vo"] = np.kron(middle[near], middle)
    raw = blocks(inner, 4)
    around = np.array(raw[p : 3 * p])
    for at in (p - 1, 2 * p - 1, 3 * p - 1):
        for row in (at, at + 1):
            if p <= row < 3 * p:
                around[row - p] = raw[at] + raw[at + 1]
    pair["vb"] = np.kron(around[:, near], around)

    def weights(points):
        line = line_weights(points, 2)
        low_side, high_side = np.zeros(2 * points), np.zeros(2 * points)
        low_side[0], high_side[-1] = 0.5, 0.5
        return np.stack([np.kron(line, line), np.kron(line, low_side), np.kron(line, high_side)], 1)

    wt7, wt3 = weights(p), weights(q)
    columns = np.zeros((256, 128))
    columns[:, 0:3] = wt7
    columns[:64, 6:9] = wt3
    columns[:, 9] = np.kron(np.tile(fine[1], 2), np.tile(fine[1], 2))
    plain["columns"] = (columns, F32)

    def three(stiff, mass, count):
        stiff, mass = blocks(stiff, count), blocks(mass, count)
        return np.kron(stiff, mass), np.kron(mass, stiff), np.kron(mass, mass)

    la = np.concatenate(three(jf.T @ k7, jf.T @ w7, 2), 0)
    ra = side_by_side(blocks(w7 @ jf, ez), blocks(k7 @ jf, ez))
    pair["la"] = la
    pair["bzra"] = bz @ ra
    pair["jxy"] = np.kron(blocks(jf.T, 2), blocks(jf.T, 2))
    pair["jz"] = blocks(jf, ez)
    k7x, k7y, _ = three(k7, w7, 2)
    pair["k7"] = np.concatenate([k7x, k7y], 0)
    pair["kz7"] = blocks(k7, ez)
    plain["wz7"] = (np.tile(np.tile(fine[1], ez)[None], (8, 1)), F32)
    pair["lp"] = np.concatenate(three(k7 @ jf, w7 @ jf, 2), 0)
    pair["rp"] = side_by_side(blocks((w7 @ jf).T, ez), blocks((k7 @ jf).T, ez))
    pair["bzrp"] = z_back(s3[1:-1], q, ez) @ pair["rp"]
    pair["pxy"] = np.kron(blocks(jf, 2), blocks(jf, 2))
    pair["pz"] = blocks(jf.T, ez)

    def factor_rows(elements, scale):
        table = np.zeros((len(elements), 16))
        for at, (ex, ey) in enumerate(elements):
            for d in range(3):
                if scale[d] is not None:
                    table[at, d * 4 + ex * 2 + ey] = scale[d][at]
        return table

    def grid_elements(per):
        return [(x // per, y // per) for x in range(2 * per) for y in range(2 * per)]

    def direction_rows(elements):
        one = np.ones(len(elements))
        return np.concatenate([factor_rows(elements, [one if d == e else None for e in range(3)]) for d in range(3)], 0)

    spread = lambda per: np.kron(np.eye(ez), np.ones((1, per)))
    plain["e7"] = (direction_rows(grid_elements(p)), BF)
    plain["e3"] = (direction_rows(grid_elements(q)), BF)
    plain["e1"] = (direction_rows(grid_elements(2)), BF)
    plain["s64"] = (spread(p), BF)
    plain["s32"] = (spread(q), BF)
    plain["s256"] = (corner_columns(np.ones((1, 2)), ez), BF)
    plain["s80"] = (spread(modes), BF)
    pair["sl80"] = spread(modes) * np.tile(l7, ez)[None]

    m3 = q + 2
    ext = np.zeros((4, m3, 6 * q))
    for element in range(4):
        start = q * (element + 1)
        ext[element, 0, start - 2] += 1
        for at in range(q):
            ext[element, 1 + at, start + at] += 1
        ext[element, 1, start - 1] += 1
        ext[element, q, start + q] += 1
        ext[element, q + 1, start + q + 1] += 1
    a1m = blocks(s3.T, 4) @ ext.reshape(4 * m3, 6 * q)
    order = RING + ((0, 0),)
    span = lambda d: slice((d + 1) * 2 * q, (d + 2) * 2 * q)
    wm = [np.kron(a1m[:, span(dx)], a1m[:, span(dy)]) for dx, dy in order]
    pair["wmn"] = np.concatenate(wm[:8], 1)
    pair["wmo"] = wm[8]
    pair["azm"] = (blocks(s3.T, ez) @ line_extension(q, ez, True)).T
    inner3 = s3[1:-1]
    raw3 = blocks(inner3, 4)
    back3 = np.array(raw3[q : 3 * q])
    for at in (q - 1, 2 * q - 1, 3 * q - 1):
        total = raw3[at] + raw3[at + 1]
        for row in (at, at + 1):
            if q <= row < 3 * q:
                back3[row - q] = total
    bm = np.kron(back3, back3)
    pair["bm"] = bm
    bzm = z_back(inner3, q, ez)
    pair["bzm"] = bzm
    ll = np.concatenate(three(jm.T @ k3, jm.T @ w3, 2), 0)
    pair["lb"] = np.concatenate([ll @ ((wt3[:, 0] + extra)[:, None] * bm) for extra in (0, wt3[:, 1], wt3[:, 2])], 0)
    pair["rb"] = bzm @ np.concatenate([corner_columns(w3 @ jm, ez), corner_columns(k3 @ jm, ez)], 1)
    pair["jl"] = np.kron(blocks(jm.T, 2), blocks(jm.T, 2))
    pair["rj"] = corner_columns(jm, ez)
    place = {direction: at for at, direction in enumerate(order)}

    def ring_row(ex, ey, d):
        dx, dy = ex // 2 - 1, ey // 2 - 1
        return place[(dx, dy)] * 16 + d * 4 + (ex % 2) * 2 + ey % 2

    ld3, le3 = np.zeros((576, 144)), np.zeros((576, 144))
    for x in range(24):
        for y in range(24):
            ex, ey = x // m3 + 1, y // m3 + 1
            ld3[x * 24 + y, ring_row(ex, ey, 0)] = l3[x % m3]
            ld3[x * 24 + y, ring_row(ex, ey, 1)] = l3[y % m3]
            le3[x * 24 + y, ring_row(ex, ey, 2)] = 1
    ld9, le9 = np.zeros((count * count, 144)), np.zeros((count * count, 144))
    for x in range(count):
        for y in range(count):
            ex, ey = x // modes + 1, y // modes + 1
            ex = ex if ex < 3 else 7 - ex
            ld9[x * count + y, ring_row(ex, ey, 0)] = l7[x % modes]
            ld9[x * count + y, ring_row(ex, ey, 1)] = l7[y % modes]
            le9[x * count + y, ring_row(ex, ey, 2)] = 1
    pair["ld9"] = ld9 + le9
    pair["ld3"] = ld3 + le3
    plain["s48"] = (spread(m3), BF)
    pair["sl48"] = spread(m3) * np.tile(l3, ez)[None]
    er = np.zeros((3, 9, 2 * q, 2 * q, 144))
    for at in range(9):
        for x in range(2 * q):
            for y in range(2 * q):
                for d in range(3):
                    er[d, at, x, y, at * 16 + d * 4 + (x // q) * 2 + y // q] = 1
    plain["er"] = (er.reshape(3 * 576, 144), BF)
    pair["k3"] = np.concatenate(three(k3, w3, 2), 0)
    pair["rk3"] = side_by_side(blocks(w3, ez), blocks(k3, ez))
    corner_line = lambda table: np.kron(np.eye(6), table)
    modes_of = [a1m @ corner_line(table) for table in (k3 @ jm, w3 @ jm)]
    pair["wl"] = np.concatenate(
        [np.kron(modes_of[left], modes_of[right]) for left, right in ((0, 1), (1, 0), (1, 1))], 1
    )
    pair["ra3"] = side_by_side(
        blocks((w3 @ jm).T, ez) @ pair["azm"], blocks((k3 @ jm).T, ez) @ pair["azm"]
    )
    spread_vertices, spread_factors = np.zeros((144, 128)), np.zeros((3, 144, 144))
    for row in range(144):
        (ex, cx), (ey, cy) = divmod(row // 12, 2), divmod(row % 12, 2)
        vx, vy = ex + cx, ey + cy
        column = (AHEAD.index(vx // 2 - 1) * 4 + vy // 2) * 8 + (vx % 2) * 2 + vy % 2
        spread_vertices[row, column] = 1
        for d in range(3):
            at = order.index((ex // 2 - 1, ey // 2 - 1))
            spread_factors[d, row, at * 16 + d * 4 + (ex % 2) * 2 + ey % 2] = 1
    plain["ev"] = (spread_vertices, BF)
    plain["ef"] = (spread_factors.reshape(432, 144), BF)
    corner_z = np.zeros((ez, 2 * ez))
    for element in range(ez):
        for at in range(2):
            corner_z[(element + at) % ez, 2 * element + at] = 1
    plain["cz"] = (np.tile(corner_z, (4, 1)), BF)
    plain["s16"] = (spread(2), BF)
    vertex_line = lambda table: np.array(
        [[table[at % q, v - at // q] if 0 <= v - at // q <= 1 else 0.0 for v in range(8)] for at in range(6 * q)]
    )
    plain1 = vertex_line(jm)

    def vertex_columns(left, right, dx, dy):
        table = np.zeros((64, 4, 4, 8))
        for iy in range(4):
            for ix, ahead in enumerate(AHEAD):
                for x in range(2):
                    for y in range(2):
                        table[:, ix, iy, x * 2 + y] = np.kron(
                            left[span(dx), (ahead + 1) * 2 + x], right[span(dy), iy * 2 + y]
                        )
        return table.reshape(64, 128)

    pair["jc"] = vertex_columns(plain1, plain1, 0, 0)

    def z_vertices(table):
        result = np.zeros((ez, ez * q))
        for element in range(ez):
            for at in range(q):
                result[element, element * q + at] += table[at, 0]
                result[(element + 1) % ez, element * q + at] += table[at, 1]
        return np.tile(result, (4, 1))

    pair["rcj"] = z_vertices(jm)
    mask, left = np.zeros((n_gy, 16, 128)), np.zeros((n_gy, 16, 16))
    for gy in range(n_gy):
        for row in range(16):
            vx, vy = row // 8 + row // 4 % 2, row // 2 % 2 + row % 2
            owner = gy + vy // 2
            if owner < n_gy:
                first = owner * 32 + (vx % 2) * 16 + (vy % 2) * 8
                mask[gy, row, first % 128 : first % 128 + 8] = 1
                left[gy, first // 128 + 4 * (vx // 2), row] = 1
    plain["mask"] = (mask.reshape(-1, 128), F32)
    plain["left"] = (left.reshape(-1, 16), BF)
    chosen = np.zeros((8, 32))
    select = np.zeros((32, 8))
    for lane in range(32):
        chosen[lane // 8, lane] = 1
        select[lane, lane % 8] = 1
    plain["chosen"] = (chosen, F32)
    plain["select"] = (select, BF)
    tables = {}
    for name, table in pair.items():
        table = fitted(np.asarray(table, np.float64), name in RIGHT)
        high = table.astype(ml_dtypes.bfloat16)
        rest = (table - high.astype(np.float64)).astype(ml_dtypes.bfloat16)
        if name in RIGHT:
            tables[name] = np.block([[high, rest], [high, np.zeros_like(rest)]])[None]
        else:
            tables[name] = np.stack([high, rest])
    for name, (table, kind) in plain.items():
        table = fitted(np.asarray(table), name in RIGHT)
        table = np.concatenate([table, table], 0) if name in RIGHT else table
        tables[name] = table.astype(ml_dtypes.bfloat16 if kind is BF else np.float32)[None]
    return tables


STAGES = (
    ("columns", "vo", "jxy", "jz", "s80", "sl80", "e7", "e3", "e1", "s64", "s32", "s256", "wz7", "chosen", "mask"),
    ("ld9", "vl", "az", "vb", "la", "bzra"),
    ("ld3", "s48", "sl48", "er"),
    (
        "wmo", "jl", "rj", "bz", "k7", "kz7", "wmn", "azm", "lb", "rb", "left", "bm", "bzm", "select",
        "rk3", "k3", "wl", "ra3", "ev", "ef", "cz", "s16", "jc", "rcj", "rp", "bzrp", "lp", "pxy", "pz",
    ),
)


def pack(tables):
    stacks, places = {}, {}
    for stage, names in enumerate(STAGES):
        for name in names:
            table = tables[name]
            key = (stage, table.dtype.name, table.shape[-1])
            parts = stacks.setdefault(key, [])
            at = sum(part.shape[0] for part in parts)
            height = -(-table.shape[1] // 16) * 16
            for part in table:
                parts.append(np.pad(part, ((0, height - part.shape[0]), (0, 0))))
            places[name] = (key, at, height, table.shape[1])
    keys = tuple(stacks)
    return keys, [np.concatenate(stacks[key], 0) for key in keys], places


class Table:
    def __init__(self, ref, place):
        _, self.at, self.height, self.rows = place
        self.ref = ref
        self.shape = (2, self.rows, ref.shape[-1])

    def __getitem__(self, part):
        part = 0 if part is Ellipsis else part
        return self.ref[self.at + part * self.height : self.at + part * self.height + self.rows, :]

    def piece(self, part, start, rows):
        return self.ref[pl.ds(self.at + part * self.height + start, rows), :]


def dot(a, b):
    return jnp.dot(a, b, preferred_element_type=F32)


def split(x):
    high = x.astype(BF)
    return high, (x - high.astype(F32)).astype(BF)


def wide(x, lanes=128):
    if x.shape[1] == lanes:
        return x
    return jnp.concatenate([x, jnp.zeros((x.shape[0], lanes - x.shape[1]), x.dtype)], 1)


def tall(x, rows):
    if x.shape[0] == rows:
        return x
    return jnp.concatenate([x, jnp.zeros((rows - x.shape[0], x.shape[1]), x.dtype)], 0)


def halves(x):
    middle = x.shape[1] // 2
    return x[:, :middle] + x[:, middle:]


def exactly(main, small, x):
    high, rest = split(x)
    return halves(dot(main, jnp.concatenate([high, rest], 1))) + dot(small, high)


def left3(table, x):
    return exactly(table[0], table[1], tall(x, table.shape[-1]))


def left2(table, x):
    return halves(dot(table[...], jnp.concatenate(split(tall(x, table.shape[-1])), 1)))


def terms3(table, x):
    x = tall(x, table.shape[-1])
    rows = table.shape[1] // 3
    first = exactly(table.piece(0, 0, 2 * rows), table.piece(1, 0, 2 * rows), x[:, 0:128])
    third = exactly(table.piece(0, 2 * rows, rows), table.piece(1, 2 * rows, rows), x[:, 128:256])
    return first[0:rows], first[rows:], third


def right3(x, table):
    return halves(right2(x, table))


def right2(x, table):
    return dot(jnp.concatenate(split(wide(x)), 1), table[...])


KEPT = {
    "fine_f": (768, 128), "mid_f": (192, 128), "low_f": (48, 256), "ring_f": (1728, 128), "inverse3": (576, 128), "wt7": (256, 128), "wt3": (64, 128), "base_mid": (64, 128),
    "base_low": (16, 256), "first_fine": (256, 128), "base_fine": (256, 128),
    "first_mid": (64, 128), "modal3": (576, 128), "base_ring": (576, 128),
    "ww7": (256, 128), "inverse9": (1600, 128), "corner_f": (432, 128), "modal9": (800, 256),
}


def cycle_kernel(keys, places, n_gx, n_gy, *refs):
    r_hbm, len_hbm, inv_hbm = refs[:3]
    count = len(keys)
    packed = refs[3 : 3 + count]
    out_fine, out_mid, out_low = refs[3 + count : 6 + count]
    stores = refs[6 + count : 6 + 2 * count]
    (
        r_ref, len_ref, inv_ref, rs, fs, hb1, rm, fm, rp, fp, hb2, hs1, hs2, rb, corner, held, gs, gb, cb, invs,
        send_sem, recv_sem, gsend, grecv, csend, crecv, isend, irecv, in_sem, table_sem,
    ) = refs[6 + 2 * count : -len(KEPT)]
    gx, gy = lax.axis_index("gx"), lax.axis_index("gy")
    last = n_gy - 1
    barrier = pltpu.get_barrier_semaphore()

    def greet(ahead, row):
        pl.semaphore_signal(
            barrier, inc=1, device_id=(lax.rem(gx + (ahead + n_gx), n_gx), row), device_id_type=MESH
        )

    def greet_if(row, *columns):
        @pl.when((row >= 0) & (row <= last))
        def _():
            for ahead in columns:
                greet(ahead, row)

    def other_row(flips):
        row = gy
        for bit in (8, 4, 2, 1):
            if flips & bit:
                row = row + bit * (1 - 2 * (gy // bit % 2))
        return row

    def greet_rows(*several):
        for flips in several:
            if flips < n_gy:
                greet(-1, other_row(flips))
                if flips:
                    greet(0, other_row(flips))

    greet_rows(12, 13, 10, 11, 14, 15, 8, 9)
    greet_if(gy + 1, 1)
    greet_if(gy - 1, 1)
    greet(1, gy)
    greet(2, gy)
    greet_rows(4, 5, 2, 3, 6, 7, 1, 0)
    inputs = [
        pltpu.make_async_copy(source, target, in_sem.at[at])
        for at, (source, target) in enumerate(((len_hbm, len_ref), (r_hbm, r_ref), (inv_hbm, inv_ref)))
    ]
    loads = [pltpu.make_async_copy(packed[at], stores[at], table_sem.at[at]) for at in range(count)]
    for load in inputs:
        load.start()

    def fetch(*stages):
        for key, load in zip(keys, loads):
            if key[0] in stages:
                load.start()

    fetch(0)

    def ready(stage):
        for key, load in zip(keys, loads):
            if key[0] == stage:
                load.wait()

    kept = dict(zip(KEPT, refs[-len(KEPT) :]))

    def keep(name, value):
        kept[name][...] = value
        return kept[name]

    t = {name: Table(stores[keys.index(place[0])], place) for name, place in places.items()}
    at_bottom, at_top = gy == 0, gy == last
    not_bottom, not_top = gy > 0, gy < last
    sent = {0: None, 1: not_bottom, 2: not_top}

    def guarded(condition, action):
        if condition is None:
            action()
        else:
            pl.when(condition)(action)

    def exchange(phase, source, buffer, rows, numbers=(1, 2, 0)):
        at = offsets(rows)

        def group(number):
            def action():
                for index in range(*GROUPS[number]):
                    tx, ty = RING[index]
                    slot = RING.index((-tx, -ty))
                    landing = (0, 2, 1)[number]
                    pltpu.make_async_remote_copy(
                        src_ref=source(index),
                        dst_ref=buffer.at[pl.ds(at[slot], rows[slot])],
                        send_sem=send_sem.at[phase, number],
                        recv_sem=recv_sem.at[phase, landing],
                        device_id=(lax.rem(gx + (tx + n_gx), n_gx), gy + ty),
                        device_id_type=MESH,
                    ).start()

            return action

        for number in numbers:
            guarded(sent[number], group(number))

    def settle(phase, sems, buffer, rows):
        at = offsets(rows)
        for number in range(3):
            first, end = GROUPS[number]
            piece = buffer.at[pl.ds(at[first], at[end] - at[first])]
            guarded(sent[number], lambda: pltpu.make_async_copy(piece, piece, sems.at[phase, number]).wait())

    def clear(number):
        first, end = GROUPS[number]
        for buffer, rows in (
            (fs, BLOCK_ROWS), (hb1, WIDE_ROWS), (rp, BLOCK_ROWS), (fp, BLOCK_ROWS), (hb2, WIDE_ROWS),
        ):
            at = offsets(rows)
            buffer[at[first] : at[end], :] = jnp.zeros((at[end] - at[first], buffer.shape[1]), buffer.dtype)

    @pl.when(at_bottom)
    def _():
        clear(1)
        invs[0:32, :] = jnp.zeros((32, invs.shape[1]), BF)

    @pl.when(at_top)
    def _():
        clear(2)
        invs[64:96, :] = jnp.zeros((32, invs.shape[1]), BF)

    @pl.when(gy >= last - 1)
    def _():
        invs[96:128, :] = jnp.zeros((32, invs.shape[1]), BF)

    at_wide = offsets(WIDE_ROWS)

    def mirrored(values):
        return jnp.concatenate([values[(15 - x) * 16 : (16 - x) * 16] for x in range(16)], 0)

    def wide_halo(field, stage):
        for x in range(16):
            rb[x] = field[15 - x]
        for index, (tx, ty) in enumerate(RING):
            source, ys = (rb if tx < 0 else field), (6, 0)[ty < 0]
            if 0 not in (tx, ty):
                corner[48:64, :] = jnp.zeros((16, 128), F32)
            for pair in range(5):
                xa, ya = 6 + 2 * pair, ys + 2 * pair
                at = at_wide[index] + pair * 16
                if ty == 0:
                    layers = source[xa, :, :], source[xa + 1, :, :]
                    stage[at : at + 16, :] = jnp.concatenate(layers, 1).astype(stage.dtype)
                elif tx == 0:
                    rows = [jnp.concatenate([field[0:8, y, :], rb[0:8, y, :]], 1) for y in (ya, ya + 1)]
                    stage[at : at + 16, :] = jnp.concatenate(rows, 0).astype(stage.dtype)
                else:
                    layers = source[6:16, ya, :], source[6:16, ya + 1, :]
                    corner[pair * 10 : pair * 10 + 10, :] = jnp.concatenate(layers, 1)
            if 0 not in (tx, ty):
                stage[at_wide[index] : at_wide[index + 1], :] = corner[...].astype(stage.dtype)

    def side_values(buffer):
        plain, turned_back = {}, {}
        for index, direction in enumerate(RING):
            piece = buffer[at_wide[index] : at_wide[index + 1], :]
            plain[direction] = piece
            turned_back[direction] = pltpu.roll(piece.astype(F32), 64, 1).astype(BF)
        ends, flanks = LOW_SIDE[:3], LOW_SIDE[3:]
        opposite = [(-dx, dy) for dx, dy in ends]
        low_part = [plain[d] for d in ends + flanks] + [turned_back[d] for d in ends + flanks]
        high_part = [plain[d] for d in opposite] + [turned_back[d] for d in flanks]
        high_part += [turned_back[d] for d in opposite] + [plain[d] for d in flanks]
        return jnp.concatenate([tall(jnp.concatenate(part, 0), 768) for part in (low_part, high_part)], 1)

    def fold(block):
        result = block[0:16]
        for part in range(1, 4):
            result = result + pltpu.roll(block[part * 16 : part * 16 + 16], part * 32, 1)
        return result

    def spread_blocks(folded, blocks_ref):
        for part in range(4):
            turned_back = pltpu.roll(folded[0:128, :], (128 - part * 32) % 128, 1) if part else folded[0:128, :]
            for slot in range(8):
                blocks_ref[slot * 64 + part * 16 : slot * 64 + part * 16 + 16, :] = turned_back[
                    slot * 16 : slot * 16 + 16
                ]


    inputs[0].wait()
    own_f = 8 * 16
    for ex in range(2):
        a, b, c = len_ref[0, ex], len_ref[1, ex], len_ref[2, ex]
        fs[own_f + ex * 2 : own_f + ex * 2 + 2, :] = wide(b * c / (2.0 * a))
        fs[own_f + 4 + ex * 2 : own_f + 6 + ex * 2, :] = wide(a * c / (2.0 * b))
        fs[own_f + 8 + ex * 2 : own_f + 10 + ex * 2, :] = wide(a * b / (2.0 * c))
    fs[own_f + 12 : own_f + 16, :] = jnp.zeros((4, 128), F32)
    inputs[1].wait()
    wide_halo(r_ref, hs1)
    near = jnp.minimum(gy + 1, last) - jnp.maximum(gy - 1, 0) + 1
    pl.semaphore_wait(barrier, 2 * n_gy + near)
    for numbers in ((1, 2), (0,)):
        exchange(1, lambda index: hs1.at[pl.ds(at_wide[index], WIDE_ROWS[index])], hb1, WIDE_ROWS, numbers)
        exchange(0, lambda index: fs.at[pl.ds(own_f, 16)], fs, BLOCK_ROWS, numbers)
    fetch(1, 2)
    inputs[2].wait()
    invs[32:64, :] = inv_ref[0]
    reach = ((1, 0, not_top, not_bottom), (-1, 2, not_bottom, not_top), (-2, 3, gy > 1, gy < last - 1))

    def inverse_copy(at):
        step, slot, _, _ = reach[at]
        return pltpu.make_async_remote_copy(
            src_ref=invs.at[pl.ds(32, 32)],
            dst_ref=invs.at[pl.ds(slot * 32, 32)],
            send_sem=isend.at[at],
            recv_sem=irecv.at[at],
            device_id=(gx, gy + step),
            device_id_type=MESH,
        )

    for at in range(3):
        pl.when(reach[at][2])(lambda: inverse_copy(at).start())

    bottom_on = jnp.where(at_bottom, 1.0, 0.0)
    top_on = jnp.where(at_top, 1.0, 0.0)

    ready(0)
    columns = t["columns"][...]

    def wall_weight(rows, at):
        piece = columns[0:rows]
        return piece[:, at : at + 1] + bottom_on * piece[:, at + 1 : at + 2] + top_on * piece[:, at + 2 : at + 3]

    wt7 = keep("wt7", jnp.broadcast_to(wall_weight(256, 0), (256, 128)))
    wt3 = keep("wt3", jnp.broadcast_to(wall_weight(64, 6), (64, 128)))
    ww7 = keep("ww7", jnp.broadcast_to(columns[:, 9:10], (256, 128)))
    r = wide(r_ref[...].reshape(256, 64))
    f_own = wide(fs[own_f : own_f + 16, :])
    modal9 = keep("modal9", left3(t["vo"], jnp.concatenate([r, mirrored(r)], 1)))
    base_mid = keep("base_mid", right3(left3(t["jxy"], r), t["jz"]))
    fine_f = keep("fine_f", left2(t["e7"], right2(f_own, t["s64"])))
    mid_f = keep("mid_f", left2(t["e3"], right2(f_own, t["s32"])))
    low_f = keep("low_f", left2(t["e1"], right2(f_own, t["s256"])))

    def ring_modes(buffer):
        modal = modal9[...] + dot(t["vl"][...], side_values(buffer))
        modal = right3(jnp.concatenate([modal[:, 0:128], modal[:, 128:256]], 0), t["az"]) * inverse9[...]
        return jnp.concatenate([modal[0:800], modal[800:1600]], 1)

    def joined(values):
        return values[:, 0:128] + mirrored(values[:, 128:256])

    ready(1)
    fetch(3)
    settle(0, recv_sem, fs, BLOCK_ROWS)
    ring_l = wide(fs[...])
    kind = lax.broadcasted_iota(jnp.int32, (144, 128), 0) % 16 // 4
    d9 = left3(t["ld9"], jnp.where(kind == 2, right3(ring_l, t["sl80"]), right2(ring_l, t["s80"])))
    inverse9 = keep("inverse9", jnp.where(d9 > 0.0, 1.0 / d9, 0.0))
    settle(1, recv_sem, hb1, WIDE_ROWS)
    local = joined(left3(t["vb"], ring_modes(hb1))) * wt7[...]
    terms = terms3(t["la"], right3(local, t["bzra"]))
    residual_mid = base_mid[...] - (mid_f[0:64] * terms[0] + mid_f[64:128] * terms[1] + mid_f[128:192] * terms[2])
    rp[128:144, :] = fold(residual_mid)
    exchange(3, lambda index: rp.at[pl.ds(128, 16)], rp, BLOCK_ROWS)
    rm[512:576, :] = residual_mid

    ready(2)
    ready(3)
    ring_l = wide(fs[...])
    d3 = left3(t["ld3"], jnp.where(kind == 2, right3(ring_l, t["sl48"]), right2(ring_l, t["s48"])))
    inverse3 = keep("inverse3", jnp.where(d3 > 0.0, 1.0 / d3, 0.0))
    own_modal = keep("modal3", left3(t["wmo"], residual_mid))
    base_low = keep("base_low", right3(left3(t["jl"], residual_mid), t["rj"]))
    first_fine = keep("first_fine", right3(local, t["bz"]))
    massed = left3(t["k7"], first_fine[...] * t["wz7"][...][0:1])
    along_z = right3(first_fine[...], t["kz7"]) * ww7[...]
    base_fine = keep(
        "base_fine",
        wide(r_ref[...].reshape(256, 64))
        - (fine_f[0:256] * massed[0:256] + fine_f[256:512] * massed[256:512] + fine_f[512:768] * along_z),
    )

    settle(3, recv_sem, rp, BLOCK_ROWS)
    spread_blocks(rp, rm)
    modal3 = own_modal[...] + left3(t["wmn"], rm[0:512, :])
    modal3 = right3(modal3, t["azm"]) * inverse3[...]
    variant = jnp.where(at_bottom, 1, jnp.where(at_top, 2, 0))
    rows = pl.multiple_of(variant * 48, 16)
    low = exactly(t["lb"].piece(0, rows, 48), t["lb"].piece(1, rows, 48), tall(modal3, t["lb"].shape[-1]))
    low = right3(low, t["rb"])
    low = base_low[...] - (
        low_f[0:16] * low[0:16, 0:256] + low_f[16:32] * low[16:32, 0:256] + low_f[32:48] * low[32:48, 256:512]
    )
    wall = pl.multiple_of(gy * 16, 16)
    low = tall(halves(low) * t["mask"].piece(0, wall, 16), 128)
    message = halves(dot(t["left"].piece(0, wall, 16), jnp.concatenate(split(low), 1)))[0:8]
    gs[...] = message

    def send_slab(flips, ahead):
        row = other_row(flips)
        pltpu.make_async_remote_copy(
            src_ref=gs,
            dst_ref=gb.at[flips + (n_gy - 1 if ahead else -1)],
            send_sem=gsend,
            recv_sem=grecv,
            device_id=(lax.rem(gx + ahead, n_gx), row),
            device_id_type=MESH,
        ).start()

    for flips in (12, 13, 10, 11, 14, 15, 8, 9, 4, 5, 2, 3, 6, 7, 1, 0):
        if flips < n_gy:
            send_slab(flips, 1)
            if flips:
                send_slab(flips, 0)

    first_mid = keep("first_mid", right3(left3(t["bm"], modal3) * wt3[...], t["bzm"]))
    fm[512:576, :] = first_mid[...]
    fp[128:144, :] = fold(first_mid[...])
    exchange(4, lambda index: fp.at[pl.ds(128, 16)], fp, BLOCK_ROWS)

    for at in range(3):
        pl.when(reach[at][3])(lambda: inverse_copy(at).wait_recv())
    pltpu.make_async_copy(gb, gb, grecv).wait()
    here = gs[...] + jnp.sum(gb[0 : n_gy - 1], axis=0)
    behind = jnp.sum(gb[n_gy - 1 :], axis=0)
    chunks = inv_ref.shape[2] // 128
    vector = here + pltpu.roll(behind, 4, 0)
    row = lax.broadcasted_iota(jnp.int32, (8, 128), 0)
    vector = jnp.concatenate([jnp.where(row == chunk, vector, 0.0) for chunk in range(chunks)], 1)
    vector = tall(vector, 16).astype(BF)
    solved = lax.dot_general(vector, invs[...], (((1,), (1,)), ((), ())), preferred_element_type=F32)
    solved = jnp.broadcast_to(jnp.sum(solved, axis=0, keepdims=True), (8, 128))
    chosen = t["chosen"][...]
    for iy in range(4):
        cb[96 + iy * 8 : 104 + iy * 8, :] = (pltpu.roll(solved, 128 - iy * 32, 1) if iy else solved) * chosen
    for ix in (2, 1, 0):
        pltpu.make_async_remote_copy(
            src_ref=cb.at[pl.ds(96, 32)],
            dst_ref=cb.at[pl.ds(ix * 32, 32)],
            send_sem=csend,
            recv_sem=crecv,
            device_id=(lax.rem(gx - AHEAD[ix] + n_gx, n_gx), gy),
            device_id_type=MESH,
        ).start()

    others = cb.at[pl.ds(0, 96)]

    ring_l = wide(fs[...])
    ring_f = keep("ring_f", left2(t["er"], right2(ring_l, t["s32"])))
    corner_f = keep("corner_f", left2(t["ef"], right2(ring_l, t["s16"])))
    low_out = right2(tall(cb[104:112, :], 16), t["select"])
    out_low[0] = low_out[0:2, 0:8]
    out_low[1] = low_out[2:4, 0:8]
    settle(4, recv_sem, fp, BLOCK_ROWS)
    spread_blocks(fp, fm)
    turned = right3(fm[...], t["rk3"])
    parts = []
    for at in range(9):
        piece = terms3(t["k3"], turned[at * 64 : (at + 1) * 64])
        parts.append(
            rm[at * 64 : (at + 1) * 64, :]
            - (
                ring_f[at * 64 : (at + 1) * 64] * piece[0]
                + ring_f[576 + at * 64 : 576 + (at + 1) * 64] * piece[1]
                + ring_f[1152 + at * 64 : 1152 + (at + 1) * 64] * piece[2]
            )
        )
    base_ring = keep("base_ring", jnp.concatenate(parts, 0))
    modal3 = left3(t["wmn"], base_ring[0:512]) + left3(t["wmo"], base_ring[512:576])
    modal3 = keep("modal3", right3(modal3, t["azm"]))

    pltpu.make_async_copy(others, others, crecv).wait()
    corrections = wide(cb[...])
    change = left2(t["ev"], right2(corrections, t["cz"]))
    change = right3(jnp.concatenate([change * corner_f[at * 144 : at * 144 + 144] for at in range(3)], 0), t["ra3"])
    change = jnp.concatenate([change[0:288, 0:128], change[288:432, 128:256]], 0)
    modal3 = (modal3[...] - left3(t["wl"], change)) * inverse3[...]
    held[0:64, :] = first_mid[...] + right3(left3(t["jc"], corrections), t["rcj"])
    smoothed = left3(t["bm"], modal3) * wt3[...]

    turned = terms3(t["lp"], right3(smoothed, t["bzrp"]) + right3(held[0:64, :], t["rp"]))
    residual = base_fine[...] - (
        fine_f[0:256] * turned[0]
        + fine_f[256:512] * turned[1]
        + fine_f[512:768] * turned[2]
    )
    rs[...] = residual[:, 0:64].reshape(16, 16, 64)
    wide_halo(rs, hs2)
    exchange(5, lambda index: hs2.at[pl.ds(at_wide[index], WIDE_ROWS[index])], hb2, WIDE_ROWS)
    mid_result = held[0:64, :] + right3(smoothed, t["bzm"])
    out_mid[...] = mid_result[:, 0:32].reshape(8, 8, 32)
    modal9 = keep("modal9", dot(t["vo"][0], jnp.concatenate([residual, mirrored(residual)], 1).astype(BF)))
    held[...] = first_fine[...] + right3(left3(t["pxy"], mid_result), t["pz"])
    settle(5, recv_sem, hb2, WIDE_ROWS)
    local = joined(dot(t["vb"][0], tall(ring_modes(hb2), 896).astype(BF))) * wt7[...]
    result = held[...] + right3(local, t["bz"])
    out_fine[...] = result[:, 0:64].reshape(16, 16, 64)

    for phase, buffer, rows in (
        (0, fs, BLOCK_ROWS), (1, hb1, WIDE_ROWS), (3, rp, BLOCK_ROWS), (4, fp, BLOCK_ROWS), (5, hb2, WIDE_ROWS),
    ):
        settle(phase, send_sem, buffer, rows)
    pltpu.make_async_copy(gb, gb, gsend).wait()
    pltpu.make_async_copy(others, others, csend).wait()
    for at in range(3):
        pl.when(reach[at][2])(lambda: inverse_copy(at).wait_send())


def hand_over(*refs):
    copies = [pltpu.make_async_copy(refs[at], refs[3 + at], refs[6].at[at]) for at in range(3)]
    for copy in copies:
        copy.start()
    for copy in copies:
        copy.wait()


def shards(n_gx, n_gy, local_residual, lengths, coarse_inverse):
    keys, packed, places = pack(build_tables(n_gy, lengths.shape[3]))
    vmem = pl.BlockSpec(memory_space=pltpu.VMEM)
    scratch = [pltpu.VMEM(table.shape, BF if key[1] == "bfloat16" else F32) for key, table in zip(keys, packed)]
    scratch += [
        pltpu.VMEM(local_residual.shape, F32),
        pltpu.VMEM(lengths.shape, F32),
        pltpu.VMEM(coarse_inverse.shape, BF),
        pltpu.VMEM((16, 16, 64), F32),
        pltpu.VMEM((144, 128), F32),
        pltpu.VMEM((576, 128), BF),
        pltpu.VMEM((576, 128), F32),
        pltpu.VMEM((576, 128), F32),
        pltpu.VMEM((144, 128), F32),
        pltpu.VMEM((144, 128), F32),
        pltpu.VMEM((576, 128), BF),
        pltpu.VMEM((576, 128), BF),
        pltpu.VMEM((576, 128), BF),
        pltpu.VMEM((16, 16, 64), F32),
        pltpu.VMEM((64, 128), F32),
        pltpu.VMEM((256, 128), F32),
        pltpu.VMEM((8, 128), F32),
        pltpu.VMEM((2 * n_gy - 1, 8, 128), F32),
        pltpu.VMEM((128, 128), F32),
        pltpu.VMEM((128, coarse_inverse.shape[2]), BF),
        pltpu.SemaphoreType.DMA((6, 3)),
        pltpu.SemaphoreType.DMA((6, 3)),
        pltpu.SemaphoreType.DMA,
        pltpu.SemaphoreType.DMA,
        pltpu.SemaphoreType.DMA,
        pltpu.SemaphoreType.DMA,
        pltpu.SemaphoreType.DMA((3,)),
        pltpu.SemaphoreType.DMA((3,)),
        pltpu.SemaphoreType.DMA((3,)),
        pltpu.SemaphoreType.DMA((len(keys),)),
    ]
    scratch += [pltpu.VMEM(shape, F32) for shape in KEPT.values()]
    outs = pl.pallas_call(
        functools.partial(cycle_kernel, keys, places, n_gx, n_gy),
        out_shape=(
            jax.ShapeDtypeStruct((16, 16, 64), F32),
            jax.ShapeDtypeStruct((8, 8, 32), F32),
            jax.ShapeDtypeStruct((2, 2, 8), F32),
        ),
        in_specs=[pl.BlockSpec(memory_space=pl.ANY)] * (3 + len(keys)),
        out_specs=(vmem, vmem, vmem),
        scratch_shapes=scratch,
        compiler_params=pltpu.CompilerParams(collective_id=0, has_side_effects=True, vmem_limit_bytes=60 * 1024 * 1024),
    )(local_residual, lengths, coarse_inverse, *[jnp.asarray(table) for table in packed])
    return pl.pallas_call(
        hand_over,
        out_shape=tuple(jax.ShapeDtypeStruct(out.shape, out.dtype) for out in outs),
        in_specs=[vmem] * 3,
        out_specs=[pl.BlockSpec(memory_space=pl.ANY)] * 3,
        scratch_shapes=[pltpu.SemaphoreType.DMA((3,))],
    )(*outs)


def solution(mesh):
    in_specs = (P("gx", "gy", None), P(None, "gx", "gy", None), P("gx", "gy", None))
    out_specs = (P("gx", "gy", None), P("gx", "gy", None), P("gx", "gy", None))
    return jax.shard_map(
        functools.partial(shards, mesh.shape["gx"], mesh.shape["gy"]),
        mesh=mesh,
        in_specs=in_specs,
        out_specs=out_specs,
        check_vma=False,
    )
```
